32 devices in a mesh: wide: 16 (over z, y, core), batch: 2 (over x).
Axes of the slice: x: 2, y: 2, z: 4, core: 2. Of those that a mesh axis runs over, the one named last changes fastest.
Arguments:
- integrals: bfloat16 [1536, 16, 640], P('wide'), may hold values from -0.8984375 to 0.8984375
- vir_coeff: bfloat16 [640, 512], P(None, 'batch'), may hold values from -0.25 to 0.25
- occ_energy: float32 [16], replicated, may hold values from -1.6 to -0.4
- vir_energy: float32 [512], replicated, may hold values from 0.2 to 3
- kappas: float32 [8], replicated, may hold values from 0.1 to 3
Outputs:
- density: bfloat16 [8, 16, 512, 1536], P(None, 'wide', 'batch')
The draws below stay inside these ranges and needn't reach their ends.
All inputs are finite; a program needn't handle non-finite values.
Results may differ from the reference program's by a relative error of at most 0.0051.
Values may be sent and summed in bfloat16 or wider, within the bound.
No kernel may reach another device: no remote copies, remote signals or barrier semaphores. Data moves between devices by JAX's collectives and lax.ppermute only.
A program may use at most 128 MiB of HBM per device.

```python
import math
import jax
import jax.numpy as jnp
from jax import lax

NBF = 640
NAUX = 1536
NVIR = 512
NKAP = 8
HALF = 2
NOCC = 16


def steps_of(stream_key, dims, split, low, largest):
    gain, own = 1.0, jax.random.fold_in(stream_key, 6)
    for position, parts in split:
        draws = jnp.exp(jax.random.uniform(jax.random.fold_in(own, position), (parts,), jnp.float32, low / len(split), largest / len(split)))
        gain = gain * jnp.repeat(draws, dims[position] // parts).reshape([-1 if axis == position else 1 for axis in range(len(dims))])
    return gain


def scatter_about(key, extent, deviation, bound, cuts=(), held_as=jnp.bfloat16):
    values = deviation * jax.random.normal(key, extent, jnp.float32)
    if cuts:
        values = values * steps_of(key, extent, cuts, -0.22, 0.18)
    return jnp.clip(values, -bound, bound).astype(held_as)


def setup_inputs(seed: int = 0) -> dict:
    keys = jax.random.split(jax.random.key(seed), 6)
    integrals = scatter_about(keys[0], (NAUX, NOCC, NBF), 0.15, 0.8984375, ((0, 16),))
    vir_coeff = scatter_about(keys[1], (NBF, NVIR), NBF ** -0.5, 0.25, ((1, 2),))
    occ_energy = jnp.clip(jax.random.uniform(keys[2], (NOCC,), jnp.float32, -1.6, -0.4), -1.6, -0.4)
    vir_energy = jnp.clip(jax.random.uniform(keys[3], (NVIR,), jnp.float32, 0.2, 3.0), 0.2, 3.0)
    kappas = jnp.clip(jnp.exp(jax.random.uniform(keys[4], (NKAP,), jnp.float32, math.log(0.1), math.log(3.0))), 0.1, 3.0)
    return dict(integrals=integrals, vir_coeff=vir_coeff, occ_energy=occ_energy, vir_energy=vir_energy, kappas=kappas)


def pair_density(own, partner, own_energy, partner_energy, row_energy, vir_energy, kappas):
    coulomb = jnp.dot(own.T, partner, preferred_element_type=jnp.float32)
    denominator = row_energy[:, None] + vir_energy[None, :] - own_energy - partner_energy
    damping = 1.0 - jnp.exp(-kappas[:, None, None] * denominator[None])
    amplitude = ((-coulomb[None] * (damping * damping)) / denominator[None]).astype(jnp.bfloat16)
    return jnp.einsum("kab,pb->kap", amplitude.astype(jnp.float32), partner.astype(jnp.float32))


def reference(integrals, vir_coeff, occ_energy, vir_energy, kappas):
    flat = integrals.reshape(NAUX * NOCC, NBF)
    transformed = jnp.dot(flat, vir_coeff, preferred_element_type=jnp.float32).astype(jnp.bfloat16)
    by_occ = jnp.transpose(transformed.reshape(NAUX, NOCC, NVIR), (1, 0, 2))

    def one_orbital(index):
        own = by_occ[index]
        density = jnp.zeros((NKAP, NVIR, NAUX), jnp.float32)
        for offset in range(-HALF, HALF + 1):
            other = ((index + offset) % NOCC).astype(jnp.int32)
            density = density + pair_density(own, by_occ[other], occ_energy[index], occ_energy[other], vir_energy, vir_energy, kappas)
        return density.astype(jnp.bfloat16)

    result = lax.map(one_orbital, jnp.arange(NOCC, dtype=jnp.int32))
    return jnp.transpose(result, (1, 0, 2, 3))
```

```python
import functools

import jax
import jax.numpy as jnp
from jax import lax
from jax.experimental import pallas as pl
from jax.experimental.pallas import tpu as pltpu
from jax.sharding import PartitionSpec as P

HALF = 2
P_TILE = 256


def from_behind(shard, axis, by):
    peers = lax.axis_size(axis)
    return lax.ppermute(shard, axis, [(i, (i + by) % peers) for i in range(peers)])


def swap_pairs(shard, axis):
    peers = lax.axis_size(axis)
    return lax.ppermute(shard, axis, [(i, i ^ 1) for i in range(peers)])


def shift_by_parity(shard, axis, even_by):
    peers = lax.axis_size(axis)
    return lax.ppermute(
        shard,
        axis,
        [(i, (i + (even_by if i % 2 == 0 else -even_by)) % peers) for i in range(peers)],
    )


def terms_kernel(
    blocks, has_partial, place, kappas, occ_energy, vir_rows, own, *refs
):
    n = len(blocks)
    partners = refs[:n]
    refs = refs[n:]
    partial = None
    if has_partial:
        partial, refs = refs[0], refs[1:]
    out, amp = refs
    nkap, rows = amp.shape[0], amp.shape[1]
    cols = partners[0].shape[1]
    step = pl.program_id(0)

    @pl.when(step == 0)
    def _():
        orbital, half, count = place[0], place[1], place[2]
        sign = 1 - 2 * lax.rem(orbital, 2)
        own_energy = occ_energy[orbital]
        row_energy = vir_rows[pl.ds(half, 1), :] - own_energy
        row_full = jnp.transpose(jnp.broadcast_to(row_energy, (128, rows)))
        row_full = jnp.concatenate([row_full] * (cols // 128), axis=1)
        own_t = jnp.transpose(own[...])
        for k, (offset, other) in enumerate(blocks):
            index = lax.rem(orbital + sign * offset + count, count)
            column_half = lax.rem(half + other, 2)
            column_energy = vir_rows[pl.ds(column_half, 1), :] - occ_energy[index]
            coulomb = jnp.dot(own_t, partners[k][...], preferred_element_type=jnp.float32)
            ratio = -coulomb / (row_full + column_energy)
            for q in range(nkap):
                row_factor = jnp.exp(-kappas[q] * row_full[:, :128])
                row_factor = jnp.concatenate([row_factor] * (cols // 128), axis=1)
                column_factor = jnp.exp(-kappas[q] * column_energy)
                damping = 1.0 - row_factor * column_factor
                amp[q, :, k * cols:(k + 1) * cols] = (ratio * damping * damping).astype(amp.dtype)

    rhs = jnp.concatenate(
        [ref[pl.ds(pl.multiple_of(step * P_TILE, P_TILE), P_TILE), :] for ref in partners], axis=1
    )
    for q in range(nkap):
        value = lax.dot_general(
            amp[q], rhs, (((1,), (1,)), ((), ())), preferred_element_type=jnp.float32
        )
        if has_partial:
            value = value + partial[q]
        out[q] = value.astype(out.dtype)


def add_terms(place, kappas, occ_energy, vir_rows, own, partners, blocks, partial, final):
    naux, rows = own.shape
    cols = partners[0].shape[1]
    nkap = kappas.shape[0]
    n = len(partners)
    whole = pl.BlockSpec(memory_space=pltpu.VMEM)
    scalars = pl.BlockSpec(memory_space=pltpu.SMEM)
    tile = pl.BlockSpec((nkap, rows, P_TILE), lambda p: (0, 0, p))
    in_specs = [scalars, scalars, scalars, whole, whole] + [whole] * n
    operands = [place, kappas, occ_energy, vir_rows, own] + list(partners)
    if partial is not None:
        in_specs.append(tile)
        operands.append(partial)
    if final:
        out_shape = jax.ShapeDtypeStruct((nkap, 1, rows, naux), jnp.bfloat16)
        out_spec = pl.BlockSpec((nkap, None, rows, P_TILE), lambda p: (0, 0, 0, p))
    else:
        out_shape = jax.ShapeDtypeStruct((nkap, rows, naux), jnp.float32)
        out_spec = tile
    flops = 2 * rows * cols * naux * n * (nkap + 1)
    moved = (n + 1) * naux * cols * 2 + nkap * rows * naux * (4 if partial is not None else 0)
    moved += nkap * rows * naux * (2 if final else 4)
    return pl.pallas_call(
        functools.partial(terms_kernel, blocks, partial is not None),
        out_shape=out_shape,
        grid=(naux // P_TILE,),
        in_specs=in_specs,
        out_specs=out_spec,
        scratch_shapes=[pltpu.VMEM((nkap, rows, n * cols), jnp.bfloat16)],
        compiler_params=pltpu.CompilerParams(vmem_limit_bytes=40 * 1024 * 1024),
        cost_estimate=pl.CostEstimate(flops=flops, bytes_accessed=moved, transcendentals=0),
    )(*operands)


def pair_terms(integrals, vir_coeff, occ_energy, vir_energy, kappas):
    aux_local, occ_count, basis = integrals.shape
    vir_local = vir_coeff.shape[1]
    wide_index = lax.axis_index("wide")
    batch_index = lax.axis_index("batch")
    place = jnp.stack(
        [wide_index, batch_index, jnp.full((), occ_count, wide_index.dtype)]
    ).astype(jnp.int32)
    vir_rows = vir_energy.reshape(-1, vir_local)
    flat_ints = integrals.reshape(aux_local * occ_count, basis)
    transformed = jnp.dot(flat_ints, vir_coeff, preferred_element_type=jnp.float32).astype(
        jnp.bfloat16
    )
    transformed = transformed.reshape(aux_local, occ_count, vir_local)
    own = lax.all_to_all(transformed, "wide", split_axis=1, concat_axis=0, tiled=True)[:, 0, :]

    own_o = from_behind(own, "batch", 1)
    first = shift_by_parity(own, "wide", -HALF)
    sibling = swap_pairs(own, "wide")
    second = shift_by_parity(own, "wide", HALF)
    third = swap_pairs(first, "wide")
    sibling_o = swap_pairs(own_o, "wide")
    first_o = from_behind(first, "batch", 1)
    second_o = from_behind(second, "batch", 1)
    third_o = swap_pairs(first_o, "wide")

    step = functools.partial(add_terms, place, kappas, occ_energy, vir_rows, own)
    density = step([own, sibling, own_o, sibling_o], [(0, 0), (1, 0), (0, 1), (1, 1)], None, False)
    density = step([first, third, second], [(2, 0), (-1, 0), (-2, 0)], density, False)
    return step([first_o, third_o, second_o], [(2, 1), (-1, 1), (-2, 1)], density, True)


def pair_density(own_slice, partner, own_energy, partner_energy, row_energy, vir_energy, kappas):
    coulomb = lax.dot_general(
        own_slice, partner, (((0,), (0,)), ((), ())), preferred_element_type=jnp.float32
    )
    denominator = row_energy[:, None] + vir_energy[None, :] - own_energy - partner_energy
    damping = 1.0 - jnp.exp(-kappas[:, None, None] * denominator[None])
    amplitude = (-coulomb[None] * (damping * damping) / denominator[None]).astype(jnp.bfloat16)
    flat = amplitude.reshape(-1, amplitude.shape[2])
    density = lax.dot_general(
        flat, partner, (((1,), (1,)), ((), ())), preferred_element_type=jnp.float32
    )
    return density.reshape(kappas.shape[0], own_slice.shape[1], partner.shape[0])


def ring_terms(integrals, vir_coeff, occ_energy, vir_energy, kappas):
    aux_local, occ_count, basis = integrals.shape
    vir_local = vir_coeff.shape[1]
    batch_index = lax.axis_index("batch")
    wide_index = lax.axis_index("wide")
    flat_ints = integrals.reshape(aux_local * occ_count, basis)
    row_energy = lax.dynamic_slice_in_dim(vir_energy, batch_index * vir_local, vir_local, 0)
    own_energy = lax.dynamic_slice_in_dim(occ_energy, wide_index, 1, 0)[0]

    def term(partner, offset, own_slice):
        partner_index = (wide_index + offset) % occ_count
        partner_energy = lax.dynamic_slice_in_dim(occ_energy, partner_index, 1, 0)[0]
        return pair_density(
            own_slice, partner, own_energy, partner_energy, row_energy, vir_energy, kappas
        )

    transformed = jnp.dot(flat_ints, vir_coeff, preferred_element_type=jnp.float32).astype(
        jnp.bfloat16
    )
    transformed = transformed.reshape(aux_local, occ_count, vir_local)
    own_slice = lax.all_to_all(transformed, "wide", split_axis=1, concat_axis=0, tiled=True)[
        :, 0, :
    ]
    own_full = lax.all_gather(own_slice, "batch", axis=1, tiled=True)
    density = term(own_full, 0, own_slice)
    upper = own_full
    lower = own_full
    for offset in range(1, HALF + 1):
        upper = from_behind(upper, "wide", -1)
        lower = from_behind(lower, "wide", 1)
        density = density + term(upper, offset, own_slice) + term(lower, -offset, own_slice)
    return density.astype(jnp.bfloat16)[:, None, :, :]


def solution(mesh):
    paired = mesh.shape["batch"] == 2 and mesh.shape["wide"] % 2 == 0
    return jax.shard_map(
        pair_terms if paired else ring_terms,
        mesh=mesh,
        in_specs=(P("wide", None, None), P(None, "batch"), P(), P(), P()),
        out_specs=P(None, "wide", "batch", None),
        check_vma=False,
    )
```

```python
import functools

import jax
import jax.numpy as jnp
from jax import lax
from jax.experimental import pallas as pl
from jax.experimental.pallas import tpu as pltpu
from jax.sharding import PartitionSpec as P

HALF = 2
P_TILE = 256


def from_behind(shard, axis, by):
    peers = lax.axis_size(axis)
    return lax.ppermute(shard, axis, [(i, (i + by) % peers) for i in range(peers)])


def swap_pairs(shard, axis):
    peers = lax.axis_size(axis)
    return lax.ppermute(shard, axis, [(i, i ^ 1) for i in range(peers)])


def shift_by_parity(shard, axis, even_by):
    peers = lax.axis_size(axis)
    return lax.ppermute(
        shard,
        axis,
        [(i, (i + (even_by if i % 2 == 0 else -even_by)) % peers) for i in range(peers)],
    )


def terms_kernel(
    blocks, has_partial, place, kappas, occ_energy, vir_rows, own, *refs
):
    n = len(blocks)
    partners = refs[:n]
    refs = refs[n:]
    partial = None
    if has_partial:
        partial, refs = refs[0], refs[1:]
    out, amp = refs
    nkap, rows = out.shape[0], own.shape[1]
    cols = partners[0].shape[1]
    step = pl.program_id(0)

    @pl.when(step == 0)
    def _():
        orbital, half, count = place[0], place[1], place[2]
        sign = 1 - 2 * lax.rem(orbital, 2)
        own_energy = occ_energy[orbital]
        row_energy = vir_rows[pl.ds(half, 1), :] - own_energy
        row_full = jnp.transpose(jnp.broadcast_to(row_energy, (128, rows)))
        row_full = jnp.concatenate([row_full] * (cols // 128), axis=1)
        own_t = jnp.transpose(own[...])
        for k, (offset, other) in enumerate(blocks):
            index = lax.rem(orbital + sign * offset + count, count)
            column_half = lax.rem(half + other, 2)
            column_energy = vir_rows[pl.ds(column_half, 1), :] - occ_energy[index]
            coulomb = jnp.dot(own_t, partners[k][...], preferred_element_type=jnp.float32)
            ratio = -coulomb / (row_full + column_energy)
            for q in range(nkap):
                row_factor = jnp.exp(-kappas[q] * row_full[:, :128])
                row_factor = jnp.concatenate([row_factor] * (cols // 128), axis=1)
                column_factor = jnp.exp(-kappas[q] * column_energy)
                damping = 1.0 - row_factor * column_factor
                amp[q * rows:(q + 1) * rows, k * cols:(k + 1) * cols] = (
                    ratio * damping * damping
                ).astype(amp.dtype)

    rhs = jnp.concatenate(
        [ref[pl.ds(pl.multiple_of(step * P_TILE, P_TILE), P_TILE), :] for ref in partners], axis=1
    )
    value = lax.dot_general(
        amp[...], rhs, (((1,), (1,)), ((), ())), preferred_element_type=jnp.float32
    ).reshape(nkap, rows, P_TILE)
    tile = pl.ds(pl.multiple_of(step * P_TILE, P_TILE), P_TILE)
    if has_partial:
        value = value + partial[:, :, tile]
    if out.shape[-1] == P_TILE:
        out[...] = value.astype(out.dtype)
    else:
        out[:, :, tile] = value.astype(out.dtype)


def add_terms(place, kappas, occ_energy, vir_rows, own, partners, blocks, partial, final):
    naux, rows = own.shape
    cols = partners[0].shape[1]
    nkap = kappas.shape[0]
    n = len(partners)
    whole = pl.BlockSpec(memory_space=pltpu.VMEM)
    scalars = pl.BlockSpec(memory_space=pltpu.SMEM)
    in_specs = [scalars, scalars, scalars, whole, whole] + [whole] * n
    operands = [place, kappas, occ_energy, vir_rows, own] + list(partners)
    if partial is not None:
        in_specs.append(whole)
        operands.append(partial)
    if final:
        out_shape = jax.ShapeDtypeStruct((nkap, 1, rows, naux), jnp.bfloat16)
        out_spec = pl.BlockSpec((nkap, None, rows, P_TILE), lambda p: (0, 0, 0, p))
    else:
        out_shape = jax.ShapeDtypeStruct((nkap, rows, naux), jnp.float32)
        out_spec = whole
    flops = 2 * rows * cols * naux * n * (nkap + 1)
    moved = (n + 1) * naux * cols * 2 + nkap * rows * naux * (4 if partial is not None else 0)
    moved += nkap * rows * naux * (2 if final else 4)
    return pl.pallas_call(
        functools.partial(terms_kernel, blocks, partial is not None),
        out_shape=out_shape,
        grid=(naux // P_TILE,),
        input_output_aliases={} if partial is None or final else {len(operands) - 1: 0},
        in_specs=in_specs,
        out_specs=out_spec,
        scratch_shapes=[pltpu.VMEM((nkap * rows, n * cols), jnp.bfloat16)],
        compiler_params=pltpu.CompilerParams(vmem_limit_bytes=28 * 1024 * 1024),
        cost_estimate=pl.CostEstimate(flops=flops, bytes_accessed=moved, transcendentals=0),
    )(*operands)


def pair_terms(integrals, vir_coeff, occ_energy, vir_energy, kappas):
    aux_local, occ_count, basis = integrals.shape
    vir_local = vir_coeff.shape[1]
    wide_index = lax.axis_index("wide")
    batch_index = lax.axis_index("batch")
    place = jnp.stack(
        [wide_index, batch_index, jnp.full((), occ_count, wide_index.dtype)]
    ).astype(jnp.int32)
    vir_rows = vir_energy.reshape(-1, vir_local)
    flat_ints = integrals.reshape(aux_local * occ_count, basis)
    transformed = jnp.dot(flat_ints, vir_coeff, preferred_element_type=jnp.float32).astype(
        jnp.bfloat16
    )
    transformed = transformed.reshape(aux_local, occ_count, vir_local)
    own = lax.all_to_all(transformed, "wide", split_axis=1, concat_axis=0, tiled=True)[:, 0, :]

    step = functools.partial(add_terms, place, kappas, occ_energy, vir_rows, own)

    own_o = from_behind(own, "batch", 1)
    first = shift_by_parity(own, "wide", -HALF)
    sibling = swap_pairs(own, "wide")
    density = step([own, sibling], [(0, 0), (1, 0)], None, False)
    own_after, first, density = lax.optimization_barrier((own, first, density))

    second = shift_by_parity(own_after, "wide", HALF)
    own_o, first = lax.optimization_barrier((own_o, first))
    first_o = from_behind(first, "batch", 1)
    third = swap_pairs(first, "wide")
    sibling_o = swap_pairs(own_o, "wide")
    density = step(
        [own_o, sibling_o, first, third], [(0, 1), (1, 1), (2, 0), (-1, 0)], density, False
    )
    second, first_o, density = lax.optimization_barrier((second, first_o, density))
    second_o = from_behind(second, "batch", 1)
    third_o = swap_pairs(first_o, "wide")
    density = step([second, first_o, third_o], [(-2, 0), (2, 1), (-1, 1)], density, False)
    return step([second_o], [(-2, 1)], density, True)


def pair_density(own_slice, partner, own_energy, partner_energy, row_energy, vir_energy, kappas):
    coulomb = lax.dot_general(
        own_slice, partner, (((0,), (0,)), ((), ())), preferred_element_type=jnp.float32
    )
    denominator = row_energy[:, None] + vir_energy[None, :] - own_energy - partner_energy
    damping = 1.0 - jnp.exp(-kappas[:, None, None] * denominator[None])
    amplitude = (-coulomb[None] * (damping * damping) / denominator[None]).astype(jnp.bfloat16)
    flat = amplitude.reshape(-1, amplitude.shape[2])
    density = lax.dot_general(
        flat, partner, (((1,), (1,)), ((), ())), preferred_element_type=jnp.float32
    )
    return density.reshape(kappas.shape[0], own_slice.shape[1], partner.shape[0])


def ring_terms(integrals, vir_coeff, occ_energy, vir_energy, kappas):
    aux_local, occ_count, basis = integrals.shape
    vir_local = vir_coeff.shape[1]
    batch_index = lax.axis_index("batch")
    wide_index = lax.axis_index("wide")
    flat_ints = integrals.reshape(aux_local * occ_count, basis)
    row_energy = lax.dynamic_slice_in_dim(vir_energy, batch_index * vir_local, vir_local, 0)
    own_energy = lax.dynamic_slice_in_dim(occ_energy, wide_index, 1, 0)[0]

    def term(partner, offset, own_slice):
        partner_index = (wide_index + offset) % occ_count
        partner_energy = lax.dynamic_slice_in_dim(occ_energy, partner_index, 1, 0)[0]
        return pair_density(
            own_slice, partner, own_energy, partner_energy, row_energy, vir_energy, kappas
        )

    transformed = jnp.dot(flat_ints, vir_coeff, preferred_element_type=jnp.float32).astype(
        jnp.bfloat16
    )
    transformed = transformed.reshape(aux_local, occ_count, vir_local)
    own_slice = lax.all_to_all(transformed, "wide", split_axis=1, concat_axis=0, tiled=True)[
        :, 0, :
    ]
    own_full = lax.all_gather(own_slice, "batch", axis=1, tiled=True)
    density = term(own_full, 0, own_slice)
    upper = own_full
    lower = own_full
    for offset in range(1, HALF + 1):
        upper = from_behind(upper, "wide", -1)
        lower = from_behind(lower, "wide", 1)
        density = density + term(upper, offset, own_slice) + term(lower, -offset, own_slice)
    return density.astype(jnp.bfloat16)[:, None, :, :]


def solution(mesh):
    paired = mesh.shape["batch"] == 2 and mesh.shape["wide"] % 2 == 0
    return jax.shard_map(
        pair_terms if paired else ring_terms,
        mesh=mesh,
        in_specs=(P("wide", None, None), P(None, "batch"), P(), P(), P()),
        out_specs=P(None, "wide", "batch", None),
        check_vma=False,
    )
```

```python
import functools

import jax
import jax.numpy as jnp
from jax import lax
from jax.experimental import pallas as pl
from jax.experimental.pallas import tpu as pltpu
from jax.sharding import PartitionSpec as P

HALF = 2
P_TILE = 256


def from_behind(shard, axis, by):
    peers = lax.axis_size(axis)
    return lax.ppermute(shard, axis, [(i, (i + by) % peers) for i in range(peers)])


def swap_pairs(shard, axis):
    peers = lax.axis_size(axis)
    return lax.ppermute(shard, axis, [(i, i ^ 1) for i in range(peers)])


def shift_by_parity(shard, axis, even_by):
    peers = lax.axis_size(axis)
    return lax.ppermute(
        shard,
        axis,
        [(i, (i + (even_by if i % 2 == 0 else -even_by)) % peers) for i in range(peers)],
    )


def terms_kernel(blocks, has_partial, place, kappas, occ_energy, vir_rows, own_a, own_b, *refs):
    n = len(blocks)
    partners = refs[:2 * n]
    refs = refs[2 * n:]
    partial = None
    if has_partial:
        partial, refs = refs[0], refs[1:]
    out, amp, turned = refs
    nkap = out.shape[0]
    rows = 2 * own_a.shape[1]
    cols = rows
    step = pl.program_id(0)

    @pl.when(step == 0)
    def _():
        orbital, half, count = place[0], place[1], place[2]
        sign = 1 - 2 * lax.rem(orbital, 2)
        row_energy = vir_rows[pl.ds(half, 1), :] - occ_energy[orbital]

        def down_columns(row):
            tall = jnp.transpose(jnp.broadcast_to(row, (128, rows)))
            return jnp.concatenate([tall] * (cols // 128), axis=1)

        row_full = down_columns(row_energy)
        row_factors = [down_columns(jnp.exp(-kappas[q] * row_energy)) for q in range(nkap)]
        own_t = jnp.concatenate([jnp.transpose(own_a[...]), jnp.transpose(own_b[...])], axis=0)
        for k, (offset, other) in enumerate(blocks):
            index = lax.rem(orbital + sign * offset + count, count)
            column_half = lax.rem(half + other, 2)
            column_energy = vir_rows[pl.ds(column_half, 1), :] - occ_energy[index]
            partner = jnp.concatenate([partners[2 * k][...], partners[2 * k + 1][...]], axis=1)
            turned[k * cols:(k + 1) * cols, :] = jnp.transpose(partner)
            coulomb = jnp.dot(own_t, partner, preferred_element_type=jnp.float32)
            ratio = -coulomb / (row_full + column_energy)
            for q in range(nkap):
                damping = 1.0 - row_factors[q] * jnp.exp(-kappas[q] * column_energy)
                amp[q * rows:(q + 1) * rows, k * cols:(k + 1) * cols] = (
                    ratio * damping * damping
                ).astype(amp.dtype)

    tile = pl.ds(pl.multiple_of(step * P_TILE, P_TILE), P_TILE)
    value = jnp.dot(amp[...], turned[:, tile], preferred_element_type=jnp.float32).reshape(
        nkap, rows, P_TILE
    )
    if has_partial:
        value = value + partial[:, :, tile]
    if out.shape[-1] == P_TILE:
        out[...] = value.astype(out.dtype)
    else:
        out[:, :, tile] = value.astype(out.dtype)


def add_terms(place, kappas, occ_energy, vir_rows, own, partners, blocks, partial, final):
    naux = own[0].shape[0]
    rows = own[0].shape[1] + own[1].shape[1]
    cols = rows
    nkap = kappas.shape[0]
    n = len(partners)
    whole = pl.BlockSpec(memory_space=pltpu.VMEM)
    scalars = pl.BlockSpec(memory_space=pltpu.SMEM)
    in_specs = [scalars, scalars, scalars] + [whole] * (3 + 2 * n)
    operands = [place, kappas, occ_energy, vir_rows] + list(own)
    for pair in partners:
        operands.extend(pair)
    if partial is not None:
        in_specs.append(whole)
        operands.append(partial)
    if final:
        out_shape = jax.ShapeDtypeStruct((nkap, 1, rows, naux), jnp.bfloat16)
        out_spec = pl.BlockSpec((nkap, None, rows, P_TILE), lambda p: (0, 0, 0, p))
    else:
        out_shape = jax.ShapeDtypeStruct((nkap, rows, naux), jnp.float32)
        out_spec = whole
    flops = 2 * rows * cols * naux * n * (nkap + 1)
    moved = (n + 1) * naux * cols * 2 + nkap * rows * naux * (4 if partial is not None else 0)
    moved += nkap * rows * naux * (2 if final else 4)
    return pl.pallas_call(
        functools.partial(terms_kernel, blocks, partial is not None),
        out_shape=out_shape,
        grid=(naux // P_TILE,),
        input_output_aliases={} if partial is None or final else {len(operands) - 1: 0},
        in_specs=in_specs,
        out_specs=out_spec,
        scratch_shapes=[
            pltpu.VMEM((nkap * rows, n * cols), jnp.bfloat16),
            pltpu.VMEM((n * cols, naux), jnp.bfloat16),
        ],
        compiler_params=pltpu.CompilerParams(vmem_limit_bytes=28 * 1024 * 1024),
        cost_estimate=pl.CostEstimate(flops=flops, bytes_accessed=moved, transcendentals=0),
    )(*operands)


def after(value, *others):
    return lax.optimization_barrier((value,) + others)[0]


def pair_terms(integrals, vir_coeff, occ_energy, vir_energy, kappas):
    aux_local, occ_count, basis = integrals.shape
    vir_local = vir_coeff.shape[1]
    wide_index = lax.axis_index("wide")
    batch_index = lax.axis_index("batch")
    place = jnp.stack(
        [wide_index, batch_index, jnp.full((), occ_count, wide_index.dtype)]
    ).astype(jnp.int32)
    vir_rows = vir_energy.reshape(-1, vir_local)
    flat_ints = integrals.reshape(aux_local * occ_count, basis)
    transformed = jnp.dot(flat_ints, vir_coeff, preferred_element_type=jnp.float32).astype(
        jnp.bfloat16
    )
    transformed = transformed.reshape(aux_local, occ_count, vir_local)

    def to_owner(columns):
        return lax.all_to_all(columns, "wide", split_axis=1, concat_axis=0, tiled=True)[:, 0, :]

    def over_batch(value):
        return from_behind(value, "batch", 1)

    def over_cores(value):
        return swap_pairs(value, "wide")

    def to_first(value):
        return shift_by_parity(value, "wide", -HALF)

    def to_second(value):
        return shift_by_parity(value, "wide", HALF)

    cut = vir_local // 2
    step = functools.partial(add_terms, place, kappas, occ_energy, vir_rows)

    low, high = transformed[:, :, :cut], transformed[:, :, cut:]
    own_low = to_owner(low)
    own_o_low = over_batch(own_low)
    first_low = to_first(own_low)
    sibling_low = over_cores(own_low)

    own_high = to_owner(after(high, sibling_low))
    own = [own_low, own_high]
    own_o_high = over_batch(own_high)
    sibling_high = over_cores(own_high)
    first_high = to_first(after(own_high, first_low))
    first_o_low = over_batch(first_low)
    third_low = over_cores(first_low)
    own_o = [own_o_low, own_o_high]
    sibling = [sibling_low, sibling_high]
    density = step(own, [own, sibling], [(0, 0), (1, 0)], None, False)

    own_low_b, first_high, own_o_high, density = lax.optimization_barrier(
        (own_low, first_high, own_o_high, density)
    )
    own_o = [own_o_low, own_o_high]
    first = [first_low, first_high]
    second_low = to_second(own_low_b)
    first_o_high = over_batch(first_high)
    third_high = over_cores(first_high)
    sibling_o = [over_cores(own_o_low), over_cores(own_o_high)]
    density = step(own, [own_o, sibling_o], [(0, 1), (1, 1)], density, False)

    second_high = to_second(after(own_high, second_low, density))
    second_o_high = to_second(after(own_o_high, second_low, density))
    third = [third_low, third_high]
    density = step(own, [first, third], [(2, 0), (-1, 0)], density, False)

    second_o_low = over_batch(after(second_low, first_o_high))
    first_o = [first_o_low, first_o_high]
    third_o = [over_cores(after(value, density)) for value in first_o]
    density = step(own, [first_o, third_o], [(2, 1), (-1, 1)], density, False)
    second = [second_low, second_high]
    second_o = [second_o_low, second_o_high]
    return step(own, [second, second_o], [(-2, 0), (-2, 1)], density, True)


def pair_density(own_slice, partner, own_energy, partner_energy, row_energy, vir_energy, kappas):
    coulomb = lax.dot_general(
        own_slice, partner, (((0,), (0,)), ((), ())), preferred_element_type=jnp.float32
    )
    denominator = row_energy[:, None] + vir_energy[None, :] - own_energy - partner_energy
    damping = 1.0 - jnp.exp(-kappas[:, None, None] * denominator[None])
    amplitude = (-coulomb[None] * (damping * damping) / denominator[None]).astype(jnp.bfloat16)
    flat = amplitude.reshape(-1, amplitude.shape[2])
    density = lax.dot_general(
        flat, partner, (((1,), (1,)), ((), ())), preferred_element_type=jnp.float32
    )
    return density.reshape(kappas.shape[0], own_slice.shape[1], partner.shape[0])


def ring_terms(integrals, vir_coeff, occ_energy, vir_energy, kappas):
    aux_local, occ_count, basis = integrals.shape
    vir_local = vir_coeff.shape[1]
    batch_index = lax.axis_index("batch")
    wide_index = lax.axis_index("wide")
    flat_ints = integrals.reshape(aux_local * occ_count, basis)
    row_energy = lax.dynamic_slice_in_dim(vir_energy, batch_index * vir_local, vir_local, 0)
    own_energy = lax.dynamic_slice_in_dim(occ_energy, wide_index, 1, 0)[0]

    def term(partner, offset, own_slice):
        partner_index = (wide_index + offset) % occ_count
        partner_energy = lax.dynamic_slice_in_dim(occ_energy, partner_index, 1, 0)[0]
        return pair_density(
            own_slice, partner, own_energy, partner_energy, row_energy, vir_energy, kappas
        )

    transformed = jnp.dot(flat_ints, vir_coeff, preferred_element_type=jnp.float32).astype(
        jnp.bfloat16
    )
    transformed = transformed.reshape(aux_local, occ_count, vir_local)
    own_slice = lax.all_to_all(transformed, "wide", split_axis=1, concat_axis=0, tiled=True)[
        :, 0, :
    ]
    own_full = lax.all_gather(own_slice, "batch", axis=1, tiled=True)
    density = term(own_full, 0, own_slice)
    upper = own_full
    lower = own_full
    for offset in range(1, HALF + 1):
        upper = from_behind(upper, "wide", -1)
        lower = from_behind(lower, "wide", 1)
        density = density + term(upper, offset, own_slice) + term(lower, -offset, own_slice)
    return density.astype(jnp.bfloat16)[:, None, :, :]


def solution(mesh):
    paired = mesh.shape["batch"] == 2 and mesh.shape["wide"] % 2 == 0

    return jax.shard_map(
        pair_terms if paired else ring_terms,
        mesh=mesh,
        in_specs=(P("wide", None, None), P(None, "batch"), P(), P(), P()),
        out_specs=P(None, "wide", "batch", None),
        check_vma=False,
    )
```

```python
import functools

import jax
import jax.numpy as jnp
from jax import lax
from jax.experimental import pallas as pl
from jax.experimental.pallas import tpu as pltpu
from jax.sharding import PartitionSpec as P

HALF = 2
P_TILE = 256
LANES = 128


def from_behind(shard, axis, by):
    peers = lax.axis_size(axis)
    return lax.ppermute(shard, axis, [(i, (i + by) % peers) for i in range(peers)])


def swap_by(shard, axis, bit):
    peers = lax.axis_size(axis)
    return lax.ppermute(shard, axis, [(i, i ^ bit) for i in range(peers)])


def hand_along(shard, axis):
    peers = lax.axis_size(axis)
    return lax.ppermute(
        shard,
        axis,
        [(i, (i + (4 if i // 2 % 2 == 0 else -4)) % peers) for i in range(peers)],
    )


def prepare_kernel(place, kappas, occ_energy, vir_rows, own, own_t, row_energies, row_factors):
    rows = own.shape[1]
    row_energy = vir_rows[pl.ds(place[1], 1), :] - occ_energy[place[0]]

    def down_columns(row):
        return jnp.transpose(jnp.broadcast_to(row, (LANES, rows)))

    own_t[...] = jnp.transpose(own[...])
    row_energies[...] = down_columns(row_energy)
    for q in range(row_factors.shape[0]):
        row_factors[q] = down_columns(jnp.exp(-kappas[q] * row_energy))


def prepare(scalars, vir_rows, own):
    naux, rows = own.shape
    nkap = scalars[1].shape[0]
    vmem = pl.BlockSpec(memory_space=pltpu.VMEM)
    smem = pl.BlockSpec(memory_space=pltpu.SMEM)
    return pl.pallas_call(
        prepare_kernel,
        out_shape=(
            jax.ShapeDtypeStruct((rows, naux), own.dtype),
            jax.ShapeDtypeStruct((rows, LANES), jnp.float32),
            jax.ShapeDtypeStruct((nkap, rows, LANES), jnp.float32),
        ),
        in_specs=[smem, smem, smem, vmem, vmem],
        out_specs=(vmem, vmem, vmem),
        compiler_params=pltpu.CompilerParams(vmem_limit_bytes=28 * 1024 * 1024),
    )(*scalars, vir_rows, own)


def terms_kernel(
    pieces, has_partial, place, kappas, occ_energy, vir_rows, own_t, row_energies, row_factors, *refs
):
    partners = refs[:len(pieces)]
    refs = refs[len(pieces):]
    partial = None
    if has_partial:
        partial, refs = refs[0], refs[1:]
    out, amp = refs
    nkap, rows = row_factors.shape[0], row_factors.shape[1]
    p_tile = P_TILE
    step = pl.program_id(0)

    @pl.when(step == 0)
    def _():
        orbital, half, count = place[0], place[1], place[2]
        core_sign = 1 - 2 * lax.rem(orbital, 2)
        pair_sign = 1 - 2 * lax.rem(lax.div(orbital, 2), 2)
        offsets = dict(
            own=0, sibling=core_sign, third=-core_sign, near=HALF * pair_sign, far=-HALF * pair_sign
        )
        at = 0
        for (name, other, start), partner in zip(pieces, partners):
            width = partner.shape[1]
            index = lax.rem(orbital + offsets[name] + count, count)
            column_half = lax.rem(half + other, 2)
            column_energy = vir_rows[pl.ds(column_half, 1), :] - occ_energy[index]
            column_energy = column_energy[:, start:start + width]
            column_factors = [jnp.exp(-kappas[q] * column_energy) for q in range(nkap)]
            coulomb = jnp.dot(own_t[...], partner[...], preferred_element_type=jnp.float32)
            for c in range(0, width, LANES):
                ratio = -coulomb[:, c:c + LANES] / (
                    row_energies[...] + column_energy[:, c:c + LANES]
                )
                for q in range(nkap):
                    damping = 1.0 - row_factors[q] * column_factors[q][:, c:c + LANES]
                    amp[q * rows:(q + 1) * rows, at + c:at + c + LANES] = (
                        ratio * damping * damping
                    ).astype(amp.dtype)
            at += width

    tile = pl.ds(pl.multiple_of(step * p_tile, p_tile), p_tile)
    rhs = jnp.concatenate([partner[tile, :] for partner in partners], axis=1)
    value = lax.dot_general(
        amp[...], rhs, (((1,), (1,)), ((), ())), preferred_element_type=jnp.float32
    ).reshape(nkap, rows, p_tile)
    if has_partial:
        value = value + partial[:, :, tile]
    if out.shape[-1] == p_tile:
        out[...] = value.astype(out.dtype)
    else:
        out[:, :, tile] = value.astype(out.dtype)


def add_terms(scalars, vir_rows, prepared, partners, partial, final=False):
    rows, naux = prepared[0].shape
    nkap = prepared[2].shape[0]
    pieces = tuple(partner[:3] for partner in partners)
    arrays = [partner[3] for partner in partners]
    vmem = pl.BlockSpec(memory_space=pltpu.VMEM)
    smem = pl.BlockSpec(memory_space=pltpu.SMEM)
    operands = list(scalars) + [vir_rows] + list(prepared) + arrays
    if partial is not None:
        operands.append(partial)
    in_specs = [smem] * len(scalars) + [vmem] * (len(operands) - len(scalars))
    if final:
        out_shape = jax.ShapeDtypeStruct((nkap, 1, rows, naux), jnp.bfloat16)
        out_spec = pl.BlockSpec((nkap, None, rows, P_TILE), lambda p: (0, 0, 0, p))
    else:
        out_shape = jax.ShapeDtypeStruct((nkap, rows, naux), jnp.float32)
        out_spec = vmem
    width = sum(array.shape[1] for array in arrays)
    return pl.pallas_call(
        functools.partial(terms_kernel, pieces, partial is not None),
        out_shape=out_shape,
        grid=(naux // P_TILE,),
        input_output_aliases={} if partial is None or final else {len(operands) - 1: 0},
        in_specs=in_specs,
        out_specs=out_spec,
        scratch_shapes=[pltpu.VMEM((nkap * rows, width), jnp.bfloat16)],
        compiler_params=pltpu.CompilerParams(vmem_limit_bytes=28 * 1024 * 1024),
        cost_estimate=pl.CostEstimate(flops=1, bytes_accessed=1, transcendentals=0),
    )(*operands)


def pair_terms(integrals, vir_coeff, occ_energy, vir_energy, kappas):
    aux_local, occ_count, basis = integrals.shape
    vir_local = vir_coeff.shape[1]
    wide_index = lax.axis_index("wide")
    batch_index = lax.axis_index("batch")
    place = jnp.stack(
        [wide_index, batch_index, jnp.full((), occ_count, wide_index.dtype)]
    ).astype(jnp.int32)
    vir_rows = vir_energy.reshape(-1, vir_local)
    flat_ints = integrals.reshape(aux_local * occ_count, basis)
    transformed = jnp.dot(flat_ints, vir_coeff, preferred_element_type=jnp.float32).astype(
        jnp.bfloat16
    )
    transformed = transformed.reshape(aux_local, occ_count, vir_local)

    def to_owner(columns):
        return lax.all_to_all(columns, "wide", split_axis=1, concat_axis=0, tiled=True)[:, 0, :]

    def over_batch(value):
        return from_behind(value, "batch", 1)

    def over_cores(value):
        return swap_by(value, "wide", 1)

    def over_pairs(value):
        return swap_by(value, "wide", 2)

    def along(value):
        return hand_along(value, "wide")

    sends_near = wide_index % 2 == wide_index // 2 % 2

    def for_sibling(near, far):
        return over_cores(jnp.where(sends_near, near, far))

    together = lax.optimization_barrier
    scalars = (place, kappas, occ_energy)
    own = to_owner(transformed)
    cut = vir_local // 2
    low, high = own[:, :cut], own[:, cut:]

    own_o_high = over_batch(high)
    near_low = over_pairs(low)
    sibling = over_cores(own)
    step = functools.partial(add_terms, scalars, vir_rows, prepare(scalars, vir_rows, own))
    density = step([("own", 0, 0, own), ("sibling", 0, 0, sibling)], None)

    low, high, own_o_high, near_low, density = together((low, high, own_o_high, near_low, density))
    own_o_low = over_batch(low)
    near_high = over_pairs(high)
    far_low = along(near_low)
    sibling_o_high = over_cores(own_o_high)
    density = step(
        [
            ("own", 1, cut, own_o_high),
            ("near", 0, 0, near_low),
            ("sibling", 1, cut, sibling_o_high),
        ],
        density,
    )

    own_o_low, own_o_high, near_low, near_high, far_low, density = together(
        (own_o_low, own_o_high, near_low, near_high, far_low, density)
    )
    near_o_low = over_batch(near_low)
    near_o_high = over_pairs(own_o_high)
    far_high = along(near_high)
    sibling_o_low = over_cores(own_o_low)
    third_low = for_sibling(near_low, far_low)
    density = step(
        [
            ("own", 1, 0, own_o_low),
            ("near", 0, cut, near_high),
            ("far", 0, 0, far_low),
            ("sibling", 1, 0, sibling_o_low),
            ("third", 0, 0, third_low),
        ],
        density,
    )

    near_high, near_o_low, near_o_high, far_low, far_high, density = together(
        (near_high, near_o_low, near_o_high, far_low, far_high, density)
    )
    far_o_low = over_batch(far_low)
    far_o_high = along(near_o_high)
    third_high = for_sibling(near_high, far_high)
    density = step(
        [
            ("near", 1, 0, near_o_low),
            ("near", 1, cut, near_o_high),
            ("far", 0, cut, far_high),
            ("third", 0, cut, third_high),
        ],
        density,
    )

    far_o_low, far_o_high, density = together((far_o_low, far_o_high, density))
    third_o_low = for_sibling(near_o_low, far_o_low)
    third_o_high = for_sibling(near_o_high, far_o_high)
    return step(
        [
            ("far", 1, 0, far_o_low),
            ("far", 1, cut, far_o_high),
            ("third", 1, 0, third_o_low),
            ("third", 1, cut, third_o_high),
        ],
        density,
        True,
    )


def pair_density(own_slice, partner, own_energy, partner_energy, row_energy, vir_energy, kappas):
    coulomb = lax.dot_general(
        own_slice, partner, (((0,), (0,)), ((), ())), preferred_element_type=jnp.float32
    )
    denominator = row_energy[:, None] + vir_energy[None, :] - own_energy - partner_energy
    damping = 1.0 - jnp.exp(-kappas[:, None, None] * denominator[None])
    amplitude = (-coulomb[None] * (damping * damping) / denominator[None]).astype(jnp.bfloat16)
    flat = amplitude.reshape(-1, amplitude.shape[2])
    density = lax.dot_general(
        flat, partner, (((1,), (1,)), ((), ())), preferred_element_type=jnp.float32
    )
    return density.reshape(kappas.shape[0], own_slice.shape[1], partner.shape[0])


def ring_terms(integrals, vir_coeff, occ_energy, vir_energy, kappas):
    aux_local, occ_count, basis = integrals.shape
    vir_local = vir_coeff.shape[1]
    batch_index = lax.axis_index("batch")
    wide_index = lax.axis_index("wide")
    flat_ints = integrals.reshape(aux_local * occ_count, basis)
    row_energy = lax.dynamic_slice_in_dim(vir_energy, batch_index * vir_local, vir_local, 0)
    own_energy = lax.dynamic_slice_in_dim(occ_energy, wide_index, 1, 0)[0]

    def term(partner, offset, own_slice):
        partner_index = (wide_index + offset) % occ_count
        partner_energy = lax.dynamic_slice_in_dim(occ_energy, partner_index, 1, 0)[0]
        return pair_density(
            own_slice, partner, own_energy, partner_energy, row_energy, vir_energy, kappas
        )

    transformed = jnp.dot(flat_ints, vir_coeff, preferred_element_type=jnp.float32).astype(
        jnp.bfloat16
    )
    transformed = transformed.reshape(aux_local, occ_count, vir_local)
    own_slice = lax.all_to_all(transformed, "wide", split_axis=1, concat_axis=0, tiled=True)[
        :, 0, :
    ]
    own_full = lax.all_gather(own_slice, "batch", axis=1, tiled=True)
    density = term(own_full, 0, own_slice)
    upper = own_full
    lower = own_full
    for offset in range(1, HALF + 1):
        upper = from_behind(upper, "wide", -1)
        lower = from_behind(lower, "wide", 1)
        density = density + term(upper, offset, own_slice) + term(lower, -offset, own_slice)
    return density.astype(jnp.bfloat16)[:, None, :, :]


def solution(mesh):
    paired = mesh.shape["batch"] == 2 and mesh.shape["wide"] % 4 == 0

    return jax.shard_map(
        pair_terms if paired else ring_terms,
        mesh=mesh,
        in_specs=(P("wide", None, None), P(None, "batch"), P(), P(), P()),
        out_specs=P(None, "wide", "batch", None),
        check_vma=False,
    )
```

```python
import functools

import jax
import jax.numpy as jnp
from jax import lax
from jax.experimental import pallas as pl
from jax.experimental.pallas import tpu as pltpu
from jax.sharding import PartitionSpec as P

HALF = 2
P_TILE = 256
WIDE_TILE = 512
LANES = 128


def from_behind(shard, axis, by):
    peers = lax.axis_size(axis)
    return lax.ppermute(shard, axis, [(i, (i + by) % peers) for i in range(peers)])


def swap_by(shard, axis, bit):
    peers = lax.axis_size(axis)
    return lax.ppermute(shard, axis, [(i, i ^ bit) for i in range(peers)])


def hand_along(shard, axis):
    peers = lax.axis_size(axis)
    return lax.ppermute(
        shard,
        axis,
        [(i, (i + (4 if i // 2 % 2 == 0 else -4)) % peers) for i in range(peers)],
    )


def prepare_kernel(place, kappas, occ_energy, vir_rows, own, own_t, row_energies, row_factors):
    rows = own.shape[1]
    row_energy = vir_rows[pl.ds(place[1], 1), :] - occ_energy[place[0]]

    def down_columns(row):
        return jnp.transpose(jnp.broadcast_to(row, (LANES, rows)))

    own_t[...] = jnp.transpose(own[...])
    row_energies[...] = down_columns(row_energy)
    for q in range(row_factors.shape[0]):
        row_factors[q] = down_columns(jnp.exp(-kappas[q] * row_energy))


def prepare(scalars, vir_rows, own):
    naux, rows = own.shape
    nkap = scalars[1].shape[0]
    vmem = pl.BlockSpec(memory_space=pltpu.VMEM)
    smem = pl.BlockSpec(memory_space=pltpu.SMEM)
    return pl.pallas_call(
        prepare_kernel,
        out_shape=(
            jax.ShapeDtypeStruct((rows, naux), own.dtype),
            jax.ShapeDtypeStruct((rows, LANES), jnp.float32),
            jax.ShapeDtypeStruct((nkap, rows, LANES), jnp.float32),
        ),
        in_specs=[smem, smem, smem, vmem, vmem],
        out_specs=(vmem, vmem, vmem),
        compiler_params=pltpu.CompilerParams(vmem_limit_bytes=18 * 1024 * 1024),
    )(*scalars, vir_rows, own)


def terms_kernel(
    pieces, has_partial, place, kappas, occ_energy, vir_rows, own_t, row_energies, row_factors, *refs
):
    partners = refs[:len(pieces)]
    refs = refs[len(pieces):]
    partial = None
    if has_partial:
        partial, refs = refs[0], refs[1:]
    out, amp = refs
    nkap, rows = row_factors.shape[0], row_factors.shape[1]
    naux = own_t.shape[1]

    def amplitudes():
        orbital, half, count = place[0], place[1], place[2]
        core_sign = 1 - 2 * lax.rem(orbital, 2)
        pair_sign = 1 - 2 * lax.rem(lax.div(orbital, 2), 2)
        offsets = dict(
            own=0, sibling=core_sign, third=-core_sign, near=HALF * pair_sign, far=-HALF * pair_sign
        )
        at = 0
        for (name, other, start), partner in zip(pieces, partners):
            width = partner.shape[1]
            index = lax.rem(orbital + offsets[name] + count, count)
            column_half = lax.rem(half + other, 2)
            column_energy = vir_rows[pl.ds(column_half, 1), :] - occ_energy[index]
            column_energy = column_energy[:, start:start + width]
            column_factors = [jnp.exp(-kappas[q] * column_energy) for q in range(nkap)]
            coulomb = jnp.dot(own_t[...], partner[...], preferred_element_type=jnp.float32)
            for c in range(0, width, LANES):
                ratio = -coulomb[:, c:c + LANES] / (
                    row_energies[...] + column_energy[:, c:c + LANES]
                )
                for q in range(nkap):
                    damping = 1.0 - row_factors[q] * column_factors[q][:, c:c + LANES]
                    amp[q * rows:(q + 1) * rows, at + c:at + c + LANES] = (
                        ratio * damping * damping
                    ).astype(amp.dtype)
            at += width

    def density(tile):
        rhs = jnp.concatenate([partner[tile, :] for partner in partners], axis=1)
        value = lax.dot_general(
            amp[...], rhs, (((1,), (1,)), ((), ())), preferred_element_type=jnp.float32
        ).reshape(nkap, rows, rhs.shape[0])
        return value if partial is None else value + partial[:, :, tile]

    if out.shape[-1] == naux:
        amplitudes()
        for start in range(0, naux, WIDE_TILE):
            tile = slice(start, start + WIDE_TILE)
            out[:, :, tile] = density(tile).astype(out.dtype)
    else:
        step = pl.program_id(0)
        pl.when(step == 0)(amplitudes)
        out[...] = density(
            pl.ds(pl.multiple_of(step * P_TILE, P_TILE), P_TILE)
        ).astype(out.dtype)


def add_terms(scalars, vir_rows, prepared, partners, partial, final=False):
    rows, naux = prepared[0].shape
    nkap = prepared[2].shape[0]
    pieces = tuple(partner[:3] for partner in partners)
    arrays = [partner[3] for partner in partners]
    vmem = pl.BlockSpec(memory_space=pltpu.VMEM)
    smem = pl.BlockSpec(memory_space=pltpu.SMEM)
    operands = list(scalars) + [vir_rows] + list(prepared) + arrays
    if partial is not None:
        operands.append(partial)
    in_specs = [smem] * len(scalars) + [vmem] * (len(operands) - len(scalars))
    if final:
        out_shape = jax.ShapeDtypeStruct((nkap, 1, rows, naux), jnp.bfloat16)
        out_spec = pl.BlockSpec((nkap, None, rows, P_TILE), lambda p: (0, 0, 0, p))
    else:
        out_shape = jax.ShapeDtypeStruct((nkap, rows, naux), jnp.float32)
        out_spec = vmem
    width = sum(array.shape[1] for array in arrays)
    return pl.pallas_call(
        functools.partial(terms_kernel, pieces, partial is not None),
        out_shape=out_shape,
        grid=(naux // P_TILE,) if final else (),
        input_output_aliases={} if partial is None or final else {len(operands) - 1: 0},
        in_specs=in_specs,
        out_specs=out_spec,
        scratch_shapes=[pltpu.VMEM((nkap * rows, width), jnp.bfloat16)],
        compiler_params=pltpu.CompilerParams(vmem_limit_bytes=18 * 1024 * 1024),
        cost_estimate=pl.CostEstimate(flops=1, bytes_accessed=1, transcendentals=0),
    )(*operands)


def pair_terms(integrals, vir_coeff, occ_energy, vir_energy, kappas):
    aux_local, occ_count, basis = integrals.shape
    vir_local = vir_coeff.shape[1]
    wide_index = lax.axis_index("wide")
    batch_index = lax.axis_index("batch")
    place = jnp.stack(
        [wide_index, batch_index, jnp.full((), occ_count, wide_index.dtype)]
    ).astype(jnp.int32)
    vir_rows = vir_energy.reshape(-1, vir_local)
    flat_ints = integrals.reshape(aux_local * occ_count, basis)
    transformed = jnp.dot(flat_ints, vir_coeff, preferred_element_type=jnp.float32).astype(
        jnp.bfloat16
    )
    transformed = transformed.reshape(aux_local, occ_count, vir_local)

    def to_owner(columns):
        return lax.all_to_all(columns, "wide", split_axis=1, concat_axis=0, tiled=True)[:, 0, :]

    def over_batch(value):
        return from_behind(value, "batch", 1)

    def over_cores(value):
        return swap_by(value, "wide", 1)

    def over_pairs(value):
        return swap_by(value, "wide", 2)

    def along(value):
        return hand_along(value, "wide")

    sends_near = wide_index % 2 == wide_index // 2 % 2

    def for_sibling(near, far):
        return over_cores(jnp.where(sends_near, near, far))

    together = lax.optimization_barrier
    scalars = (place, kappas, occ_energy)
    own = to_owner(transformed)
    cut = vir_local // 2
    low, high = own[:, :cut], own[:, cut:]

    own_o_high = over_batch(high)
    near_low = over_pairs(low)
    sibling = over_cores(own)
    step = functools.partial(add_terms, scalars, vir_rows, prepare(scalars, vir_rows, own))
    density = step([("own", 0, 0, own), ("sibling", 0, 0, sibling)], None)

    low, high, own_o_high, near_low, density = together((low, high, own_o_high, near_low, density))
    own_o_low = over_batch(low)
    near_high = over_pairs(high)
    far_low = along(near_low)
    sibling_o_high = over_cores(own_o_high)
    density = step(
        [
            ("own", 1, cut, own_o_high),
            ("near", 0, 0, near_low),
            ("sibling", 1, cut, sibling_o_high),
        ],
        density,
    )

    own_o_low, own_o_high, near_low, near_high, far_low, density = together(
        (own_o_low, own_o_high, near_low, near_high, far_low, density)
    )
    near_o_low = over_batch(near_low)
    near_o_high = over_pairs(own_o_high)
    far_high = along(near_high)
    sibling_o_low = over_cores(own_o_low)
    third_low = for_sibling(near_low, far_low)
    density = step(
        [
            ("own", 1, 0, own_o_low),
            ("near", 0, cut, near_high),
            ("far", 0, 0, far_low),
            ("sibling", 1, 0, sibling_o_low),
            ("third", 0, 0, third_low),
        ],
        density,
    )

    near_high, near_o_low, near_o_high, far_low, far_high, density = together(
        (near_high, near_o_low, near_o_high, far_low, far_high, density)
    )
    far_o_low = over_batch(far_low)
    far_o_high = along(near_o_high)
    third_high = for_sibling(near_high, far_high)
    density = step(
        [
            ("near", 1, 0, near_o_low),
            ("near", 1, cut, near_o_high),
            ("far", 0, cut, far_high),
            ("third", 0, cut, third_high),
        ],
        density,
    )

    far_o_low, far_o_high, density = together((far_o_low, far_o_high, density))
    third_o_low = for_sibling(near_o_low, far_o_low)
    third_o_high = for_sibling(near_o_high, far_o_high)
    return step(
        [
            ("far", 1, 0, far_o_low),
            ("far", 1, cut, far_o_high),
            ("third", 1, 0, third_o_low),
            ("third", 1, cut, third_o_high),
        ],
        density,
        True,
    )


def pair_density(own_slice, partner, own_energy, partner_energy, row_energy, vir_energy, kappas):
    coulomb = lax.dot_general(
        own_slice, partner, (((0,), (0,)), ((), ())), preferred_element_type=jnp.float32
    )
    denominator = row_energy[:, None] + vir_energy[None, :] - own_energy - partner_energy
    damping = 1.0 - jnp.exp(-kappas[:, None, None] * denominator[None])
    amplitude = (-coulomb[None] * (damping * damping) / denominator[None]).astype(jnp.bfloat16)
    flat = amplitude.reshape(-1, amplitude.shape[2])
    density = lax.dot_general(
        flat, partner, (((1,), (1,)), ((), ())), preferred_element_type=jnp.float32
    )
    return density.reshape(kappas.shape[0], own_slice.shape[1], partner.shape[0])


def ring_terms(integrals, vir_coeff, occ_energy, vir_energy, kappas):
    aux_local, occ_count, basis = integrals.shape
    vir_local = vir_coeff.shape[1]
    batch_index = lax.axis_index("batch")
    wide_index = lax.axis_index("wide")
    flat_ints = integrals.reshape(aux_local * occ_count, basis)
    row_energy = lax.dynamic_slice_in_dim(vir_energy, batch_index * vir_local, vir_local, 0)
    own_energy = lax.dynamic_slice_in_dim(occ_energy, wide_index, 1, 0)[0]

    def term(partner, offset, own_slice):
        partner_index = (wide_index + offset) % occ_count
        partner_energy = lax.dynamic_slice_in_dim(occ_energy, partner_index, 1, 0)[0]
        return pair_density(
            own_slice, partner, own_energy, partner_energy, row_energy, vir_energy, kappas
        )

    transformed = jnp.dot(flat_ints, vir_coeff, preferred_element_type=jnp.float32).astype(
        jnp.bfloat16
    )
    transformed = transformed.reshape(aux_local, occ_count, vir_local)
    own_slice = lax.all_to_all(transformed, "wide", split_axis=1, concat_axis=0, tiled=True)[
        :, 0, :
    ]
    own_full = lax.all_gather(own_slice, "batch", axis=1, tiled=True)
    density = term(own_full, 0, own_slice)
    upper = own_full
    lower = own_full
    for offset in range(1, HALF + 1):
        upper = from_behind(upper, "wide", -1)
        lower = from_behind(lower, "wide", 1)
        density = density + term(upper, offset, own_slice) + term(lower, -offset, own_slice)
    return density.astype(jnp.bfloat16)[:, None, :, :]


def solution(mesh):
    paired = mesh.shape["batch"] == 2 and mesh.shape["wide"] % 4 == 0

    return jax.shard_map(
        pair_terms if paired else ring_terms,
        mesh=mesh,
        in_specs=(P("wide", None, None), P(None, "batch"), P(), P(), P()),
        out_specs=P(None, "wide", "batch", None),
        check_vma=False,
    )
```

```python
import functools

import jax
import jax.numpy as jnp
from jax import lax
from jax.experimental import pallas as pl
from jax.experimental.pallas import tpu as pltpu
from jax.sharding import PartitionSpec as P

HALF = 2
P_TILE = 512
KAPPA_GROUP = 2
VMEM_LIMIT = 18 * 1024 * 1024
LANES = 128


def from_behind(shard, axis, by):
    peers = lax.axis_size(axis)
    return lax.ppermute(shard, axis, [(i, (i + by) % peers) for i in range(peers)])


def swap_by(shard, axis, bit):
    peers = lax.axis_size(axis)
    return lax.ppermute(shard, axis, [(i, i ^ bit) for i in range(peers)])


def hand_along(shard, axis):
    peers = lax.axis_size(axis)
    return lax.ppermute(
        shard,
        axis,
        [(i, (i + (4 if i // 2 % 2 == 0 else -4)) % peers) for i in range(peers)],
    )


def prepare_kernel(
    place, kappas, occ_energy, vir_rows, own, low, high, own_t, row_energies, row_factors
):
    rows = own.shape[1]
    row_energy = vir_rows[pl.ds(place[1], 1), :] - occ_energy[place[0]]

    def down_columns(row):
        return jnp.transpose(jnp.broadcast_to(row, (LANES, rows)))

    low[...] = own[:, :rows // 2]
    high[...] = own[:, rows // 2:]
    own_t[...] = jnp.transpose(own[...])
    row_energies[...] = down_columns(row_energy)
    for q in range(row_factors.shape[0]):
        row_factors[q] = down_columns(jnp.exp(-kappas[q] * row_energy))


def prepare(scalars, vir_rows, own):
    naux, rows = own.shape
    nkap = scalars[1].shape[0]
    vmem = pl.BlockSpec(memory_space=pltpu.VMEM)
    smem = pl.BlockSpec(memory_space=pltpu.SMEM)
    return pl.pallas_call(
        prepare_kernel,
        out_shape=(
            jax.ShapeDtypeStruct((naux, rows // 2), own.dtype),
            jax.ShapeDtypeStruct((naux, rows // 2), own.dtype),
            jax.ShapeDtypeStruct((rows, naux), own.dtype),
            jax.ShapeDtypeStruct((rows, LANES), jnp.float32),
            jax.ShapeDtypeStruct((nkap, rows, LANES), jnp.float32),
        ),
        in_specs=[smem, smem, smem, vmem, vmem],
        out_specs=(vmem,) * 5,
        compiler_params=pltpu.CompilerParams(vmem_limit_bytes=VMEM_LIMIT),
        cost_estimate=pl.CostEstimate(flops=1, bytes_accessed=1, transcendentals=0),
    )(*scalars, vir_rows, own)


def terms_kernel(
    pieces,
    has_partial,
    final,
    place,
    kappas,
    occ_energy,
    vir_rows,
    own_t,
    row_energies,
    row_factors,
    *refs,
):
    partners = refs[:len(pieces)]
    refs = refs[len(pieces):]
    partial = None
    if has_partial:
        partial, refs = refs[0], refs[1:]
    if final:
        result, amp, ratio, out, sems = refs
    else:
        out, amp, ratio = refs
    nkap, rows = row_factors.shape[0], row_factors.shape[1]
    naux = own_t.shape[1]
    orbital, half, count = place[0], place[1], place[2]
    core_sign = 1 - 2 * lax.rem(orbital, 2)
    pair_sign = 1 - 2 * lax.rem(lax.div(orbital, 2), 2)
    offsets = dict(
        own=0, sibling=core_sign, third=-core_sign, near=HALF * pair_sign, far=-HALF * pair_sign
    )

    column_energies = []
    for (name, other, start), partner in zip(pieces, partners):
        index = lax.rem(orbital + offsets[name] + count, count)
        column_half = lax.rem(half + other, 2)
        energy = vir_rows[pl.ds(column_half, 1), :] - occ_energy[index]
        for c in range(start, start + partner.shape[1], LANES):
            column_energies.append(energy[:, c:c + LANES])
    width = LANES * len(column_energies)

    def partner_columns(tile):
        return jnp.concatenate([partner[tile, :] for partner in partners], axis=1)

    for at in range(0, width, 2 * LANES):
        columns = partner_columns(slice(None))[:, at:at + 2 * LANES]
        coulomb = jnp.dot(own_t[...], columns, preferred_element_type=jnp.float32)
        for c in range(0, columns.shape[1], LANES):
            energy = column_energies[(at + c) // LANES]
            ratio[:, at + c:at + c + LANES] = -coulomb[:, c:c + LANES] / (
                row_energies[...] + energy
            )

    copies = []
    for group in range(0, nkap, KAPPA_GROUP):
        top, bottom = group * rows, (group + KAPPA_GROUP) * rows
        for q in range(group, group + KAPPA_GROUP):
            for position, energy in enumerate(column_energies):
                columns = slice(position * LANES, (position + 1) * LANES)
                damping = 1.0 - row_factors[q] * jnp.exp(-kappas[q] * energy)
                amp[q * rows:(q + 1) * rows, columns] = (
                    ratio[:, columns] * damping * damping
                ).astype(amp.dtype)
        span = slice(group, group + KAPPA_GROUP)
        for start in range(0, naux, P_TILE):
            tile = slice(start, start + P_TILE)
            value = lax.dot_general(
                amp[top:bottom, :],
                partner_columns(tile),
                (((1,), (1,)), ((), ())),
                preferred_element_type=jnp.float32,
            ).reshape(KAPPA_GROUP, rows, P_TILE)
            if has_partial:
                value = value + partial[span, :, tile]
            out[span, :, tile] = value.astype(out.dtype)
        if final:
            copy = pltpu.make_async_copy(
                out.at[span], result.at[span, 0], sems.at[group // KAPPA_GROUP]
            )
            copy.start()
            copies.append(copy)
    for copy in copies:
        copy.wait()


def add_terms(scalars, vir_rows, prepared, partners, partial, final=False):
    rows, naux = prepared[0].shape
    nkap = prepared[2].shape[0]
    pieces = tuple(partner[:3] for partner in partners)
    arrays = [partner[3] for partner in partners]
    vmem = pl.BlockSpec(memory_space=pltpu.VMEM)
    smem = pl.BlockSpec(memory_space=pltpu.SMEM)
    operands = list(scalars) + [vir_rows] + list(prepared) + arrays
    if partial is not None:
        operands.append(partial)
    in_specs = [smem] * len(scalars) + [vmem] * (len(operands) - len(scalars))
    width = sum(array.shape[1] for array in arrays)
    scratch = [
        pltpu.VMEM((nkap * rows, width), jnp.bfloat16),
        pltpu.VMEM((rows, width), jnp.float32),
    ]
    if final:
        out_shape = jax.ShapeDtypeStruct((nkap, 1, rows, naux), jnp.bfloat16)
        out_spec = pl.BlockSpec(memory_space=pl.ANY)
        scratch.append(pltpu.VMEM((nkap, rows, naux), jnp.bfloat16))
        scratch.append(pltpu.SemaphoreType.DMA((nkap // KAPPA_GROUP,)))
    else:
        out_shape = jax.ShapeDtypeStruct((nkap, rows, naux), jnp.float32)
        out_spec = vmem
    return pl.pallas_call(
        functools.partial(terms_kernel, pieces, partial is not None, final),
        out_shape=out_shape,
        input_output_aliases={} if partial is None or final else {len(operands) - 1: 0},
        in_specs=in_specs,
        out_specs=out_spec,
        scratch_shapes=scratch,
        compiler_params=pltpu.CompilerParams(vmem_limit_bytes=VMEM_LIMIT),
        cost_estimate=pl.CostEstimate(flops=1, bytes_accessed=1, transcendentals=0),
    )(*operands)


def pair_terms(integrals, vir_coeff, occ_energy, vir_energy, kappas):
    aux_local, occ_count, basis = integrals.shape
    vir_local = vir_coeff.shape[1]
    wide_index = lax.axis_index("wide")
    batch_index = lax.axis_index("batch")
    place = jnp.stack(
        [wide_index, batch_index, jnp.full((), occ_count, wide_index.dtype)]
    ).astype(jnp.int32)
    vir_rows = vir_energy.reshape(-1, vir_local)
    flat_ints = integrals.reshape(aux_local * occ_count, basis)
    transformed = jnp.dot(flat_ints, vir_coeff, preferred_element_type=jnp.float32).astype(
        jnp.bfloat16
    )
    transformed = transformed.reshape(aux_local, occ_count, vir_local)

    def to_owner(columns):
        return lax.all_to_all(columns, "wide", split_axis=1, concat_axis=0, tiled=True)[:, 0, :]

    def over_batch(value):
        return from_behind(value, "batch", 1)

    def over_cores(value):
        return swap_by(value, "wide", 1)

    def over_pairs(value):
        return swap_by(value, "wide", 2)

    def along(value):
        return hand_along(value, "wide")

    together = lax.optimization_barrier
    sends_near = ((wide_index ^ (wide_index >> 1)) & 1) == 0
    own, sends_near, vir_rows, place = together(
        (to_owner(transformed), sends_near, vir_rows, place)
    )

    def for_sibling(near, far):
        return over_cores(jnp.where(sends_near, near, far))

    scalars = (place, kappas, occ_energy)
    cut = vir_local // 2
    sibling = over_cores(own)
    low, high, *prepared = prepare(scalars, vir_rows, own)
    step = functools.partial(add_terms, scalars, vir_rows, prepared)

    own_o_high = over_batch(high)
    near_low = over_pairs(low)
    density = step([("own", 0, 0, low), ("own", 0, cut, high), ("sibling", 0, 0, sibling)], None)

    low, high, own_o_high, near_low, density = together((low, high, own_o_high, near_low, density))
    own_o_low = over_batch(low)
    near_high = over_pairs(high)
    far_low = along(near_low)
    sibling_o_high = over_cores(own_o_high)
    density = step([("own", 1, cut, own_o_high), ("sibling", 1, cut, sibling_o_high)], density)

    own_o_low, own_o_high, near_low, near_high, far_low, density = together(
        (own_o_low, own_o_high, near_low, near_high, far_low, density)
    )
    near_o_low = over_batch(near_low)
    near_o_high = over_pairs(own_o_high)
    far_high = along(near_high)
    sibling_o_low = over_cores(own_o_low)
    third_low = for_sibling(near_low, far_low)
    density = step(
        [
            ("own", 1, 0, own_o_low),
            ("near", 0, 0, near_low),
            ("near", 0, cut, near_high),
            ("far", 0, 0, far_low),
            ("sibling", 1, 0, sibling_o_low),
            ("third", 0, 0, third_low),
        ],
        density,
    )

    near_high, near_o_low, near_o_high, far_low, far_high, density = together(
        (near_high, near_o_low, near_o_high, far_low, far_high, density)
    )
    far_o_low = over_batch(far_low)
    far_o_high = along(near_o_high)
    third_high = for_sibling(near_high, far_high)
    density = step(
        [
            ("near", 1, 0, near_o_low),
            ("near", 1, cut, near_o_high),
            ("far", 0, cut, far_high),
            ("third", 0, cut, third_high),
        ],
        density,
    )

    far_o_low, far_o_high, density = together((far_o_low, far_o_high, density))
    third_o_low = for_sibling(near_o_low, far_o_low)
    third_o_high = for_sibling(near_o_high, far_o_high)
    return step(
        [
            ("far", 1, 0, far_o_low),
            ("far", 1, cut, far_o_high),
            ("third", 1, 0, third_o_low),
            ("third", 1, cut, third_o_high),
        ],
        density,
        True,
    )


def pair_density(own_slice, partner, own_energy, partner_energy, row_energy, vir_energy, kappas):
    coulomb = lax.dot_general(
        own_slice, partner, (((0,), (0,)), ((), ())), preferred_element_type=jnp.float32
    )
    denominator = row_energy[:, None] + vir_energy[None, :] - own_energy - partner_energy
    damping = 1.0 - jnp.exp(-kappas[:, None, None] * denominator[None])
    amplitude = (-coulomb[None] * (damping * damping) / denominator[None]).astype(jnp.bfloat16)
    flat = amplitude.reshape(-1, amplitude.shape[2])
    density = lax.dot_general(
        flat, partner, (((1,), (1,)), ((), ())), preferred_element_type=jnp.float32
    )
    return density.reshape(kappas.shape[0], own_slice.shape[1], partner.shape[0])


def ring_terms(integrals, vir_coeff, occ_energy, vir_energy, kappas):
    aux_local, occ_count, basis = integrals.shape
    vir_local = vir_coeff.shape[1]
    batch_index = lax.axis_index("batch")
    wide_index = lax.axis_index("wide")
    flat_ints = integrals.reshape(aux_local * occ_count, basis)
    row_energy = lax.dynamic_slice_in_dim(vir_energy, batch_index * vir_local, vir_local, 0)
    own_energy = lax.dynamic_slice_in_dim(occ_energy, wide_index, 1, 0)[0]

    def term(partner, offset, own_slice):
        partner_index = (wide_index + offset) % occ_count
        partner_energy = lax.dynamic_slice_in_dim(occ_energy, partner_index, 1, 0)[0]
        return pair_density(
            own_slice, partner, own_energy, partner_energy, row_energy, vir_energy, kappas
        )

    transformed = jnp.dot(flat_ints, vir_coeff, preferred_element_type=jnp.float32).astype(
        jnp.bfloat16
    )
    transformed = transformed.reshape(aux_local, occ_count, vir_local)
    own_slice = lax.all_to_all(transformed, "wide", split_axis=1, concat_axis=0, tiled=True)[
        :, 0, :
    ]
    own_full = lax.all_gather(own_slice, "batch", axis=1, tiled=True)
    density = term(own_full, 0, own_slice)
    upper = own_full
    lower = own_full
    for offset in range(1, HALF + 1):
        upper = from_behind(upper, "wide", -1)
        lower = from_behind(lower, "wide", 1)
        density = density + term(upper, offset, own_slice) + term(lower, -offset, own_slice)
    return density.astype(jnp.bfloat16)[:, None, :, :]


def solution(mesh):
    paired = mesh.shape["batch"] == 2 and mesh.shape["wide"] % 4 == 0

    return jax.shard_map(
        pair_terms if paired else ring_terms,
        mesh=mesh,
        in_specs=(P("wide", None, None), P(None, "batch"), P(), P(), P()),
        out_specs=P(None, "wide", "batch", None),
        check_vma=False,
    )
```

```python
import functools

import jax
import jax.numpy as jnp
from jax import lax
from jax.experimental import pallas as pl
from jax.experimental.pallas import tpu as pltpu
from jax.sharding import PartitionSpec as P

HALF = 2
P_TILE = 512
KAPPA_GROUP = 2
TRANSFORM_STEPS = 3
VMEM_LIMIT = 18 * 1024 * 1024
LANES = 128


def from_behind(shard, axis, by):
    peers = lax.axis_size(axis)
    return lax.ppermute(shard, axis, [(i, (i + by) % peers) for i in range(peers)])


def swap_by(shard, axis, bit):
    peers = lax.axis_size(axis)
    return lax.ppermute(shard, axis, [(i, i ^ bit) for i in range(peers)])


def hand_along(shard, axis):
    peers = lax.axis_size(axis)
    return lax.ppermute(
        shard,
        axis,
        [(i, (i + (4 if i // 2 % 2 == 0 else -4)) % peers) for i in range(peers)],
    )


def transform_kernel(integrals, vir_coeff, low, high, held, product, sems):
    occ_count, aux_local, cut = low.shape
    rows = aux_local // TRANSFORM_STEPS

    def fetch(step):
        span = pl.ds(step * rows, rows)
        return pltpu.make_async_copy(integrals.at[span], held.at[span], sems.at[step])

    for step in range(TRANSFORM_STEPS):
        fetch(step).start()
    for step in range(TRANSFORM_STEPS):
        fetch(step).wait()
        span = slice(step * rows, (step + 1) * rows)
        value = jnp.dot(
            held[span].reshape(rows * occ_count, held.shape[2]),
            vir_coeff[...],
            preferred_element_type=jnp.float32,
        )
        for part, out in enumerate((low, high)):
            product[part, step] = value[:, part * cut:(part + 1) * cut]
            for orbital in range(occ_count):
                picked = product[part, step, pl.ds(orbital, rows, stride=occ_count), :]
                out[orbital, span, :] = picked.astype(out.dtype)


def transform(integrals, vir_coeff):
    aux_local, occ_count, basis = integrals.shape
    vir_local = vir_coeff.shape[1]
    vmem = pl.BlockSpec(memory_space=pltpu.VMEM)
    half = jax.ShapeDtypeStruct((occ_count, aux_local, vir_local // 2), integrals.dtype)
    rows = aux_local // TRANSFORM_STEPS
    return pl.pallas_call(
        transform_kernel,
        out_shape=(half, half),
        in_specs=[pl.BlockSpec(memory_space=pltpu.HBM), vmem],
        out_specs=(vmem, vmem),
        scratch_shapes=[
            pltpu.VMEM((aux_local, occ_count, basis), integrals.dtype),
            pltpu.VMEM((2, TRANSFORM_STEPS, rows * occ_count, vir_local // 2), jnp.float32),
            pltpu.SemaphoreType.DMA((TRANSFORM_STEPS,)),
        ],
        compiler_params=pltpu.CompilerParams(vmem_limit_bytes=VMEM_LIMIT),
        cost_estimate=pl.CostEstimate(flops=1, bytes_accessed=1, transcendentals=0),
    )(integrals, vir_coeff)


def prepare_kernel(
    place, kappas, occ_energy, vir_rows, own_low, own_high, own_t, row_energies, row_factors
):
    rows = own_t.shape[0]
    row_energy = vir_rows[pl.ds(place[1], 1), :] - occ_energy[place[0]]

    def down_columns(row):
        return jnp.transpose(jnp.broadcast_to(row, (LANES, rows)))

    own_t[:rows // 2, :] = jnp.transpose(own_low[...])
    own_t[rows // 2:, :] = jnp.transpose(own_high[...])
    row_energies[...] = down_columns(row_energy)
    for q in range(row_factors.shape[0]):
        row_factors[q] = down_columns(jnp.exp(-kappas[q] * row_energy))


def prepare(scalars, vir_rows, own_low, own_high):
    naux, rows = own_low.shape[0], 2 * own_low.shape[1]
    nkap = scalars[1].shape[0]
    vmem = pl.BlockSpec(memory_space=pltpu.VMEM)
    smem = pl.BlockSpec(memory_space=pltpu.SMEM)
    return pl.pallas_call(
        prepare_kernel,
        out_shape=(
            jax.ShapeDtypeStruct((rows, naux), own_low.dtype),
            jax.ShapeDtypeStruct((rows, LANES), jnp.float32),
            jax.ShapeDtypeStruct((nkap, rows, LANES), jnp.float32),
        ),
        in_specs=[smem, smem, smem, vmem, vmem, vmem],
        out_specs=(vmem,) * 3,
        compiler_params=pltpu.CompilerParams(vmem_limit_bytes=VMEM_LIMIT),
        cost_estimate=pl.CostEstimate(flops=1, bytes_accessed=1, transcendentals=0),
    )(*scalars, vir_rows, own_low, own_high)


def terms_kernel(
    pieces,
    has_partial,
    final,
    place,
    kappas,
    occ_energy,
    vir_rows,
    own_t,
    row_energies,
    row_factors,
    *refs,
):
    partners = refs[:len(pieces)]
    refs = refs[len(pieces):]
    partial = None
    if has_partial:
        partial, refs = refs[0], refs[1:]
    if final:
        result, amp, ratio, out, sems = refs
    else:
        out, amp, ratio = refs
    nkap, rows = row_factors.shape[0], row_factors.shape[1]
    naux = own_t.shape[1]
    orbital, half, count = place[0], place[1], place[2]
    core_sign = 1 - 2 * lax.rem(orbital, 2)
    pair_sign = 1 - 2 * lax.rem(lax.div(orbital, 2), 2)
    offsets = dict(
        own=0, sibling=core_sign, third=-core_sign, near=HALF * pair_sign, far=-HALF * pair_sign
    )

    column_energies = []
    for (name, other, start), partner in zip(pieces, partners):
        index = lax.rem(orbital + offsets[name] + count, count)
        column_half = lax.rem(half + other, 2)
        energy = vir_rows[pl.ds(column_half, 1), :] - occ_energy[index]
        for c in range(start, start + partner.shape[1], LANES):
            column_energies.append(energy[:, c:c + LANES])
    width = LANES * len(column_energies)

    def partner_columns(tile):
        return jnp.concatenate([partner[tile, :] for partner in partners], axis=1)

    for at in range(0, width, 2 * LANES):
        columns = partner_columns(slice(None))[:, at:at + 2 * LANES]
        coulomb = jnp.dot(own_t[...], columns, preferred_element_type=jnp.float32)
        for c in range(0, columns.shape[1], LANES):
            energy = column_energies[(at + c) // LANES]
            ratio[:, at + c:at + c + LANES] = -coulomb[:, c:c + LANES] / (
                row_energies[...] + energy
            )

    copies = []
    for group in range(0, nkap, KAPPA_GROUP):
        top, bottom = group * rows, (group + KAPPA_GROUP) * rows
        for q in range(group, group + KAPPA_GROUP):
            for position, energy in enumerate(column_energies):
                columns = slice(position * LANES, (position + 1) * LANES)
                damping = 1.0 - row_factors[q] * jnp.exp(-kappas[q] * energy)
                amp[q * rows:(q + 1) * rows, columns] = (
                    ratio[:, columns] * damping * damping
                ).astype(amp.dtype)
        span = slice(group, group + KAPPA_GROUP)
        for start in range(0, naux, P_TILE):
            tile = slice(start, start + P_TILE)
            value = lax.dot_general(
                amp[top:bottom, :],
                partner_columns(tile),
                (((1,), (1,)), ((), ())),
                preferred_element_type=jnp.float32,
            ).reshape(KAPPA_GROUP, rows, P_TILE)
            if has_partial:
                value = value + partial[span, :, tile]
            out[span, :, tile] = value.astype(out.dtype)
        if final:
            copy = pltpu.make_async_copy(
                out.at[span], result.at[span, 0], sems.at[group // KAPPA_GROUP]
            )
            copy.start()
            copies.append(copy)
    for copy in copies:
        copy.wait()


def add_terms(scalars, vir_rows, prepared, partners, partial, final=False):
    rows, naux = prepared[0].shape
    nkap = prepared[2].shape[0]
    pieces = tuple(partner[:3] for partner in partners)
    arrays = [partner[3] for partner in partners]
    vmem = pl.BlockSpec(memory_space=pltpu.VMEM)
    smem = pl.BlockSpec(memory_space=pltpu.SMEM)
    operands = list(scalars) + [vir_rows] + list(prepared) + arrays
    if partial is not None:
        operands.append(partial)
    in_specs = [smem] * len(scalars) + [vmem] * (len(operands) - len(scalars))
    width = sum(array.shape[1] for array in arrays)
    scratch = [
        pltpu.VMEM((nkap * rows, width), jnp.bfloat16),
        pltpu.VMEM((rows, width), jnp.float32),
    ]
    if final:
        out_shape = jax.ShapeDtypeStruct((nkap, 1, rows, naux), jnp.bfloat16)
        out_spec = pl.BlockSpec(memory_space=pl.ANY)
        scratch.append(pltpu.VMEM((nkap, rows, naux), jnp.bfloat16))
        scratch.append(pltpu.SemaphoreType.DMA((nkap // KAPPA_GROUP,)))
    else:
        out_shape = jax.ShapeDtypeStruct((nkap, rows, naux), jnp.float32)
        out_spec = vmem
    return pl.pallas_call(
        functools.partial(terms_kernel, pieces, partial is not None, final),
        out_shape=out_shape,
        input_output_aliases={} if partial is None or final else {len(operands) - 1: 0},
        in_specs=in_specs,
        out_specs=out_spec,
        scratch_shapes=scratch,
        compiler_params=pltpu.CompilerParams(vmem_limit_bytes=VMEM_LIMIT),
        cost_estimate=pl.CostEstimate(flops=1, bytes_accessed=1, transcendentals=0),
    )(*operands)


def pair_terms(integrals, vir_coeff, occ_energy, vir_energy, kappas):
    occ_count = integrals.shape[1]
    vir_local = vir_coeff.shape[1]
    wide_index = lax.axis_index("wide")
    batch_index = lax.axis_index("batch")
    place = jnp.stack(
        [wide_index, batch_index, jnp.full((), occ_count, wide_index.dtype)]
    ).astype(jnp.int32)
    vir_rows = vir_energy.reshape(-1, vir_local)
    def to_owner(columns):
        owned = lax.all_to_all(columns, "wide", split_axis=0, concat_axis=0, tiled=True)
        return owned.reshape(-1, owned.shape[2])

    def over_batch(value):
        return from_behind(value, "batch", 1)

    def over_cores(value):
        return swap_by(value, "wide", 1)

    def over_pairs(value):
        return swap_by(value, "wide", 2)

    def along(value):
        return hand_along(value, "wide")

    together = lax.optimization_barrier
    sends_near = ((wide_index ^ (wide_index >> 1)) & 1) == 0
    low, high = transform(integrals, vir_coeff)
    sends_near, vir_rows, place, low = together((sends_near, vir_rows, place, low))

    def for_sibling(near, far):
        return over_cores(jnp.where(sends_near, near, far))

    scalars = (place, kappas, occ_energy)
    cut = vir_local // 2
    low, high = together((to_owner(low), high))
    own_o_low = over_batch(low)
    near_low = over_pairs(low)
    sibling_low = over_cores(low)
    high = to_owner(high)

    own_o_low, near_low, sibling_low, high = together((own_o_low, near_low, sibling_low, high))
    own_o_high = over_batch(high)
    near_high = over_pairs(high)
    far_low = along(near_low)
    sibling_high = over_cores(high)
    sibling_o_low = over_cores(own_o_low)
    step = functools.partial(
        add_terms, scalars, vir_rows, prepare(scalars, vir_rows, low, high)
    )
    density = step(
        [
            ("own", 0, 0, low),
            ("own", 0, cut, high),
            ("sibling", 0, 0, sibling_low),
            ("sibling", 0, cut, sibling_high),
        ],
        None,
    )
    density = step([("own", 1, 0, own_o_low), ("near", 0, 0, near_low)], density)
    own_o_low, own_o_high, near_high, far_low, sibling_o_low, density = together(
        (own_o_low, own_o_high, near_high, far_low, sibling_o_low, density)
    )
    far_o_low = over_batch(far_low)
    near_o_low = over_pairs(own_o_low)
    far_high = along(near_high)
    sibling_o_high = over_cores(own_o_high)
    third_low = for_sibling(near_low, far_low)
    density = step(
        [
            ("own", 1, cut, own_o_high),
            ("near", 0, cut, near_high),
            ("far", 0, 0, far_low),
            ("sibling", 1, 0, sibling_o_low),
        ],
        density,
    )
    far_o_low, near_o_low, far_high, sibling_o_high, third_low, density = together(
        (far_o_low, near_o_low, far_high, sibling_o_high, third_low, density)
    )
    far_o_high = over_batch(far_high)
    near_o_high = over_pairs(own_o_high)
    third_high = for_sibling(near_high, far_high)
    third_o_low = for_sibling(near_o_low, far_o_low)
    density = step(
        [
            ("near", 1, 0, near_o_low),
            ("far", 1, 0, far_o_low),
            ("far", 0, cut, far_high),
            ("sibling", 1, cut, sibling_o_high),
            ("third", 0, 0, third_low),
            ("third", 0, cut, third_high),
        ],
        density,
    )
    far_o_high, near_o_high, third_o_low, density = together(
        (far_o_high, near_o_high, third_o_low, density)
    )
    third_o_high = for_sibling(near_o_high, far_o_high)
    return step(
        [
            ("near", 1, cut, near_o_high),
            ("far", 1, cut, far_o_high),
            ("third", 1, 0, third_o_low),
            ("third", 1, cut, third_o_high),
        ],
        density,
        True,
    )


def pair_density(own_slice, partner, own_energy, partner_energy, row_energy, vir_energy, kappas):
    coulomb = lax.dot_general(
        own_slice, partner, (((0,), (0,)), ((), ())), preferred_element_type=jnp.float32
    )
    denominator = row_energy[:, None] + vir_energy[None, :] - own_energy - partner_energy
    damping = 1.0 - jnp.exp(-kappas[:, None, None] * denominator[None])
    amplitude = (-coulomb[None] * (damping * damping) / denominator[None]).astype(jnp.bfloat16)
    flat = amplitude.reshape(-1, amplitude.shape[2])
    density = lax.dot_general(
        flat, partner, (((1,), (1,)), ((), ())), preferred_element_type=jnp.float32
    )
    return density.reshape(kappas.shape[0], own_slice.shape[1], partner.shape[0])


def ring_terms(integrals, vir_coeff, occ_energy, vir_energy, kappas):
    aux_local, occ_count, basis = integrals.shape
    vir_local = vir_coeff.shape[1]
    batch_index = lax.axis_index("batch")
    wide_index = lax.axis_index("wide")
    flat_ints = integrals.reshape(aux_local * occ_count, basis)
    row_energy = lax.dynamic_slice_in_dim(vir_energy, batch_index * vir_local, vir_local, 0)
    own_energy = lax.dynamic_slice_in_dim(occ_energy, wide_index, 1, 0)[0]

    def term(partner, offset, own_slice):
        partner_index = (wide_index + offset) % occ_count
        partner_energy = lax.dynamic_slice_in_dim(occ_energy, partner_index, 1, 0)[0]
        return pair_density(
            own_slice, partner, own_energy, partner_energy, row_energy, vir_energy, kappas
        )

    transformed = jnp.dot(flat_ints, vir_coeff, preferred_element_type=jnp.float32).astype(
        jnp.bfloat16
    )
    transformed = transformed.reshape(aux_local, occ_count, vir_local)
    own_slice = lax.all_to_all(transformed, "wide", split_axis=1, concat_axis=0, tiled=True)[
        :, 0, :
    ]
    own_full = lax.all_gather(own_slice, "batch", axis=1, tiled=True)
    density = term(own_full, 0, own_slice)
    upper = own_full
    lower = own_full
    for offset in range(1, HALF + 1):
        upper = from_behind(upper, "wide", -1)
        lower = from_behind(lower, "wide", 1)
        density = density + term(upper, offset, own_slice) + term(lower, -offset, own_slice)
    return density.astype(jnp.bfloat16)[:, None, :, :]


def solution(mesh):
    paired = mesh.shape["batch"] == 2 and mesh.shape["wide"] % 4 == 0

    return jax.shard_map(
        pair_terms if paired else ring_terms,
        mesh=mesh,
        in_specs=(P("wide", None, None), P(None, "batch"), P(), P(), P()),
        out_specs=P(None, "wide", "batch", None),
        check_vma=False,
    )
```

```python
import functools

import jax
import jax.numpy as jnp
from jax import lax
from jax.experimental import pallas as pl
from jax.experimental.pallas import tpu as pltpu
from jax.sharding import PartitionSpec as P

HALF = 2
P_TILE = 512
KAPPA_GROUP = 2
VMEM_LIMIT = 18 * 1024 * 1024
LANES = 128


def from_behind(shard, axis, by):
    peers = lax.axis_size(axis)
    return lax.ppermute(shard, axis, [(i, (i + by) % peers) for i in range(peers)])


def swap_by(shard, axis, bit):
    peers = lax.axis_size(axis)
    return lax.ppermute(shard, axis, [(i, i ^ bit) for i in range(peers)])


def hand_along(shard, axis):
    peers = lax.axis_size(axis)
    return lax.ppermute(
        shard,
        axis,
        [(i, (i + (4 if i // 2 % 2 == 0 else -4)) % peers) for i in range(peers)],
    )


def prepare_kernel(
    place, kappas, occ_energy, vir_rows, own, low, high, own_t, row_energies, row_factors
):
    rows = own.shape[1]
    row_energy = vir_rows[pl.ds(place[1], 1), :] - occ_energy[place[0]]

    def down_columns(row):
        return jnp.transpose(jnp.broadcast_to(row, (LANES, rows)))

    low[...] = own[:, :rows // 2]
    high[...] = own[:, rows // 2:]
    own_t[...] = jnp.transpose(own[...])
    row_energies[...] = down_columns(row_energy)
    for q in range(row_factors.shape[0]):
        row_factors[q] = down_columns(jnp.exp(-kappas[q] * row_energy))


def prepare(scalars, vir_rows, own):
    naux, rows = own.shape
    nkap = scalars[1].shape[0]
    vmem = pl.BlockSpec(memory_space=pltpu.VMEM)
    smem = pl.BlockSpec(memory_space=pltpu.SMEM)
    return pl.pallas_call(
        prepare_kernel,
        out_shape=(
            jax.ShapeDtypeStruct((naux, rows // 2), own.dtype),
            jax.ShapeDtypeStruct((naux, rows // 2), own.dtype),
            jax.ShapeDtypeStruct((rows, naux), own.dtype),
            jax.ShapeDtypeStruct((rows, LANES), jnp.float32),
            jax.ShapeDtypeStruct((nkap, rows, LANES), jnp.float32),
        ),
        in_specs=[smem, smem, smem, vmem, vmem],
        out_specs=(vmem,) * 5,
        compiler_params=pltpu.CompilerParams(vmem_limit_bytes=VMEM_LIMIT),
        cost_estimate=pl.CostEstimate(flops=1, bytes_accessed=1, transcendentals=0),
    )(*scalars, vir_rows, own)


def terms_kernel(
    pieces,
    has_partial,
    final,
    place,
    kappas,
    occ_energy,
    vir_rows,
    own_t,
    row_energies,
    row_factors,
    *refs,
):
    partners = refs[:len(pieces)]
    refs = refs[len(pieces):]
    partial = None
    if has_partial:
        partial, refs = refs[0], refs[1:]
    if final:
        result, amp, ratio, out, sems = refs
    else:
        out, amp, ratio = refs
    nkap, rows = row_factors.shape[0], row_factors.shape[1]
    naux = own_t.shape[1]
    orbital, half, count = place[0], place[1], place[2]
    core_sign = 1 - 2 * lax.rem(orbital, 2)
    pair_sign = 1 - 2 * lax.rem(lax.div(orbital, 2), 2)
    offsets = dict(
        own=0, sibling=core_sign, third=-core_sign, near=HALF * pair_sign, far=-HALF * pair_sign
    )

    column_energies = []
    for (name, other, start), partner in zip(pieces, partners):
        index = lax.rem(orbital + offsets[name] + count, count)
        column_half = lax.rem(half + other, 2)
        energy = vir_rows[pl.ds(column_half, 1), :] - occ_energy[index]
        for c in range(start, start + partner.shape[1], LANES):
            column_energies.append(energy[:, c:c + LANES])
    width = LANES * len(column_energies)

    def partner_columns(tile):
        return jnp.concatenate([partner[tile, :] for partner in partners], axis=1)

    for at in range(0, width, 2 * LANES):
        columns = partner_columns(slice(None))[:, at:at + 2 * LANES]
        coulomb = jnp.dot(own_t[...], columns, preferred_element_type=jnp.float32)
        for c in range(0, columns.shape[1], LANES):
            energy = column_energies[(at + c) // LANES]
            ratio[:, at + c:at + c + LANES] = -coulomb[:, c:c + LANES] / (
                row_energies[...] + energy
            )

    copies = []
    for group in range(0, nkap, KAPPA_GROUP):
        top, bottom = group * rows, (group + KAPPA_GROUP) * rows
        for q in range(group, group + KAPPA_GROUP):
            for position, energy in enumerate(column_energies):
                columns = slice(position * LANES, (position + 1) * LANES)
                damping = 1.0 - row_factors[q] * jnp.exp(-kappas[q] * energy)
                amp[q * rows:(q + 1) * rows, columns] = (
                    ratio[:, columns] * damping * damping
                ).astype(amp.dtype)
        span = slice(group, group + KAPPA_GROUP)
        for start in range(0, naux, P_TILE):
            tile = slice(start, start + P_TILE)
            value = lax.dot_general(
                amp[top:bottom, :],
                partner_columns(tile),
                (((1,), (1,)), ((), ())),
                preferred_element_type=jnp.float32,
            ).reshape(KAPPA_GROUP, rows, P_TILE)
            if has_partial:
                value = value + partial[span, :, tile]
            out[span, :, tile] = value.astype(out.dtype)
        if final:
            copy = pltpu.make_async_copy(
                out.at[span], result.at[span, 0], sems.at[group // KAPPA_GROUP]
            )
            copy.start()
            copies.append(copy)
    for copy in copies:
        copy.wait()


def add_terms(scalars, vir_rows, prepared, partners, partial, final=False):
    rows, naux = prepared[0].shape
    nkap = prepared[2].shape[0]
    pieces = tuple(partner[:3] for partner in partners)
    arrays = [partner[3] for partner in partners]
    vmem = pl.BlockSpec(memory_space=pltpu.VMEM)
    smem = pl.BlockSpec(memory_space=pltpu.SMEM)
    operands = list(scalars) + [vir_rows] + list(prepared) + arrays
    if partial is not None:
        operands.append(partial)
    in_specs = [smem] * len(scalars) + [vmem] * (len(operands) - len(scalars))
    width = sum(array.shape[1] for array in arrays)
    scratch = [
        pltpu.VMEM((nkap * rows, width), jnp.bfloat16),
        pltpu.VMEM((rows, width), jnp.float32),
    ]
    if final:
        out_shape = jax.ShapeDtypeStruct((nkap, 1, rows, naux), jnp.bfloat16)
        out_spec = pl.BlockSpec(memory_space=pl.ANY)
        scratch.append(pltpu.VMEM((nkap, rows, naux), jnp.bfloat16))
        scratch.append(pltpu.SemaphoreType.DMA((nkap // KAPPA_GROUP,)))
    else:
        out_shape = jax.ShapeDtypeStruct((nkap, rows, naux), jnp.float32)
        out_spec = vmem
    return pl.pallas_call(
        functools.partial(terms_kernel, pieces, partial is not None, final),
        out_shape=out_shape,
        input_output_aliases={} if partial is None or final else {len(operands) - 1: 0},
        in_specs=in_specs,
        out_specs=out_spec,
        scratch_shapes=scratch,
        compiler_params=pltpu.CompilerParams(vmem_limit_bytes=VMEM_LIMIT),
        cost_estimate=pl.CostEstimate(flops=1, bytes_accessed=1, transcendentals=0),
    )(*operands)


def pair_terms(integrals, vir_coeff, occ_energy, vir_energy, kappas):
    aux_local, occ_count, basis = integrals.shape
    vir_local = vir_coeff.shape[1]
    wide_index = lax.axis_index("wide")
    batch_index = lax.axis_index("batch")
    place = jnp.stack(
        [wide_index, batch_index, jnp.full((), occ_count, wide_index.dtype)]
    ).astype(jnp.int32)
    vir_rows = vir_energy.reshape(-1, vir_local)
    flat_ints = integrals.reshape(aux_local * occ_count, basis)
    transformed = jnp.dot(flat_ints, vir_coeff, preferred_element_type=jnp.float32).astype(
        jnp.bfloat16
    )
    transformed = transformed.reshape(aux_local, occ_count, vir_local)

    def to_owner(columns):
        return lax.all_to_all(columns, "wide", split_axis=1, concat_axis=0, tiled=True)[:, 0, :]

    def over_batch(value):
        return from_behind(value, "batch", 1)

    def over_cores(value):
        return swap_by(value, "wide", 1)

    def over_pairs(value):
        return swap_by(value, "wide", 2)

    def along(value):
        return hand_along(value, "wide")

    together = lax.optimization_barrier
    sends_near = ((wide_index ^ (wide_index >> 1)) & 1) == 0
    own, sends_near, vir_rows, place = together(
        (to_owner(transformed), sends_near, vir_rows, place)
    )

    def for_sibling(near, far):
        return over_cores(jnp.where(sends_near, near, far))

    scalars = (place, kappas, occ_energy)
    cut = vir_local // 2
    sibling = over_cores(own)
    low, high, *prepared = prepare(scalars, vir_rows, own)
    step = functools.partial(add_terms, scalars, vir_rows, prepared)

    own_o_high = over_batch(high)
    near_low = over_pairs(low)
    density = step([("own", 0, 0, low), ("own", 0, cut, high)], None)

    low, high, density = together((low, high, density))
    own_o_low = over_batch(low)
    near_high = over_pairs(high)
    density = step([("sibling", 0, 0, sibling)], density)

    near_low, own_o_high, density = together((near_low, own_o_high, density))
    far_low = along(near_low)
    near_o_high = over_pairs(own_o_high)
    near_o_low = over_batch(near_low)
    sibling_o_high = over_cores(own_o_high)
    density = step([("own", 1, cut, own_o_high), ("near", 0, 0, near_low)], density)

    own_o_low, near_high, density = together((own_o_low, near_high, density))
    far_high = along(near_high)
    sibling_o_low = over_cores(own_o_low)
    density = step([("own", 1, 0, own_o_low), ("near", 0, cut, near_high)], density)

    far_low, near_o_high, near_o_low, density = together(
        (far_low, near_o_high, near_o_low, density)
    )
    far_o_low = over_batch(far_low)
    far_o_high = along(near_o_high)
    third_low = for_sibling(near_low, far_low)
    density = step(
        [
            ("sibling", 1, 0, sibling_o_low),
            ("sibling", 1, cut, sibling_o_high),
            ("far", 0, 0, far_low),
            ("near", 1, cut, near_o_high),
        ],
        density,
    )

    far_high, density = together((far_high, density))
    third_high = for_sibling(near_high, far_high)
    density = step(
        [
            ("near", 1, 0, near_o_low),
            ("far", 0, cut, far_high),
            ("third", 0, 0, third_low),
            ("third", 0, cut, third_high),
        ],
        density,
    )

    far_o_low, far_o_high, density = together((far_o_low, far_o_high, density))
    third_o_low = for_sibling(near_o_low, far_o_low)
    third_o_high = for_sibling(near_o_high, far_o_high)
    return step(
        [
            ("far", 1, 0, far_o_low),
            ("far", 1, cut, far_o_high),
            ("third", 1, 0, third_o_low),
            ("third", 1, cut, third_o_high),
        ],
        density,
        True,
    )


def pair_density(own_slice, partner, own_energy, partner_energy, row_energy, vir_energy, kappas):
    coulomb = lax.dot_general(
        own_slice, partner, (((0,), (0,)), ((), ())), preferred_element_type=jnp.float32
    )
    denominator = row_energy[:, None] + vir_energy[None, :] - own_energy - partner_energy
    damping = 1.0 - jnp.exp(-kappas[:, None, None] * denominator[None])
    amplitude = (-coulomb[None] * (damping * damping) / denominator[None]).astype(jnp.bfloat16)
    flat = amplitude.reshape(-1, amplitude.shape[2])
    density = lax.dot_general(
        flat, partner, (((1,), (1,)), ((), ())), preferred_element_type=jnp.float32
    )
    return density.reshape(kappas.shape[0], own_slice.shape[1], partner.shape[0])


def ring_terms(integrals, vir_coeff, occ_energy, vir_energy, kappas):
    aux_local, occ_count, basis = integrals.shape
    vir_local = vir_coeff.shape[1]
    batch_index = lax.axis_index("batch")
    wide_index = lax.axis_index("wide")
    flat_ints = integrals.reshape(aux_local * occ_count, basis)
    row_energy = lax.dynamic_slice_in_dim(vir_energy, batch_index * vir_local, vir_local, 0)
    own_energy = lax.dynamic_slice_in_dim(occ_energy, wide_index, 1, 0)[0]

    def term(partner, offset, own_slice):
        partner_index = (wide_index + offset) % occ_count
        partner_energy = lax.dynamic_slice_in_dim(occ_energy, partner_index, 1, 0)[0]
        return pair_density(
            own_slice, partner, own_energy, partner_energy, row_energy, vir_energy, kappas
        )

    transformed = jnp.dot(flat_ints, vir_coeff, preferred_element_type=jnp.float32).astype(
        jnp.bfloat16
    )
    transformed = transformed.reshape(aux_local, occ_count, vir_local)
    own_slice = lax.all_to_all(transformed, "wide", split_axis=1, concat_axis=0, tiled=True)[
        :, 0, :
    ]
    own_full = lax.all_gather(own_slice, "batch", axis=1, tiled=True)
    density = term(own_full, 0, own_slice)
    upper = own_full
    lower = own_full
    for offset in range(1, HALF + 1):
        upper = from_behind(upper, "wide", -1)
        lower = from_behind(lower, "wide", 1)
        density = density + term(upper, offset, own_slice) + term(lower, -offset, own_slice)
    return density.astype(jnp.bfloat16)[:, None, :, :]


def solution(mesh):
    paired = mesh.shape["batch"] == 2 and mesh.shape["wide"] % 4 == 0

    return jax.shard_map(
        pair_terms if paired else ring_terms,
        mesh=mesh,
        in_specs=(P("wide", None, None), P(None, "batch"), P(), P(), P()),
        out_specs=P(None, "wide", "batch", None),
        check_vma=False,
    )
```

```python
import functools

import jax
import jax.numpy as jnp
from jax import lax
from jax.experimental import pallas as pl
from jax.experimental.pallas import tpu as pltpu
from jax.sharding import PartitionSpec as P

HALF = 2
VMEM_LIMIT = 18 * 1024 * 1024
LANES = 128


def from_behind(shard, axis, by):
    peers = lax.axis_size(axis)
    return lax.ppermute(shard, axis, [(i, (i + by) % peers) for i in range(peers)])


def swap_by(shard, axis, bit):
    peers = lax.axis_size(axis)
    return lax.ppermute(shard, axis, [(i, i ^ bit) for i in range(peers)])


def hand_along(shard, axis):
    peers = lax.axis_size(axis)
    return lax.ppermute(
        shard,
        axis,
        [(i, (i + (4 if i // 2 % 2 == 0 else -4)) % peers) for i in range(peers)],
    )


def cut_kernel(own, low, high):
    cut = low.shape[1]
    low[...] = own[:, :cut]
    high[...] = own[:, cut:]


def cut_in_two(own):
    vmem = pl.BlockSpec(memory_space=pltpu.VMEM)
    half = jax.ShapeDtypeStruct((own.shape[0], own.shape[1] // 2), own.dtype)
    return pl.pallas_call(
        cut_kernel,
        out_shape=(half, half),
        in_specs=[vmem],
        out_specs=(vmem, vmem),
        compiler_params=pltpu.CompilerParams(vmem_limit_bytes=VMEM_LIMIT),
        cost_estimate=pl.CostEstimate(flops=1, bytes_accessed=1, transcendentals=0),
    )(own)


def make_factors(place, kappa, occ, vir_rows, own_low, own_high, own_t, row_energies, row_factors):
    rows = own_t.shape[0]
    row_energy = vir_rows[pl.ds(place[1], 1), :] - occ(place[0])

    def down_columns(row):
        return jnp.transpose(jnp.broadcast_to(row, (LANES, rows)))

    own_t[:rows // 2, :] = jnp.transpose(own_low[...])
    own_t[rows // 2:, :] = jnp.transpose(own_high[...])
    row_energies[...] = down_columns(row_energy)
    for q in range(row_factors.shape[0]):
        row_factors[q] = down_columns(jnp.exp(-kappa(q) * row_energy))


def terms_kernel(pieces, mode, shape, place, energies, vir_rows, *refs):
    if mode == "first":
        partners = refs[:len(pieces)]
        own_t, row_energies, row_factors, out, amp, ratio = refs[len(pieces):]
    else:
        own_t, row_energies, row_factors = refs[:3]
        partners = refs[3:3 + len(pieces)]
        partial, *refs = refs[3 + len(pieces):]
        if mode == "last":
            result, amp, ratio, out, sems = refs
        else:
            out, amp, ratio = refs
    group_size, p_tile = shape
    nkap, rows = row_factors.shape[0], row_factors.shape[1]
    naux = own_t.shape[1]
    orbital, half, count = place[0], place[1], place[2]

    def kappa(q):
        return energies[q]

    def occ(index):
        return energies[nkap + index]

    if mode == "first":
        make_factors(
            place, kappa, occ, vir_rows, partners[0], partners[1], own_t, row_energies, row_factors
        )
    core_sign = 1 - 2 * lax.rem(orbital, 2)
    pair_sign = 1 - 2 * lax.rem(lax.div(orbital, 2), 2)
    offsets = dict(
        own=0, sibling=core_sign, third=-core_sign, near=HALF * pair_sign, far=-HALF * pair_sign
    )

    column_energies = []
    for (name, other, start), partner in zip(pieces, partners):
        index = lax.rem(orbital + offsets[name] + count, count)
        column_half = lax.rem(half + other, 2)
        energy = vir_rows[pl.ds(column_half, 1), :] - occ(index)
        for c in range(start, start + partner.shape[1], LANES):
            column_energies.append(energy[:, c:c + LANES])
    width = LANES * len(column_energies)

    def partner_columns(tile):
        return jnp.concatenate([partner[tile, :] for partner in partners], axis=1)

    for at in range(0, width, 2 * LANES):
        columns = partner_columns(slice(None))[:, at:at + 2 * LANES]
        coulomb = jnp.dot(own_t[...], columns, preferred_element_type=jnp.float32)
        for c in range(0, columns.shape[1], LANES):
            energy = column_energies[(at + c) // LANES]
            ratio[:, at + c:at + c + LANES] = -coulomb[:, c:c + LANES] / (
                row_energies[...] + energy
            )

    copies = []
    for group in range(0, nkap, group_size):
        top, bottom = group * rows, (group + group_size) * rows
        for q in range(group, group + group_size):
            for position, energy in enumerate(column_energies):
                columns = slice(position * LANES, (position + 1) * LANES)
                damping = 1.0 - row_factors[q] * jnp.exp(-kappa(q) * energy)
                amp[q * rows:(q + 1) * rows, columns] = (
                    ratio[:, columns] * damping * damping
                ).astype(amp.dtype)
        span = slice(group, group + group_size)
        for start in range(0, naux, p_tile):
            tile = slice(start, start + p_tile)
            value = lax.dot_general(
                amp[top:bottom, :],
                partner_columns(tile),
                (((1,), (1,)), ((), ())),
                preferred_element_type=jnp.float32,
            ).reshape(group_size, rows, p_tile)
            if mode != "first":
                value = value + partial[span, :, tile]
            out[span, :, tile] = value.astype(out.dtype)
        if mode == "last":
            copy = pltpu.make_async_copy(
                out.at[span], result.at[span, 0], sems.at[group // group_size]
            )
            copy.start()
            copies.append(copy)
    for copy in copies:
        copy.wait()


def add_terms(place, energies, vir_rows, nkap, made, partners, partial, shape, last=False):
    pieces = tuple(partner[:3] for partner in partners)
    arrays = [partner[3] for partner in partners]
    naux = arrays[0].shape[0]
    rows = vir_rows.shape[1]
    width = sum(array.shape[1] for array in arrays)
    vmem = pl.BlockSpec(memory_space=pltpu.VMEM)
    smem = pl.BlockSpec(memory_space=pltpu.SMEM)
    density = jax.ShapeDtypeStruct((nkap, rows, naux), jnp.float32)
    scratch = [
        pltpu.VMEM((nkap * rows, width), jnp.bfloat16),
        pltpu.VMEM((rows, width), jnp.float32),
    ]
    aliases = {}
    if made is None:
        mode = "first"
        operands = [place, energies, vir_rows] + arrays
        out_shape = (
            jax.ShapeDtypeStruct((rows, naux), arrays[0].dtype),
            jax.ShapeDtypeStruct((rows, LANES), jnp.float32),
            jax.ShapeDtypeStruct((nkap, rows, LANES), jnp.float32),
            density,
        )
        out_specs = (vmem,) * 4
    else:
        mode = "last" if last else "middle"
        operands = [place, energies, vir_rows] + list(made) + arrays + [partial]
        if last:
            out_shape = jax.ShapeDtypeStruct((nkap, 1, rows, naux), jnp.bfloat16)
            out_specs = pl.BlockSpec(memory_space=pl.ANY)
            scratch.append(pltpu.VMEM((nkap, rows, naux), jnp.bfloat16))
            scratch.append(pltpu.SemaphoreType.DMA((nkap // shape[0],)))
        else:
            out_shape, out_specs = density, vmem
            aliases = {len(operands) - 1: 0}
    return pl.pallas_call(
        functools.partial(terms_kernel, pieces, mode, shape),
        out_shape=out_shape,
        input_output_aliases=aliases,
        in_specs=[smem, smem] + [vmem] * (len(operands) - 2),
        out_specs=out_specs,
        scratch_shapes=scratch,
        compiler_params=pltpu.CompilerParams(vmem_limit_bytes=VMEM_LIMIT),
        cost_estimate=pl.CostEstimate(flops=1, bytes_accessed=1, transcendentals=0),
    )(*operands)


def pair_terms(integrals, vir_coeff, occ_energy, vir_energy, kappas):
    aux_local, occ_count, basis = integrals.shape
    vir_local = vir_coeff.shape[1]
    wide_index = lax.axis_index("wide")
    batch_index = lax.axis_index("batch")
    place = jnp.stack(
        [wide_index, batch_index, jnp.full((), occ_count, wide_index.dtype)]
    ).astype(jnp.int32)
    vir_rows = vir_energy.reshape(-1, vir_local)
    flat_ints = integrals.reshape(aux_local * occ_count, basis)
    transformed = jnp.dot(flat_ints, vir_coeff, preferred_element_type=jnp.float32).astype(
        jnp.bfloat16
    )
    transformed = transformed.reshape(aux_local, occ_count, vir_local)

    def to_owner(columns):
        return lax.all_to_all(columns, "wide", split_axis=1, concat_axis=0, tiled=True)[:, 0, :]

    def over_batch(value):
        return from_behind(value, "batch", 1)

    def over_cores(value):
        return swap_by(value, "wide", 1)

    def over_pairs(value):
        return swap_by(value, "wide", 2)

    def along(value):
        return hand_along(value, "wide")

    together = lax.optimization_barrier
    sends_near = ((wide_index ^ (wide_index >> 1)) & 1) == 0
    energies = jnp.concatenate([kappas, occ_energy])
    transformed, sends_near, vir_rows, place, energies = together(
        (transformed, sends_near, vir_rows, place, energies)
    )
    own = to_owner(transformed)

    def for_sibling(near, far):
        return over_cores(jnp.where(sends_near, near, far))

    cut = vir_local // 2
    sibling = over_cores(own)
    low, high = cut_in_two(own)
    step = functools.partial(add_terms, place, energies, vir_rows, kappas.shape[0])

    own_o_high = over_batch(high)
    near_low = over_pairs(low)
    *made, density = step(None, [("own", 0, 0, low), ("own", 0, cut, high)], None, (2, 512))
    step = functools.partial(step, made)

    low, high, density = together((low, high, density))
    own_o_low = over_batch(low)
    near_high = over_pairs(high)
    density = step([("sibling", 0, 0, sibling)], density, (2, 1536))

    near_low, own_o_high, density = together((near_low, own_o_high, density))
    far_low = along(near_low)
    near_o_high = over_pairs(own_o_high)
    near_o_low = over_batch(near_low)
    sibling_o_high = over_cores(own_o_high)
    density = step([("own", 1, cut, own_o_high), ("near", 0, 0, near_low)], density, (4, 768))

    own_o_low, near_high, density = together((own_o_low, near_high, density))
    far_high = along(near_high)
    sibling_o_low = over_cores(own_o_low)
    density = step([("own", 1, 0, own_o_low), ("near", 0, cut, near_high)], density, (8, 512))

    far_low, near_o_high, near_o_low, density = together(
        (far_low, near_o_high, near_o_low, density)
    )
    far_o_low = over_batch(far_low)
    far_o_high = along(near_o_high)
    density = step(
        [
            ("sibling", 1, 0, sibling_o_low),
            ("sibling", 1, cut, sibling_o_high),
            ("far", 0, 0, far_low),
            ("near", 1, cut, near_o_high),
        ],
        density,
        (2, 512),
    )

    far_low, far_high, density = together((far_low, far_high, density))
    third_low = for_sibling(near_low, far_low)
    third_high = for_sibling(near_high, far_high)
    density = step([("near", 1, 0, near_o_low), ("far", 0, cut, far_high)], density, (2, 768))

    far_o_low, far_o_high, density = together((far_o_low, far_o_high, density))
    third_o_low = for_sibling(near_o_low, far_o_low)
    third_o_high = for_sibling(near_o_high, far_o_high)
    return step(
        [
            ("third", 0, 0, third_low),
            ("third", 0, cut, third_high),
            ("far", 1, 0, far_o_low),
            ("far", 1, cut, far_o_high),
            ("third", 1, 0, third_o_low),
            ("third", 1, cut, third_o_high),
        ],
        density,
        (2, 512),
        True,
    )


def pair_density(own_slice, partner, own_energy, partner_energy, row_energy, vir_energy, kappas):
    coulomb = lax.dot_general(
        own_slice, partner, (((0,), (0,)), ((), ())), preferred_element_type=jnp.float32
    )
    denominator = row_energy[:, None] + vir_energy[None, :] - own_energy - partner_energy
    damping = 1.0 - jnp.exp(-kappas[:, None, None] * denominator[None])
    amplitude = (-coulomb[None] * (damping * damping) / denominator[None]).astype(jnp.bfloat16)
    flat = amplitude.reshape(-1, amplitude.shape[2])
    density = lax.dot_general(
        flat, partner, (((1,), (1,)), ((), ())), preferred_element_type=jnp.float32
    )
    return density.reshape(kappas.shape[0], own_slice.shape[1], partner.shape[0])


def ring_terms(integrals, vir_coeff, occ_energy, vir_energy, kappas):
    aux_local, occ_count, basis = integrals.shape
    vir_local = vir_coeff.shape[1]
    batch_index = lax.axis_index("batch")
    wide_index = lax.axis_index("wide")
    flat_ints = integrals.reshape(aux_local * occ_count, basis)
    row_energy = lax.dynamic_slice_in_dim(vir_energy, batch_index * vir_local, vir_local, 0)
    own_energy = lax.dynamic_slice_in_dim(occ_energy, wide_index, 1, 0)[0]

    def term(partner, offset, own_slice):
        partner_index = (wide_index + offset) % occ_count
        partner_energy = lax.dynamic_slice_in_dim(occ_energy, partner_index, 1, 0)[0]
        return pair_density(
            own_slice, partner, own_energy, partner_energy, row_energy, vir_energy, kappas
        )

    transformed = jnp.dot(flat_ints, vir_coeff, preferred_element_type=jnp.float32).astype(
        jnp.bfloat16
    )
    transformed = transformed.reshape(aux_local, occ_count, vir_local)
    own_slice = lax.all_to_all(transformed, "wide", split_axis=1, concat_axis=0, tiled=True)[
        :, 0, :
    ]
    own_full = lax.all_gather(own_slice, "batch", axis=1, tiled=True)
    density = term(own_full, 0, own_slice)
    upper = own_full
    lower = own_full
    for offset in range(1, HALF + 1):
        upper = from_behind(upper, "wide", -1)
        lower = from_behind(lower, "wide", 1)
        density = density + term(upper, offset, own_slice) + term(lower, -offset, own_slice)
    return density.astype(jnp.bfloat16)[:, None, :, :]


def solution(mesh):
    paired = mesh.shape["batch"] == 2 and mesh.shape["wide"] % 4 == 0

    return jax.shard_map(
        pair_terms if paired else ring_terms,
        mesh=mesh,
        in_specs=(P("wide", None, None), P(None, "batch"), P(), P(), P()),
        out_specs=P(None, "wide", "batch", None),
        check_vma=False,
    )
```

```python
import functools

import jax
import jax.numpy as jnp
from jax import lax
from jax.experimental import pallas as pl
from jax.experimental.pallas import tpu as pltpu
from jax.sharding import PartitionSpec as P

HALF = 2
P_TILE = 512
VMEM_LIMIT = 18 * 1024 * 1024
LANES = 128


def from_behind(shard, axis, by):
    peers = lax.axis_size(axis)
    return lax.ppermute(shard, axis, [(i, (i + by) % peers) for i in range(peers)])


def swap_by(shard, axis, bit):
    peers = lax.axis_size(axis)
    return lax.ppermute(shard, axis, [(i, i ^ bit) for i in range(peers)])


def hand_along(shard, axis):
    peers = lax.axis_size(axis)
    return lax.ppermute(
        shard,
        axis,
        [(i, (i + (4 if i // 2 % 2 == 0 else -4)) % peers) for i in range(peers)],
    )


def cut_kernel(own, low, high):
    cut = low.shape[1]
    low[...] = own[:, :cut]
    high[...] = own[:, cut:]


def cut_in_two(own):
    vmem = pl.BlockSpec(memory_space=pltpu.VMEM)
    half = jax.ShapeDtypeStruct((own.shape[0], own.shape[1] // 2), own.dtype)
    return pl.pallas_call(
        cut_kernel,
        out_shape=(half, half),
        in_specs=[vmem],
        out_specs=(vmem, vmem),
        compiler_params=pltpu.CompilerParams(vmem_limit_bytes=VMEM_LIMIT),
        cost_estimate=pl.CostEstimate(flops=1, bytes_accessed=1, transcendentals=0),
    )(own)


def make_factors(place, kappa, occ, vir_rows, own_low, own_high, own_t, row_energies, row_factors):
    rows = own_t.shape[0]
    row_energy = vir_rows[pl.ds(place[1], 1), :] - occ(place[0])

    def down_columns(row):
        return jnp.transpose(jnp.broadcast_to(row, (LANES, rows)))

    own_t[:rows // 2, :] = jnp.transpose(own_low[...])
    own_t[rows // 2:, :] = jnp.transpose(own_high[...])
    row_energies[...] = down_columns(row_energy)
    for q in range(row_factors.shape[0]):
        row_factors[q] = down_columns(jnp.exp(-kappa(q) * row_energy))


def terms_kernel(pieces, mode, shape, place, energies, vir_rows, *refs):
    if mode == "first":
        partners = refs[:len(pieces)]
        own_t, row_energies, row_factors, out, amp, ratio = refs[len(pieces):]
    else:
        own_t, row_energies, row_factors = refs[:3]
        partners = refs[3:3 + len(pieces)]
        partial, *refs = refs[3 + len(pieces):]
        if mode == "last":
            result, amp, ratio, out, sems = refs
        else:
            out, amp, ratio = refs
    group_size, p_tile = shape
    nkap, rows = row_factors.shape[0], row_factors.shape[1]
    naux = own_t.shape[1]
    orbital, half, count = place[0], place[1], place[2]

    def kappa(q):
        return energies[q]

    def occ(index):
        return energies[nkap + index]

    if mode == "first":
        make_factors(
            place, kappa, occ, vir_rows, partners[0], partners[1], own_t, row_energies, row_factors
        )
    core_sign = 1 - 2 * lax.rem(orbital, 2)
    pair_sign = 1 - 2 * lax.rem(lax.div(orbital, 2), 2)
    offsets = dict(
        own=0, sibling=core_sign, third=-core_sign, near=HALF * pair_sign, far=-HALF * pair_sign
    )

    column_energies = []
    for (name, other, start), partner in zip(pieces, partners):
        index = lax.rem(orbital + offsets[name] + count, count)
        column_half = lax.rem(half + other, 2)
        energy = vir_rows[pl.ds(column_half, 1), :] - occ(index)
        for c in range(start, start + partner.shape[1], LANES):
            column_energies.append(energy[:, c:c + LANES])
    width = LANES * len(column_energies)

    def partner_columns(tile):
        return jnp.concatenate([partner[tile, :] for partner in partners], axis=1)

    for at in range(0, width, 2 * LANES):
        columns = partner_columns(slice(None))[:, at:at + 2 * LANES]
        coulomb = jnp.dot(own_t[...], columns, preferred_element_type=jnp.float32)
        for c in range(0, columns.shape[1], LANES):
            energy = column_energies[(at + c) // LANES]
            ratio[:, at + c:at + c + LANES] = -coulomb[:, c:c + LANES] / (
                row_energies[...] + energy
            )

    copies = []
    for group in range(0, nkap, group_size):
        top, bottom = group * rows, (group + group_size) * rows
        for q in range(group, group + group_size):
            for position, energy in enumerate(column_energies):
                columns = slice(position * LANES, (position + 1) * LANES)
                damping = 1.0 - row_factors[q] * jnp.exp(-kappa(q) * energy)
                amp[q * rows:(q + 1) * rows, columns] = (
                    ratio[:, columns] * damping * damping
                ).astype(amp.dtype)
        span = slice(group, group + group_size)
        for start in range(0, naux, p_tile):
            tile = slice(start, start + p_tile)
            value = lax.dot_general(
                amp[top:bottom, :],
                partner_columns(tile),
                (((1,), (1,)), ((), ())),
                preferred_element_type=jnp.float32,
            ).reshape(group_size, rows, p_tile)
            if mode != "first":
                value = value + partial[span, :, tile]
            out[span, :, tile] = value.astype(out.dtype)
            if mode == "last":
                copy = pltpu.make_async_copy(
                    out.at[span, :, tile], result.at[span, 0, :, tile], sems.at[len(copies)]
                )
                copy.start()
                copies.append(copy)
    for copy in copies:
        copy.wait()


def add_terms(place, energies, vir_rows, nkap, made, partners, partial, last=False):
    shape = (nkap, P_TILE)
    pieces = tuple(partner[:3] for partner in partners)
    arrays = [partner[3] for partner in partners]
    naux = arrays[0].shape[0]
    rows = vir_rows.shape[1]
    width = sum(array.shape[1] for array in arrays)
    vmem = pl.BlockSpec(memory_space=pltpu.VMEM)
    smem = pl.BlockSpec(memory_space=pltpu.SMEM)
    density = jax.ShapeDtypeStruct((nkap, rows, naux), jnp.float32)
    scratch = [
        pltpu.VMEM((nkap * rows, width), jnp.bfloat16),
        pltpu.VMEM((rows, width), jnp.float32),
    ]
    aliases = {}
    if made is None:
        mode = "first"
        operands = [place, energies, vir_rows] + arrays
        out_shape = (
            jax.ShapeDtypeStruct((rows, naux), arrays[0].dtype),
            jax.ShapeDtypeStruct((rows, LANES), jnp.float32),
            jax.ShapeDtypeStruct((nkap, rows, LANES), jnp.float32),
            density,
        )
        out_specs = (vmem,) * 4
    else:
        mode = "last" if last else "middle"
        operands = [place, energies, vir_rows] + list(made) + arrays + [partial]
        if last:
            out_shape = jax.ShapeDtypeStruct((nkap, 1, rows, naux), jnp.bfloat16)
            out_specs = pl.BlockSpec(memory_space=pl.ANY)
            scratch.append(pltpu.VMEM((nkap, rows, naux), jnp.bfloat16))
            scratch.append(pltpu.SemaphoreType.DMA((nkap // shape[0] * (naux // shape[1]),)))
        else:
            out_shape, out_specs = density, vmem
            aliases = {len(operands) - 1: 0}
    return pl.pallas_call(
        functools.partial(terms_kernel, pieces, mode, shape),
        out_shape=out_shape,
        input_output_aliases=aliases,
        in_specs=[smem, smem] + [vmem] * (len(operands) - 2),
        out_specs=out_specs,
        scratch_shapes=scratch,
        compiler_params=pltpu.CompilerParams(vmem_limit_bytes=VMEM_LIMIT),
        cost_estimate=pl.CostEstimate(flops=1, bytes_accessed=1, transcendentals=0),
    )(*operands)


def pair_terms(integrals, vir_coeff, occ_energy, vir_energy, kappas):
    aux_local, occ_count, basis = integrals.shape
    vir_local = vir_coeff.shape[1]
    wide_index = lax.axis_index("wide")
    batch_index = lax.axis_index("batch")
    place = jnp.stack(
        [wide_index, batch_index, jnp.full((), occ_count, wide_index.dtype)]
    ).astype(jnp.int32)
    vir_rows = vir_energy.reshape(-1, vir_local)
    def to_owner(columns):
        return lax.all_to_all(columns, "wide", split_axis=1, concat_axis=0, tiled=True)[:, 0, :]

    def over_batch(value):
        return from_behind(value, "batch", 1)

    def over_cores(value):
        return swap_by(value, "wide", 1)

    def over_pairs(value):
        return swap_by(value, "wide", 2)

    def along(value):
        return hand_along(value, "wide")

    together = lax.optimization_barrier
    sends_near = ((wide_index ^ (wide_index >> 1)) & 1) == 0
    energies = jnp.concatenate([kappas, occ_energy])
    flat_ints = integrals.reshape(aux_local * occ_count, basis)
    transformed = jnp.dot(flat_ints, vir_coeff, preferred_element_type=jnp.float32).astype(
        jnp.bfloat16
    )
    own, sends_near, vir_rows, place, energies = together(
        (
            to_owner(transformed.reshape(aux_local, occ_count, vir_local)),
            sends_near,
            vir_rows,
            place,
            energies,
        )
    )

    def for_sibling(near, far):
        return over_cores(
            jnp.concatenate([jnp.where(sends_near, *pair) for pair in zip(near, far)], axis=1)
        )

    cut = vir_local // 2
    sibling = over_cores(own)
    low, high = cut_in_two(own)
    step = functools.partial(add_terms, place, energies, vir_rows, kappas.shape[0])

    own_o_high = over_batch(high)
    near_low = over_pairs(low)
    *made, density = step(None, [("own", 0, 0, low), ("own", 0, cut, high)], None)
    step = functools.partial(step, made)

    low, high, density = together((low, high, density))
    own_o_low = over_batch(low)
    near_high = over_pairs(high)
    density = step([("sibling", 0, 0, sibling)], density)

    near_low, own_o_high, density = together((near_low, own_o_high, density))
    near_o_high = over_pairs(own_o_high)
    far_low = along(near_low)
    density = step([("own", 1, cut, own_o_high), ("near", 0, 0, near_low)], density)

    own_o_low, own_o_high, near_low, near_high, density = together(
        (own_o_low, own_o_high, near_low, near_high, density)
    )
    far_high = along(near_high)
    near_o_low = over_batch(near_low)
    sibling_o = over_cores(jnp.concatenate([own_o_low, own_o_high], axis=1))
    density = step([("own", 1, 0, own_o_low), ("near", 0, cut, near_high)], density)

    far_low, near_o_high, density = together((far_low, near_o_high, density))
    far_o_high = along(near_o_high)
    far_o_low = over_batch(far_low)
    density = step([("far", 0, 0, far_low), ("near", 1, cut, near_o_high)], density)

    far_low, far_high, near_o_low, density = together((far_low, far_high, near_o_low, density))
    third_low = for_sibling((near_low,), (far_low,))
    third_high = for_sibling((near_high,), (far_high,))
    density = step(
        [("near", 1, 0, near_o_low), ("far", 0, cut, far_high), ("sibling", 1, 0, sibling_o)],
        density,
    )

    far_o_low, far_o_high, density = together((far_o_low, far_o_high, density))
    third_o_low = for_sibling((near_o_low,), (far_o_low,))
    third_o_high = for_sibling((near_o_high,), (far_o_high,))
    return step(
        [
            ("third", 0, 0, third_low),
            ("third", 0, cut, third_high),
            ("far", 1, 0, far_o_low),
            ("far", 1, cut, far_o_high),
            ("third", 1, 0, third_o_low),
            ("third", 1, cut, third_o_high),
        ],
        density,
        last=True,
    )


def pair_density(own_slice, partner, own_energy, partner_energy, row_energy, vir_energy, kappas):
    coulomb = lax.dot_general(
        own_slice, partner, (((0,), (0,)), ((), ())), preferred_element_type=jnp.float32
    )
    denominator = row_energy[:, None] + vir_energy[None, :] - own_energy - partner_energy
    damping = 1.0 - jnp.exp(-kappas[:, None, None] * denominator[None])
    amplitude = (-coulomb[None] * (damping * damping) / denominator[None]).astype(jnp.bfloat16)
    flat = amplitude.reshape(-1, amplitude.shape[2])
    density = lax.dot_general(
        flat, partner, (((1,), (1,)), ((), ())), preferred_element_type=jnp.float32
    )
    return density.reshape(kappas.shape[0], own_slice.shape[1], partner.shape[0])


def ring_terms(integrals, vir_coeff, occ_energy, vir_energy, kappas):
    aux_local, occ_count, basis = integrals.shape
    vir_local = vir_coeff.shape[1]
    batch_index = lax.axis_index("batch")
    wide_index = lax.axis_index("wide")
    flat_ints = integrals.reshape(aux_local * occ_count, basis)
    row_energy = lax.dynamic_slice_in_dim(vir_energy, batch_index * vir_local, vir_local, 0)
    own_energy = lax.dynamic_slice_in_dim(occ_energy, wide_index, 1, 0)[0]

    def term(partner, offset, own_slice):
        partner_index = (wide_index + offset) % occ_count
        partner_energy = lax.dynamic_slice_in_dim(occ_energy, partner_index, 1, 0)[0]
        return pair_density(
            own_slice, partner, own_energy, partner_energy, row_energy, vir_energy, kappas
        )

    transformed = jnp.dot(flat_ints, vir_coeff, preferred_element_type=jnp.float32).astype(
        jnp.bfloat16
    )
    transformed = transformed.reshape(aux_local, occ_count, vir_local)
    own_slice = lax.all_to_all(transformed, "wide", split_axis=1, concat_axis=0, tiled=True)[
        :, 0, :
    ]
    own_full = lax.all_gather(own_slice, "batch", axis=1, tiled=True)
    density = term(own_full, 0, own_slice)
    upper = own_full
    lower = own_full
    for offset in range(1, HALF + 1):
        upper = from_behind(upper, "wide", -1)
        lower = from_behind(lower, "wide", 1)
        density = density + term(upper, offset, own_slice) + term(lower, -offset, own_slice)
    return density.astype(jnp.bfloat16)[:, None, :, :]


def solution(mesh):
    paired = mesh.shape["batch"] == 2 and mesh.shape["wide"] % 4 == 0

    return jax.shard_map(
        pair_terms if paired else ring_terms,
        mesh=mesh,
        in_specs=(P("wide", None, None), P(None, "batch"), P(), P(), P()),
        out_specs=P(None, "wide", "batch", None),
        check_vma=False,
    )
```

```python
import functools

import jax
import jax.numpy as jnp
from jax import lax
from jax.experimental import pallas as pl
from jax.experimental.pallas import tpu as pltpu
from jax.sharding import PartitionSpec as P

HALF = 2
TRANSFORM_STEPS = 3
VMEM_LIMIT = 18 * 1024 * 1024
LANES = 128


def from_behind(shard, axis, by):
    peers = lax.axis_size(axis)
    return lax.ppermute(shard, axis, [(i, (i + by) % peers) for i in range(peers)])


def swap_by(shard, axis, bit):
    peers = lax.axis_size(axis)
    return lax.ppermute(shard, axis, [(i, i ^ bit) for i in range(peers)])


def hand_along(shard, axis):
    peers = lax.axis_size(axis)
    return lax.ppermute(
        shard,
        axis,
        [(i, (i + (4 if i // 2 % 2 == 0 else -4)) % peers) for i in range(peers)],
    )


def transform_kernel(integrals, vir_coeff, out, held, product, sems):
    occ_count, aux_local, vir_local = out.shape
    rows = aux_local // TRANSFORM_STEPS

    def fetch(step):
        span = pl.ds(step * rows, rows)
        return pltpu.make_async_copy(integrals.at[span], held.at[span], sems.at[step])

    for step in range(TRANSFORM_STEPS):
        fetch(step).start()
    for step in range(TRANSFORM_STEPS):
        fetch(step).wait()
        span = slice(step * rows, (step + 1) * rows)
        value = jnp.dot(
            held[span].reshape(rows * occ_count, held.shape[2]),
            vir_coeff[...],
            preferred_element_type=jnp.float32,
        )
        for at in range(0, vir_local, LANES):
            columns = slice(at, at + LANES)
            product[at // LANES, step] = value[:, columns]
            for orbital in range(occ_count):
                picked = product[at // LANES, step, pl.ds(orbital, rows, stride=occ_count), :]
                out[orbital, span, columns] = picked.astype(out.dtype)


def transform(integrals, vir_coeff):
    aux_local, occ_count, basis = integrals.shape
    vir_local = vir_coeff.shape[1]
    vmem = pl.BlockSpec(memory_space=pltpu.VMEM)
    rows = aux_local // TRANSFORM_STEPS
    return pl.pallas_call(
        transform_kernel,
        out_shape=jax.ShapeDtypeStruct((occ_count, aux_local, vir_local), integrals.dtype),
        in_specs=[pl.BlockSpec(memory_space=pltpu.HBM), vmem],
        out_specs=vmem,
        scratch_shapes=[
            pltpu.VMEM((aux_local, occ_count, basis), integrals.dtype),
            pltpu.VMEM((vir_local // LANES, TRANSFORM_STEPS, rows * occ_count, LANES), jnp.float32),
            pltpu.SemaphoreType.DMA((TRANSFORM_STEPS,)),
        ],
        compiler_params=pltpu.CompilerParams(vmem_limit_bytes=60 * 1024 * 1024),
        cost_estimate=pl.CostEstimate(flops=1, bytes_accessed=1, transcendentals=0),
    )(integrals, vir_coeff)


def cut_kernel(own, low, high):
    cut = low.shape[1]
    low[...] = own[:, :cut]
    high[...] = own[:, cut:]


def cut_in_two(own):
    vmem = pl.BlockSpec(memory_space=pltpu.VMEM)
    half = jax.ShapeDtypeStruct((own.shape[0], own.shape[1] // 2), own.dtype)
    return pl.pallas_call(
        cut_kernel,
        out_shape=(half, half),
        in_specs=[vmem],
        out_specs=(vmem, vmem),
        compiler_params=pltpu.CompilerParams(vmem_limit_bytes=VMEM_LIMIT),
        cost_estimate=pl.CostEstimate(flops=1, bytes_accessed=1, transcendentals=0),
    )(own)


def make_factors(place, kappa, occ, vir_rows, own_low, own_high, own_t, row_energies, row_factors):
    rows = own_t.shape[0]
    row_energy = vir_rows[pl.ds(place[1], 1), :] - occ(place[0])

    def down_columns(row):
        return jnp.transpose(jnp.broadcast_to(row, (LANES, rows)))

    own_t[:rows // 2, :] = jnp.transpose(own_low[...])
    own_t[rows // 2:, :] = jnp.transpose(own_high[...])
    row_energies[...] = down_columns(row_energy)
    for q in range(row_factors.shape[0]):
        row_factors[q] = down_columns(jnp.exp(-kappa(q) * row_energy))


def terms_kernel(pieces, mode, shape, place, energies, vir_rows, *refs):
    if mode == "first":
        partners = refs[:len(pieces)]
        own_t, row_energies, row_factors, out, amp, ratio = refs[len(pieces):]
    else:
        own_t, row_energies, row_factors = refs[:3]
        partners = refs[3:3 + len(pieces)]
        partial, *refs = refs[3 + len(pieces):]
        if mode == "last":
            result, amp, ratio, out, sems = refs
        else:
            out, amp, ratio = refs
    group_size, p_tile = shape
    nkap, rows = row_factors.shape[0], row_factors.shape[1]
    naux = own_t.shape[1]
    orbital, half, count = place[0], place[1], place[2]

    def kappa(q):
        return energies[q]

    def occ(index):
        return energies[nkap + index]

    if mode == "first":
        make_factors(
            place, kappa, occ, vir_rows, partners[0], partners[1], own_t, row_energies, row_factors
        )
    core_sign = 1 - 2 * lax.rem(orbital, 2)
    pair_sign = 1 - 2 * lax.rem(lax.div(orbital, 2), 2)
    offsets = dict(
        own=0, sibling=core_sign, third=-core_sign, near=HALF * pair_sign, far=-HALF * pair_sign
    )

    column_energies = []
    for (name, other, start), partner in zip(pieces, partners):
        index = lax.rem(orbital + offsets[name] + count, count)
        column_half = lax.rem(half + other, 2)
        energy = vir_rows[pl.ds(column_half, 1), :] - occ(index)
        for c in range(start, start + partner.shape[1], LANES):
            column_energies.append(energy[:, c:c + LANES])
    width = LANES * len(column_energies)

    def partner_columns(tile):
        return jnp.concatenate([partner[tile, :] for partner in partners], axis=1)

    for at in range(0, width, 2 * LANES):
        columns = partner_columns(slice(None))[:, at:at + 2 * LANES]
        coulomb = jnp.dot(own_t[...], columns, preferred_element_type=jnp.float32)
        for c in range(0, columns.shape[1], LANES):
            energy = column_energies[(at + c) // LANES]
            ratio[:, at + c:at + c + LANES] = -coulomb[:, c:c + LANES] / (
                row_energies[...] + energy
            )

    copies = []
    for group in range(0, nkap, group_size):
        top, bottom = group * rows, (group + group_size) * rows
        for q in range(group, group + group_size):
            for position, energy in enumerate(column_energies):
                columns = slice(position * LANES, (position + 1) * LANES)
                damping = 1.0 - row_factors[q] * jnp.exp(-kappa(q) * energy)
                amp[q * rows:(q + 1) * rows, columns] = (
                    ratio[:, columns] * damping * damping
                ).astype(amp.dtype)
        span = slice(group, group + group_size)
        for start in range(0, naux, p_tile):
            tile = slice(start, start + p_tile)
            value = lax.dot_general(
                amp[top:bottom, :],
                partner_columns(tile),
                (((1,), (1,)), ((), ())),
                preferred_element_type=jnp.float32,
            ).reshape(group_size, rows, p_tile)
            if mode != "first":
                value = value + partial[span, :, tile]
            out[span, :, tile] = value.astype(out.dtype)
        if mode == "last":
            copy = pltpu.make_async_copy(
                out.at[span], result.at[span, 0], sems.at[group // group_size]
            )
            copy.start()
            copies.append(copy)
    for copy in copies:
        copy.wait()


def add_terms(place, energies, vir_rows, nkap, made, partners, partial, shape, last=False):
    pieces = tuple(partner[:3] for partner in partners)
    arrays = [partner[3] for partner in partners]
    naux = arrays[0].shape[0]
    rows = vir_rows.shape[1]
    width = sum(array.shape[1] for array in arrays)
    vmem = pl.BlockSpec(memory_space=pltpu.VMEM)
    smem = pl.BlockSpec(memory_space=pltpu.SMEM)
    density = jax.ShapeDtypeStruct((nkap, rows, naux), jnp.float32)
    scratch = [
        pltpu.VMEM((nkap * rows, width), jnp.bfloat16),
        pltpu.VMEM((rows, width), jnp.float32),
    ]
    aliases = {}
    if made is None:
        mode = "first"
        operands = [place, energies, vir_rows] + arrays
        out_shape = (
            jax.ShapeDtypeStruct((rows, naux), arrays[0].dtype),
            jax.ShapeDtypeStruct((rows, LANES), jnp.float32),
            jax.ShapeDtypeStruct((nkap, rows, LANES), jnp.float32),
            density,
        )
        out_specs = (vmem,) * 4
    else:
        mode = "last" if last else "middle"
        operands = [place, energies, vir_rows] + list(made) + arrays + [partial]
        if last:
            out_shape = jax.ShapeDtypeStruct((nkap, 1, rows, naux), jnp.bfloat16)
            out_specs = pl.BlockSpec(memory_space=pl.ANY)
            scratch.append(pltpu.VMEM((nkap, rows, naux), jnp.bfloat16))
            scratch.append(pltpu.SemaphoreType.DMA((nkap // shape[0],)))
        else:
            out_shape, out_specs = density, vmem
            aliases = {len(operands) - 1: 0}
    return pl.pallas_call(
        functools.partial(terms_kernel, pieces, mode, shape),
        out_shape=out_shape,
        input_output_aliases=aliases,
        in_specs=[smem, smem] + [vmem] * (len(operands) - 2),
        out_specs=out_specs,
        scratch_shapes=scratch,
        compiler_params=pltpu.CompilerParams(vmem_limit_bytes=VMEM_LIMIT),
        cost_estimate=pl.CostEstimate(flops=1, bytes_accessed=1, transcendentals=0),
    )(*operands)


def pair_terms(integrals, vir_coeff, occ_energy, vir_energy, kappas):
    occ_count = integrals.shape[1]
    vir_local = vir_coeff.shape[1]
    wide_index = lax.axis_index("wide")
    batch_index = lax.axis_index("batch")
    place = jnp.stack(
        [wide_index, batch_index, jnp.full((), occ_count, wide_index.dtype)]
    ).astype(jnp.int32)
    vir_rows = vir_energy.reshape(-1, vir_local)
    def to_owner(columns):
        owned = lax.all_to_all(columns, "wide", split_axis=0, concat_axis=0, tiled=True)
        return owned.reshape(-1, owned.shape[2])

    def over_batch(value):
        return from_behind(value, "batch", 1)

    def over_cores(value):
        return swap_by(value, "wide", 1)

    def over_pairs(value):
        return swap_by(value, "wide", 2)

    def along(value):
        return hand_along(value, "wide")

    together = lax.optimization_barrier
    sends_near = ((wide_index ^ (wide_index >> 1)) & 1) == 0
    energies = jnp.concatenate([kappas, occ_energy])
    own, sends_near, vir_rows, place, energies = together(
        (
            to_owner(transform(integrals, vir_coeff)),
            sends_near,
            vir_rows,
            place,
            energies,
        )
    )

    def for_sibling(near, far):
        return over_cores(
            jnp.concatenate([jnp.where(sends_near, *pair) for pair in zip(near, far)], axis=1)
        )

    cut = vir_local // 2
    sibling = over_cores(own)
    low, high = cut_in_two(own)
    step = functools.partial(add_terms, place, energies, vir_rows, kappas.shape[0])

    own_o_high = over_batch(high)
    near_low = over_pairs(low)
    *made, density = step(None, [("own", 0, 0, low), ("own", 0, cut, high)], None, (8, 1536))
    step = functools.partial(step, made)

    low, high, density = together((low, high, density))
    own_o_low = over_batch(low)
    near_high = over_pairs(high)
    density = step([("sibling", 0, 0, sibling)], density, (8, 256))

    near_low, own_o_high, density = together((near_low, own_o_high, density))
    near_o_high = over_pairs(own_o_high)
    far_low = along(near_low)
    density = step([("own", 1, cut, own_o_high), ("near", 0, 0, near_low)], density, (8, 512))

    own_o_low, own_o_high, near_low, near_high, density = together(
        (own_o_low, own_o_high, near_low, near_high, density)
    )
    far_high = along(near_high)
    near_o_low = over_batch(near_low)
    sibling_o = over_cores(jnp.concatenate([own_o_low, own_o_high], axis=1))
    density = step([("own", 1, 0, own_o_low), ("near", 0, cut, near_high)], density, (8, 768))

    far_low, near_o_high, density = together((far_low, near_o_high, density))
    far_o_high = along(near_o_high)
    far_o_low = over_batch(far_low)
    density = step([("far", 0, 0, far_low), ("near", 1, cut, near_o_high)], density, (4, 512))

    far_low, far_high, near_o_low, density = together((far_low, far_high, near_o_low, density))
    third_low = for_sibling((near_low,), (far_low,))
    third_high = for_sibling((near_high,), (far_high,))
    density = step(
        [("near", 1, 0, near_o_low), ("far", 0, cut, far_high), ("sibling", 1, 0, sibling_o)],
        density,
        (2, 512),
    )

    far_o_low, far_o_high, density = together((far_o_low, far_o_high, density))
    third_o_low = for_sibling((near_o_low,), (far_o_low,))
    third_o_high = for_sibling((near_o_high,), (far_o_high,))
    return step(
        [
            ("third", 0, 0, third_low),
            ("third", 0, cut, third_high),
            ("far", 1, 0, far_o_low),
            ("far", 1, cut, far_o_high),
            ("third", 1, 0, third_o_low),
            ("third", 1, cut, third_o_high),
        ],
        density,
        (2, 512),
        last=True,
    )


def pair_density(own_slice, partner, own_energy, partner_energy, row_energy, vir_energy, kappas):
    coulomb = lax.dot_general(
        own_slice, partner, (((0,), (0,)), ((), ())), preferred_element_type=jnp.float32
    )
    denominator = row_energy[:, None] + vir_energy[None, :] - own_energy - partner_energy
    damping = 1.0 - jnp.exp(-kappas[:, None, None] * denominator[None])
    amplitude = (-coulomb[None] * (damping * damping) / denominator[None]).astype(jnp.bfloat16)
    flat = amplitude.reshape(-1, amplitude.shape[2])
    density = lax.dot_general(
        flat, partner, (((1,), (1,)), ((), ())), preferred_element_type=jnp.float32
    )
    return density.reshape(kappas.shape[0], own_slice.shape[1], partner.shape[0])


def ring_terms(integrals, vir_coeff, occ_energy, vir_energy, kappas):
    aux_local, occ_count, basis = integrals.shape
    vir_local = vir_coeff.shape[1]
    batch_index = lax.axis_index("batch")
    wide_index = lax.axis_index("wide")
    flat_ints = integrals.reshape(aux_local * occ_count, basis)
    row_energy = lax.dynamic_slice_in_dim(vir_energy, batch_index * vir_local, vir_local, 0)
    own_energy = lax.dynamic_slice_in_dim(occ_energy, wide_index, 1, 0)[0]

    def term(partner, offset, own_slice):
        partner_index = (wide_index + offset) % occ_count
        partner_energy = lax.dynamic_slice_in_dim(occ_energy, partner_index, 1, 0)[0]
        return pair_density(
            own_slice, partner, own_energy, partner_energy, row_energy, vir_energy, kappas
        )

    transformed = jnp.dot(flat_ints, vir_coeff, preferred_element_type=jnp.float32).astype(
        jnp.bfloat16
    )
    transformed = transformed.reshape(aux_local, occ_count, vir_local)
    own_slice = lax.all_to_all(transformed, "wide", split_axis=1, concat_axis=0, tiled=True)[
        :, 0, :
    ]
    own_full = lax.all_gather(own_slice, "batch", axis=1, tiled=True)
    density = term(own_full, 0, own_slice)
    upper = own_full
    lower = own_full
    for offset in range(1, HALF + 1):
        upper = from_behind(upper, "wide", -1)
        lower = from_behind(lower, "wide", 1)
        density = density + term(upper, offset, own_slice) + term(lower, -offset, own_slice)
    return density.astype(jnp.bfloat16)[:, None, :, :]


def solution(mesh):
    paired = mesh.shape["batch"] == 2 and mesh.shape["wide"] % 4 == 0

    return jax.shard_map(
        pair_terms if paired else ring_terms,
        mesh=mesh,
        in_specs=(P("wide", None, None), P(None, "batch"), P(), P(), P()),
        out_specs=P(None, "wide", "batch", None),
        check_vma=False,
    )
```

```python
import functools

import jax
import jax.numpy as jnp
from jax import lax
from jax.experimental import pallas as pl
from jax.experimental.pallas import tpu as pltpu
from jax.sharding import PartitionSpec as P

HALF = 2
TRANSFORM_STEPS = 3
VMEM_LIMIT = 18 * 1024 * 1024
LANES = 128


def from_behind(shard, axis, by):
    peers = lax.axis_size(axis)
    return lax.ppermute(shard, axis, [(i, (i + by) % peers) for i in range(peers)])


def swap_by(shard, axis, bit):
    peers = lax.axis_size(axis)
    return lax.ppermute(shard, axis, [(i, i ^ bit) for i in range(peers)])


def hand_along(shard, axis):
    peers = lax.axis_size(axis)
    return lax.ppermute(
        shard,
        axis,
        [(i, (i + (4 if i // 2 % 2 == 0 else -4)) % peers) for i in range(peers)],
    )


def transform_kernel(integrals, vir_coeff, out, held, coeff, turned, sems):
    occ_count, aux_local, vir_local = out.shape
    rows = aux_local // TRANSFORM_STEPS
    size = rows * occ_count

    def fetch(step):
        span = pl.ds(step * rows, rows)
        return pltpu.make_async_copy(integrals.at[span], held.at[span], sems.at[step])

    def send(step):
        return pltpu.make_async_copy(
            turned.at[step], out.at[:, pl.ds(step * rows, rows), :], sems.at[step]
        )

    fetch_coeff = pltpu.make_async_copy(vir_coeff, coeff, sems.at[TRANSFORM_STEPS])
    fetch_coeff.start()
    for step in range(TRANSFORM_STEPS):
        fetch(step).start()
    to = lax.broadcasted_iota(jnp.int32, (size, size), 0)
    source = lax.rem(to, rows) * occ_count + lax.div(to, rows)
    reorder = (lax.broadcasted_iota(jnp.int32, (size, size), 1) == source).astype(out.dtype)
    fetch_coeff.wait()
    for step in range(TRANSFORM_STEPS):
        fetch(step).wait()
        product = jnp.dot(
            held[step * rows:(step + 1) * rows].reshape(size, held.shape[2]),
            coeff[...],
            preferred_element_type=jnp.float32,
        ).astype(out.dtype)
        product = jnp.dot(reorder, product, preferred_element_type=jnp.float32)
        turned[step] = product.astype(out.dtype).reshape(occ_count, rows, vir_local)
        send(step).start()
    for step in range(TRANSFORM_STEPS):
        send(step).wait()


def transform(integrals, vir_coeff):
    aux_local, occ_count, basis = integrals.shape
    vir_local = vir_coeff.shape[1]
    hbm = pl.BlockSpec(memory_space=pl.ANY)
    rows = aux_local // TRANSFORM_STEPS
    return pl.pallas_call(
        transform_kernel,
        out_shape=jax.ShapeDtypeStruct((occ_count, aux_local, vir_local), integrals.dtype),
        in_specs=[hbm, hbm],
        out_specs=hbm,
        scratch_shapes=[
            pltpu.VMEM((aux_local, occ_count, basis), integrals.dtype),
            pltpu.VMEM((basis, vir_local), integrals.dtype),
            pltpu.VMEM((TRANSFORM_STEPS, occ_count, rows, vir_local), integrals.dtype),
            pltpu.SemaphoreType.DMA((TRANSFORM_STEPS + 1,)),
        ],
        compiler_params=pltpu.CompilerParams(vmem_limit_bytes=60 * 1024 * 1024),
        cost_estimate=pl.CostEstimate(flops=1, bytes_accessed=1, transcendentals=0),
    )(integrals, vir_coeff)


def cut_kernel(own, low, high):
    cut = low.shape[1]
    low[...] = own[:, :cut]
    high[...] = own[:, cut:]


def cut_in_two(own):
    vmem = pl.BlockSpec(memory_space=pltpu.VMEM)
    half = jax.ShapeDtypeStruct((own.shape[0], own.shape[1] // 2), own.dtype)
    return pl.pallas_call(
        cut_kernel,
        out_shape=(half, half),
        in_specs=[vmem],
        out_specs=(vmem, vmem),
        compiler_params=pltpu.CompilerParams(vmem_limit_bytes=VMEM_LIMIT),
        cost_estimate=pl.CostEstimate(flops=1, bytes_accessed=1, transcendentals=0),
    )(own)


def make_factors(place, kappa, occ, vir_rows, own_low, own_high, own_t, row_energies, row_factors):
    rows = own_t.shape[0]
    row_energy = vir_rows[pl.ds(place[1], 1), :] - occ(place[0])

    def down_columns(row):
        return jnp.transpose(jnp.broadcast_to(row, (LANES, rows)))

    own_t[:rows // 2, :] = jnp.transpose(own_low[...])
    own_t[rows // 2:, :] = jnp.transpose(own_high[...])
    row_energies[...] = down_columns(row_energy)
    for q in range(row_factors.shape[0]):
        row_factors[q] = down_columns(jnp.exp(-kappa(q) * row_energy))


def terms_kernel(pieces, mode, shape, place, energies, vir_rows, *refs):
    if mode == "first":
        partners = refs[:len(pieces)]
        own_t, row_energies, row_factors, out, amp, ratio = refs[len(pieces):]
    else:
        own_t, row_energies, row_factors = refs[:3]
        partners = refs[3:3 + len(pieces)]
        partial, *refs = refs[3 + len(pieces):]
        if mode == "last":
            result, amp, ratio, out, sems = refs
        else:
            out, amp, ratio = refs
    group_size, p_tile = shape
    nkap, rows = row_factors.shape[0], row_factors.shape[1]
    naux = own_t.shape[1]
    orbital, half, count = place[0], place[1], place[2]

    def kappa(q):
        return energies[q]

    def occ(index):
        return energies[nkap + index]

    if mode == "first":
        make_factors(
            place, kappa, occ, vir_rows, partners[0], partners[1], own_t, row_energies, row_factors
        )
    core_sign = 1 - 2 * lax.rem(orbital, 2)
    pair_sign = 1 - 2 * lax.rem(lax.div(orbital, 2), 2)
    offsets = dict(
        own=0, sibling=core_sign, third=-core_sign, near=HALF * pair_sign, far=-HALF * pair_sign
    )

    column_energies = []
    for (name, other, start), partner in zip(pieces, partners):
        index = lax.rem(orbital + offsets[name] + count, count)
        column_half = lax.rem(half + other, 2)
        energy = vir_rows[pl.ds(column_half, 1), :] - occ(index)
        for c in range(start, start + partner.shape[1], LANES):
            column_energies.append(energy[:, c:c + LANES])
    width = LANES * len(column_energies)

    def partner_columns(tile):
        return jnp.concatenate([partner[tile, :] for partner in partners], axis=1)

    for at in range(0, width, 2 * LANES):
        columns = partner_columns(slice(None))[:, at:at + 2 * LANES]
        coulomb = jnp.dot(own_t[...], columns, preferred_element_type=jnp.float32)
        for c in range(0, columns.shape[1], LANES):
            energy = column_energies[(at + c) // LANES]
            ratio[:, at + c:at + c + LANES] = -coulomb[:, c:c + LANES] / (
                row_energies[...] + energy
            )

    copies = []
    for group in range(0, nkap, group_size):
        top, bottom = group * rows, (group + group_size) * rows
        for q in range(group, group + group_size):
            for position, energy in enumerate(column_energies):
                columns = slice(position * LANES, (position + 1) * LANES)
                damping = 1.0 - row_factors[q] * jnp.exp(-kappa(q) * energy)
                amp[q * rows:(q + 1) * rows, columns] = (
                    ratio[:, columns] * damping * damping
                ).astype(amp.dtype)
        span = slice(group, group + group_size)
        for start in range(0, naux, p_tile):
            tile = slice(start, start + p_tile)
            value = lax.dot_general(
                amp[top:bottom, :],
                partner_columns(tile),
                (((1,), (1,)), ((), ())),
                preferred_element_type=jnp.float32,
            ).reshape(group_size, rows, p_tile)
            if mode != "first":
                value = value + partial[span, :, tile]
            out[span, :, tile] = value.astype(out.dtype)
        if mode == "last":
            copy = pltpu.make_async_copy(
                out.at[span], result.at[span, 0], sems.at[group // group_size]
            )
            copy.start()
            copies.append(copy)
    for copy in copies:
        copy.wait()


def add_terms(place, energies, vir_rows, nkap, made, partners, partial, shape, last=False):
    pieces = tuple(partner[:3] for partner in partners)
    arrays = [partner[3] for partner in partners]
    naux = arrays[0].shape[0]
    rows = vir_rows.shape[1]
    width = sum(array.shape[1] for array in arrays)
    vmem = pl.BlockSpec(memory_space=pltpu.VMEM)
    smem = pl.BlockSpec(memory_space=pltpu.SMEM)
    density = jax.ShapeDtypeStruct((nkap, rows, naux), jnp.float32)
    scratch = [
        pltpu.VMEM((nkap * rows, width), jnp.bfloat16),
        pltpu.VMEM((rows, width), jnp.float32),
    ]
    aliases = {}
    if made is None:
        mode = "first"
        operands = [place, energies, vir_rows] + arrays
        out_shape = (
            jax.ShapeDtypeStruct((rows, naux), arrays[0].dtype),
            jax.ShapeDtypeStruct((rows, LANES), jnp.float32),
            jax.ShapeDtypeStruct((nkap, rows, LANES), jnp.float32),
            density,
        )
        out_specs = (vmem,) * 4
    else:
        mode = "last" if last else "middle"
        operands = [place, energies, vir_rows] + list(made) + arrays + [partial]
        if last:
            out_shape = jax.ShapeDtypeStruct((nkap, 1, rows, naux), jnp.bfloat16)
            out_specs = pl.BlockSpec(memory_space=pl.ANY)
            scratch.append(pltpu.VMEM((nkap, rows, naux), jnp.bfloat16))
            scratch.append(pltpu.SemaphoreType.DMA((nkap // shape[0],)))
        else:
            out_shape, out_specs = density, vmem
            aliases = {len(operands) - 1: 0}
    return pl.pallas_call(
        functools.partial(terms_kernel, pieces, mode, shape),
        out_shape=out_shape,
        input_output_aliases=aliases,
        in_specs=[smem, smem] + [vmem] * (len(operands) - 2),
        out_specs=out_specs,
        scratch_shapes=scratch,
        compiler_params=pltpu.CompilerParams(vmem_limit_bytes=VMEM_LIMIT),
        cost_estimate=pl.CostEstimate(flops=1, bytes_accessed=1, transcendentals=0),
    )(*operands)


def pair_terms(integrals, vir_coeff, occ_energy, vir_energy, kappas):
    occ_count = integrals.shape[1]
    vir_local = vir_coeff.shape[1]
    wide_index = lax.axis_index("wide")
    batch_index = lax.axis_index("batch")
    place = jnp.stack(
        [wide_index, batch_index, jnp.full((), occ_count, wide_index.dtype)]
    ).astype(jnp.int32)
    vir_rows = vir_energy.reshape(-1, vir_local)
    def to_owner(columns):
        owned = lax.all_to_all(columns, "wide", split_axis=0, concat_axis=0, tiled=True)
        return owned.reshape(-1, owned.shape[2])

    def over_batch(value):
        return from_behind(value, "batch", 1)

    def over_cores(value):
        return swap_by(value, "wide", 1)

    def over_pairs(value):
        return swap_by(value, "wide", 2)

    def along(value):
        return hand_along(value, "wide")

    together = lax.optimization_barrier
    sends_near = ((wide_index ^ (wide_index >> 1)) & 1) == 0
    energies = jnp.concatenate([kappas, occ_energy])
    own, sends_near, vir_rows, place, energies = together(
        (
            to_owner(transform(integrals, vir_coeff)),
            sends_near,
            vir_rows,
            place,
            energies,
        )
    )

    def for_sibling(near, far):
        return over_cores(
            jnp.concatenate([jnp.where(sends_near, *pair) for pair in zip(near, far)], axis=1)
        )

    cut = vir_local // 2
    sibling = over_cores(own)
    low, high = cut_in_two(own)
    step = functools.partial(add_terms, place, energies, vir_rows, kappas.shape[0])

    own_o_high = over_batch(high)
    near_low = over_pairs(low)
    *made, density = step(None, [("own", 0, 0, low), ("own", 0, cut, high)], None, (8, 512))
    step = functools.partial(step, made)

    low, high, density = together((low, high, density))
    own_o_low = over_batch(low)
    near_high = over_pairs(high)
    density = step([("sibling", 0, 0, sibling)], density, (8, 512))

    near_low, own_o_high, density = together((near_low, own_o_high, density))
    near_o_high = over_pairs(own_o_high)
    far_low = along(near_low)
    density = step([("own", 1, cut, own_o_high), ("near", 0, 0, near_low)], density, (8, 512))

    own_o_low, own_o_high, near_low, near_high, density = together(
        (own_o_low, own_o_high, near_low, near_high, density)
    )
    far_high = along(near_high)
    near_o_low = over_batch(near_low)
    sibling_o = over_cores(jnp.concatenate([own_o_low, own_o_high], axis=1))
    density = step([("own", 1, 0, own_o_low), ("near", 0, cut, near_high)], density, (8, 512))

    far_low, near_o_high, density = together((far_low, near_o_high, density))
    far_o_high = along(near_o_high)
    far_o_low = over_batch(far_low)
    density = step([("far", 0, 0, far_low), ("near", 1, cut, near_o_high)], density, (8, 512))

    far_low, far_high, near_o_low, density = together((far_low, far_high, near_o_low, density))
    third_low = for_sibling((near_low,), (far_low,))
    third_high = for_sibling((near_high,), (far_high,))
    density = step(
        [("near", 1, 0, near_o_low), ("far", 0, cut, far_high), ("sibling", 1, 0, sibling_o)],
        density,
        (2, 512),
    )

    far_o_low, far_o_high, density = together((far_o_low, far_o_high, density))
    third_o_low = for_sibling((near_o_low,), (far_o_low,))
    third_o_high = for_sibling((near_o_high,), (far_o_high,))
    return step(
        [
            ("third", 0, 0, third_low),
            ("third", 0, cut, third_high),
            ("far", 1, 0, far_o_low),
            ("far", 1, cut, far_o_high),
            ("third", 1, 0, third_o_low),
            ("third", 1, cut, third_o_high),
        ],
        density,
        (2, 512),
        last=True,
    )


def pair_density(own_slice, partner, own_energy, partner_energy, row_energy, vir_energy, kappas):
    coulomb = lax.dot_general(
        own_slice, partner, (((0,), (0,)), ((), ())), preferred_element_type=jnp.float32
    )
    denominator = row_energy[:, None] + vir_energy[None, :] - own_energy - partner_energy
    damping = 1.0 - jnp.exp(-kappas[:, None, None] * denominator[None])
    amplitude = (-coulomb[None] * (damping * damping) / denominator[None]).astype(jnp.bfloat16)
    flat = amplitude.reshape(-1, amplitude.shape[2])
    density = lax.dot_general(
        flat, partner, (((1,), (1,)), ((), ())), preferred_element_type=jnp.float32
    )
    return density.reshape(kappas.shape[0], own_slice.shape[1], partner.shape[0])


def ring_terms(integrals, vir_coeff, occ_energy, vir_energy, kappas):
    aux_local, occ_count, basis = integrals.shape
    vir_local = vir_coeff.shape[1]
    batch_index = lax.axis_index("batch")
    wide_index = lax.axis_index("wide")
    flat_ints = integrals.reshape(aux_local * occ_count, basis)
    row_energy = lax.dynamic_slice_in_dim(vir_energy, batch_index * vir_local, vir_local, 0)
    own_energy = lax.dynamic_slice_in_dim(occ_energy, wide_index, 1, 0)[0]

    def term(partner, offset, own_slice):
        partner_index = (wide_index + offset) % occ_count
        partner_energy = lax.dynamic_slice_in_dim(occ_energy, partner_index, 1, 0)[0]
        return pair_density(
            own_slice, partner, own_energy, partner_energy, row_energy, vir_energy, kappas
        )

    transformed = jnp.dot(flat_ints, vir_coeff, preferred_element_type=jnp.float32).astype(
        jnp.bfloat16
    )
    transformed = transformed.reshape(aux_local, occ_count, vir_local)
    own_slice = lax.all_to_all(transformed, "wide", split_axis=1, concat_axis=0, tiled=True)[
        :, 0, :
    ]
    own_full = lax.all_gather(own_slice, "batch", axis=1, tiled=True)
    density = term(own_full, 0, own_slice)
    upper = own_full
    lower = own_full
    for offset in range(1, HALF + 1):
        upper = from_behind(upper, "wide", -1)
        lower = from_behind(lower, "wide", 1)
        density = density + term(upper, offset, own_slice) + term(lower, -offset, own_slice)
    return density.astype(jnp.bfloat16)[:, None, :, :]


def solution(mesh):
    paired = mesh.shape["batch"] == 2 and mesh.shape["wide"] % 4 == 0

    return jax.shard_map(
        pair_terms if paired else ring_terms,
        mesh=mesh,
        in_specs=(P("wide", None, None), P(None, "batch"), P(), P(), P()),
        out_specs=P(None, "wide", "batch", None),
        check_vma=False,
    )
```

```python
import functools

import jax
import jax.numpy as jnp
from jax import lax
from jax.experimental import pallas as pl
from jax.experimental.pallas import tpu as pltpu
from jax.sharding import PartitionSpec as P

HALF = 2
TRANSFORM_STEPS = 3
VMEM_LIMIT = 18 * 1024 * 1024
LANES = 128


def from_behind(shard, axis, by):
    peers = lax.axis_size(axis)
    return lax.ppermute(shard, axis, [(i, (i + by) % peers) for i in range(peers)])


def swap_by(shard, axis, bit):
    peers = lax.axis_size(axis)
    return lax.ppermute(shard, axis, [(i, i ^ bit) for i in range(peers)])


def hand_along(shard, axis):
    peers = lax.axis_size(axis)
    return lax.ppermute(
        shard,
        axis,
        [(i, (i + (4 if i // 2 % 2 == 0 else -4)) % peers) for i in range(peers)],
    )


def transform_kernel(integrals, vir_coeff, out, held, coeff, turned, sems):
    occ_count, aux_local, vir_local = out.shape
    rows = aux_local // TRANSFORM_STEPS
    size = rows * occ_count

    def fetch(step):
        span = pl.ds(step * rows, rows)
        return pltpu.make_async_copy(integrals.at[span], held.at[span], sems.at[step])

    def send(step):
        return pltpu.make_async_copy(
            turned.at[step], out.at[:, pl.ds(step * rows, rows), :], sems.at[step]
        )

    fetch_coeff = pltpu.make_async_copy(vir_coeff, coeff, sems.at[TRANSFORM_STEPS])
    fetch_coeff.start()
    for step in range(TRANSFORM_STEPS):
        fetch(step).start()
    source = lax.broadcasted_iota(jnp.int32, (1, size), 1)
    to = lax.rem(source, occ_count) * rows + lax.div(source, occ_count)
    reorder = (lax.broadcasted_iota(jnp.int32, (size, size), 0) == to).astype(out.dtype)
    fetch_coeff.wait()
    for step in range(TRANSFORM_STEPS):
        fetch(step).wait()
        product = jnp.dot(
            held[step * rows:(step + 1) * rows].reshape(size, held.shape[2]),
            coeff[...],
            preferred_element_type=jnp.float32,
        ).astype(out.dtype)
        product = jnp.dot(reorder, product, preferred_element_type=jnp.float32)
        turned[step] = product.astype(out.dtype).reshape(occ_count, rows, vir_local)
        send(step).start()
    for step in range(TRANSFORM_STEPS):
        send(step).wait()


def transform(integrals, vir_coeff):
    aux_local, occ_count, basis = integrals.shape
    vir_local = vir_coeff.shape[1]
    hbm = pl.BlockSpec(memory_space=pl.ANY)
    rows = aux_local // TRANSFORM_STEPS
    return pl.pallas_call(
        transform_kernel,
        out_shape=jax.ShapeDtypeStruct((occ_count, aux_local, vir_local), integrals.dtype),
        in_specs=[hbm, hbm],
        out_specs=hbm,
        scratch_shapes=[
            pltpu.VMEM((aux_local, occ_count, basis), integrals.dtype),
            pltpu.VMEM((basis, vir_local), integrals.dtype),
            pltpu.VMEM((TRANSFORM_STEPS, occ_count, rows, vir_local), integrals.dtype),
            pltpu.SemaphoreType.DMA((TRANSFORM_STEPS + 1,)),
        ],
        compiler_params=pltpu.CompilerParams(vmem_limit_bytes=60 * 1024 * 1024),
        cost_estimate=pl.CostEstimate(flops=1, bytes_accessed=1, transcendentals=0),
    )(integrals, vir_coeff)


def cut_kernel(own, low, high):
    cut = low.shape[1]
    low[...] = own[:, :cut]
    high[...] = own[:, cut:]


def cut_in_two(own):
    vmem = pl.BlockSpec(memory_space=pltpu.VMEM)
    half = jax.ShapeDtypeStruct((own.shape[0], own.shape[1] // 2), own.dtype)
    return pl.pallas_call(
        cut_kernel,
        out_shape=(half, half),
        in_specs=[vmem],
        out_specs=(vmem, vmem),
        compiler_params=pltpu.CompilerParams(vmem_limit_bytes=VMEM_LIMIT),
        cost_estimate=pl.CostEstimate(flops=1, bytes_accessed=1, transcendentals=0),
    )(own)


def make_factors(place, kappa, occ, vir_rows, own_low, own_high, own_t, row_energies, row_factors):
    rows = own_t.shape[0]
    row_energy = vir_rows[pl.ds(place[1], 1), :] - occ(place[0])

    def down_columns(row):
        return jnp.transpose(jnp.broadcast_to(row, (LANES, rows)))

    own_t[:rows // 2, :] = jnp.transpose(own_low[...])
    own_t[rows // 2:, :] = jnp.transpose(own_high[...])
    row_energies[...] = down_columns(row_energy)
    for q in range(row_factors.shape[0]):
        row_factors[q] = down_columns(jnp.exp(-kappa(q) * row_energy))


def terms_kernel(pieces, mode, shape, place, energies, vir_rows, *refs):
    if mode == "first":
        partners = refs[:len(pieces)]
        own_t, row_energies, row_factors, out, amp, ratio = refs[len(pieces):]
    else:
        own_t, row_energies, row_factors = refs[:3]
        partners = refs[3:3 + len(pieces)]
        partial, *refs = refs[3 + len(pieces):]
        if mode == "last":
            result, amp, ratio, out, sems = refs
        else:
            out, amp, ratio = refs
    group_size, p_tile = shape
    nkap, rows = row_factors.shape[0], row_factors.shape[1]
    naux = own_t.shape[1]
    orbital, half, count = place[0], place[1], place[2]

    def kappa(q):
        return energies[q]

    def occ(index):
        return energies[nkap + index]

    if mode == "first":
        make_factors(
            place, kappa, occ, vir_rows, partners[0], partners[1], own_t, row_energies, row_factors
        )
    core_sign = 1 - 2 * lax.rem(orbital, 2)
    pair_sign = 1 - 2 * lax.rem(lax.div(orbital, 2), 2)
    offsets = dict(
        own=0, sibling=core_sign, third=-core_sign, near=HALF * pair_sign, far=-HALF * pair_sign
    )

    column_energies = []
    for (name, other, start), partner in zip(pieces, partners):
        index = lax.rem(orbital + offsets[name] + count, count)
        column_half = lax.rem(half + other, 2)
        energy = vir_rows[pl.ds(column_half, 1), :] - occ(index)
        for c in range(start, start + partner.shape[1], LANES):
            column_energies.append(energy[:, c:c + LANES])
    width = LANES * len(column_energies)

    def partner_columns(tile):
        return jnp.concatenate([partner[tile, :] for partner in partners], axis=1)

    for at in range(0, width, 2 * LANES):
        columns = partner_columns(slice(None))[:, at:at + 2 * LANES]
        coulomb = jnp.dot(own_t[...], columns, preferred_element_type=jnp.float32)
        for c in range(0, columns.shape[1], LANES):
            energy = column_energies[(at + c) // LANES]
            ratio[:, at + c:at + c + LANES] = -coulomb[:, c:c + LANES] / (
                row_energies[...] + energy
            )

    copies = []
    for group in range(0, nkap, group_size):
        top, bottom = group * rows, (group + group_size) * rows
        for q in range(group, group + group_size):
            for position, energy in enumerate(column_energies):
                columns = slice(position * LANES, (position + 1) * LANES)
                damping = 1.0 - row_factors[q] * jnp.exp(-kappa(q) * energy)
                amp[q * rows:(q + 1) * rows, columns] = (
                    ratio[:, columns] * damping * damping
                ).astype(amp.dtype)
        span = slice(group, group + group_size)
        for start in range(0, naux, p_tile):
            tile = slice(start, start + p_tile)
            value = lax.dot_general(
                amp[top:bottom, :],
                partner_columns(tile),
                (((1,), (1,)), ((), ())),
                preferred_element_type=jnp.float32,
            ).reshape(group_size, rows, p_tile)
            if mode != "first":
                value = value + partial[span, :, tile]
            out[span, :, tile] = value.astype(out.dtype)
        if mode == "last":
            copy = pltpu.make_async_copy(
                out.at[span], result.at[span, 0], sems.at[group // group_size]
            )
            copy.start()
            copies.append(copy)
    for copy in copies:
        copy.wait()


def add_terms(place, energies, vir_rows, nkap, made, partners, partial, shape, last=False):
    pieces = tuple(partner[:3] for partner in partners)
    arrays = [partner[3] for partner in partners]
    naux = arrays[0].shape[0]
    rows = vir_rows.shape[1]
    width = sum(array.shape[1] for array in arrays)
    vmem = pl.BlockSpec(memory_space=pltpu.VMEM)
    smem = pl.BlockSpec(memory_space=pltpu.SMEM)
    density = jax.ShapeDtypeStruct((nkap, rows, naux), jnp.float32)
    scratch = [
        pltpu.VMEM((nkap * rows, width), jnp.bfloat16),
        pltpu.VMEM((rows, width), jnp.float32),
    ]
    aliases = {}
    if made is None:
        mode = "first"
        operands = [place, energies, vir_rows] + arrays
        out_shape = (
            jax.ShapeDtypeStruct((rows, naux), arrays[0].dtype),
            jax.ShapeDtypeStruct((rows, LANES), jnp.float32),
            jax.ShapeDtypeStruct((nkap, rows, LANES), jnp.float32),
            density,
        )
        out_specs = (vmem,) * 4
    else:
        mode = "last" if last else "middle"
        operands = [place, energies, vir_rows] + list(made) + arrays + [partial]
        if last:
            out_shape = jax.ShapeDtypeStruct((nkap, 1, rows, naux), jnp.bfloat16)
            out_specs = pl.BlockSpec(memory_space=pl.ANY)
            scratch.append(pltpu.VMEM((nkap, rows, naux), jnp.bfloat16))
            scratch.append(pltpu.SemaphoreType.DMA((nkap // shape[0],)))
        else:
            out_shape, out_specs = density, vmem
            aliases = {len(operands) - 1: 0}
    return pl.pallas_call(
        functools.partial(terms_kernel, pieces, mode, shape),
        out_shape=out_shape,
        input_output_aliases=aliases,
        in_specs=[smem, smem] + [vmem] * (len(operands) - 2),
        out_specs=out_specs,
        scratch_shapes=scratch,
        compiler_params=pltpu.CompilerParams(vmem_limit_bytes=VMEM_LIMIT),
        cost_estimate=pl.CostEstimate(flops=1, bytes_accessed=1, transcendentals=0),
    )(*operands)


def spacer_kernel(value, same):
    pass


def spaced(value):
    anywhere = pl.BlockSpec(memory_space=pl.ANY)
    return pl.pallas_call(
        spacer_kernel,
        out_shape=jax.ShapeDtypeStruct(value.shape, value.dtype),
        in_specs=[anywhere],
        out_specs=anywhere,
        input_output_aliases={0: 0},
        compiler_params=pltpu.CompilerParams(vmem_limit_bytes=1024 * 1024),
        cost_estimate=pl.CostEstimate(flops=1, bytes_accessed=1, transcendentals=0),
    )(value)


def pair_terms(integrals, vir_coeff, occ_energy, vir_energy, kappas):
    occ_count = integrals.shape[1]
    vir_local = vir_coeff.shape[1]
    wide_index = lax.axis_index("wide")
    batch_index = lax.axis_index("batch")
    place = jnp.stack(
        [wide_index, batch_index, jnp.full((), occ_count, wide_index.dtype)]
    ).astype(jnp.int32)
    vir_rows = vir_energy.reshape(-1, vir_local)
    def to_owner(columns):
        owned = lax.all_to_all(columns, "wide", split_axis=0, concat_axis=0, tiled=True)
        return owned.reshape(-1, owned.shape[2])

    def over_batch(value):
        return from_behind(value, "batch", 1)

    def over_cores(value):
        return swap_by(value, "wide", 1)

    def over_pairs(value):
        return swap_by(value, "wide", 2)

    def along(value):
        return hand_along(value, "wide")

    together = lax.optimization_barrier
    sends_near = ((wide_index ^ (wide_index >> 1)) & 1) == 0
    energies = jnp.concatenate([kappas, occ_energy])
    own, sends_near, vir_rows, place, energies = together(
        (
            to_owner(transform(integrals, vir_coeff)),
            sends_near,
            vir_rows,
            place,
            energies,
        )
    )

    def for_sibling(near, far):
        return over_cores(
            jnp.concatenate([jnp.where(sends_near, *pair) for pair in zip(near, far)], axis=1)
        )

    cut = vir_local // 2
    sibling = over_cores(own)
    low, high = cut_in_two(own)
    step = functools.partial(add_terms, place, energies, vir_rows, kappas.shape[0])

    own_o_high = over_batch(high)
    near_low = over_pairs(low)
    *made, density = step(
        None,
        [("own", 0, 0, low), ("own", 0, cut, high), ("sibling", 0, 0, sibling)],
        None,
        (2, 512),
    )
    step = functools.partial(step, made)

    low, high, density = together((low, high, density))
    own_o_low = over_batch(low)
    near_high = over_pairs(high)
    density = spaced(density)

    near_low, own_o_high, density = together((near_low, own_o_high, density))
    near_o_high = over_pairs(own_o_high)
    far_low = along(near_low)
    density = step([("own", 1, cut, own_o_high), ("near", 0, 0, near_low)], density, (8, 512))

    own_o_low, own_o_high, near_low, near_high, density = together(
        (own_o_low, own_o_high, near_low, near_high, density)
    )
    far_high = along(near_high)
    near_o_low = over_batch(near_low)
    sibling_o = over_cores(jnp.concatenate([own_o_low, own_o_high], axis=1))
    density = spaced(density)

    far_low, near_o_high, density = together((far_low, near_o_high, density))
    far_o_high = along(near_o_high)
    far_o_low = over_batch(far_low)
    density = step(
        [
            ("own", 1, 0, own_o_low),
            ("near", 0, cut, near_high),
            ("far", 0, 0, far_low),
            ("near", 1, cut, near_o_high),
        ],
        density,
        (2, 512),
    )

    far_low, far_high, near_o_low, density = together((far_low, far_high, near_o_low, density))
    third_low = for_sibling((near_low,), (far_low,))
    third_high = for_sibling((near_high,), (far_high,))
    density = step(
        [("near", 1, 0, near_o_low), ("far", 0, cut, far_high), ("sibling", 1, 0, sibling_o)],
        density,
        (2, 512),
    )

    far_o_low, far_o_high, density = together((far_o_low, far_o_high, density))
    third_o_low = for_sibling((near_o_low,), (far_o_low,))
    third_o_high = for_sibling((near_o_high,), (far_o_high,))
    return step(
        [
            ("third", 0, 0, third_low),
            ("third", 0, cut, third_high),
            ("far", 1, 0, far_o_low),
            ("far", 1, cut, far_o_high),
            ("third", 1, 0, third_o_low),
            ("third", 1, cut, third_o_high),
        ],
        density,
        (2, 512),
        last=True,
    )


def pair_density(own_slice, partner, own_energy, partner_energy, row_energy, vir_energy, kappas):
    coulomb = lax.dot_general(
        own_slice, partner, (((0,), (0,)), ((), ())), preferred_element_type=jnp.float32
    )
    denominator = row_energy[:, None] + vir_energy[None, :] - own_energy - partner_energy
    damping = 1.0 - jnp.exp(-kappas[:, None, None] * denominator[None])
    amplitude = (-coulomb[None] * (damping * damping) / denominator[None]).astype(jnp.bfloat16)
    flat = amplitude.reshape(-1, amplitude.shape[2])
    density = lax.dot_general(
        flat, partner, (((1,), (1,)), ((), ())), preferred_element_type=jnp.float32
    )
    return density.reshape(kappas.shape[0], own_slice.shape[1], partner.shape[0])


def ring_terms(integrals, vir_coeff, occ_energy, vir_energy, kappas):
    aux_local, occ_count, basis = integrals.shape
    vir_local = vir_coeff.shape[1]
    batch_index = lax.axis_index("batch")
    wide_index = lax.axis_index("wide")
    flat_ints = integrals.reshape(aux_local * occ_count, basis)
    row_energy = lax.dynamic_slice_in_dim(vir_energy, batch_index * vir_local, vir_local, 0)
    own_energy = lax.dynamic_slice_in_dim(occ_energy, wide_index, 1, 0)[0]

    def term(partner, offset, own_slice):
        partner_index = (wide_index + offset) % occ_count
        partner_energy = lax.dynamic_slice_in_dim(occ_energy, partner_index, 1, 0)[0]
        return pair_density(
            own_slice, partner, own_energy, partner_energy, row_energy, vir_energy, kappas
        )

    transformed = jnp.dot(flat_ints, vir_coeff, preferred_element_type=jnp.float32).astype(
        jnp.bfloat16
    )
    transformed = transformed.reshape(aux_local, occ_count, vir_local)
    own_slice = lax.all_to_all(transformed, "wide", split_axis=1, concat_axis=0, tiled=True)[
        :, 0, :
    ]
    own_full = lax.all_gather(own_slice, "batch", axis=1, tiled=True)
    density = term(own_full, 0, own_slice)
    upper = own_full
    lower = own_full
    for offset in range(1, HALF + 1):
        upper = from_behind(upper, "wide", -1)
        lower = from_behind(lower, "wide", 1)
        density = density + term(upper, offset, own_slice) + term(lower, -offset, own_slice)
    return density.astype(jnp.bfloat16)[:, None, :, :]


def solution(mesh):
    paired = mesh.shape["batch"] == 2 and mesh.shape["wide"] % 4 == 0

    return jax.shard_map(
        pair_terms if paired else ring_terms,
        mesh=mesh,
        in_specs=(P("wide", None, None), P(None, "batch"), P(), P(), P()),
        out_specs=P(None, "wide", "batch", None),
        check_vma=False,
    )
```

```python
import functools

import jax
import jax.numpy as jnp
from jax import lax
from jax.experimental import pallas as pl
from jax.experimental.pallas import tpu as pltpu
from jax.sharding import PartitionSpec as P

HALF = 2
TRANSFORM_STEPS = 3
VMEM_LIMIT = 18 * 1024 * 1024
LANES = 128


def from_behind(shard, axis, by):
    peers = lax.axis_size(axis)
    return lax.ppermute(shard, axis, [(i, (i + by) % peers) for i in range(peers)])


def swap_by(shard, axis, bit):
    peers = lax.axis_size(axis)
    return lax.ppermute(shard, axis, [(i, i ^ bit) for i in range(peers)])


def hand_along(shard, axis):
    peers = lax.axis_size(axis)
    return lax.ppermute(
        shard,
        axis,
        [(i, (i + (4 if i // 2 % 2 == 0 else -4)) % peers) for i in range(peers)],
    )


def transform_kernel(integrals, vir_coeff, out, held, coeff, turned, sems):
    occ_count, aux_local, vir_local = out.shape
    rows = aux_local // TRANSFORM_STEPS
    size = rows * occ_count

    def fetch(step):
        span = pl.ds(step * rows, rows)
        return pltpu.make_async_copy(integrals.at[span], held.at[span], sems.at[step])

    def send(step):
        return pltpu.make_async_copy(
            turned.at[step], out.at[:, pl.ds(step * rows, rows), :], sems.at[step]
        )

    fetch_coeff = pltpu.make_async_copy(vir_coeff, coeff, sems.at[TRANSFORM_STEPS])
    fetch_coeff.start()
    for step in range(TRANSFORM_STEPS):
        fetch(step).start()
    source = lax.broadcasted_iota(jnp.int32, (1, size), 1)
    to = lax.rem(source, occ_count) * rows + lax.div(source, occ_count)
    reorder = (lax.broadcasted_iota(jnp.int32, (size, size), 0) == to).astype(out.dtype)
    fetch_coeff.wait()
    for step in range(TRANSFORM_STEPS):
        fetch(step).wait()
        product = jnp.dot(
            held[step * rows:(step + 1) * rows].reshape(size, held.shape[2]),
            coeff[...],
            preferred_element_type=jnp.float32,
        ).astype(out.dtype)
        product = jnp.dot(reorder, product, preferred_element_type=jnp.float32)
        turned[step] = product.astype(out.dtype).reshape(occ_count, rows, vir_local)
        send(step).start()
    for step in range(TRANSFORM_STEPS):
        send(step).wait()


def transform(integrals, vir_coeff):
    aux_local, occ_count, basis = integrals.shape
    vir_local = vir_coeff.shape[1]
    hbm = pl.BlockSpec(memory_space=pl.ANY)
    rows = aux_local // TRANSFORM_STEPS
    return pl.pallas_call(
        transform_kernel,
        out_shape=jax.ShapeDtypeStruct((occ_count, aux_local, vir_local), integrals.dtype),
        in_specs=[hbm, hbm],
        out_specs=hbm,
        scratch_shapes=[
            pltpu.VMEM((aux_local, occ_count, basis), integrals.dtype),
            pltpu.VMEM((basis, vir_local), integrals.dtype),
            pltpu.VMEM((TRANSFORM_STEPS, occ_count, rows, vir_local), integrals.dtype),
            pltpu.SemaphoreType.DMA((TRANSFORM_STEPS + 1,)),
        ],
        compiler_params=pltpu.CompilerParams(vmem_limit_bytes=60 * 1024 * 1024),
        cost_estimate=pl.CostEstimate(flops=1, bytes_accessed=1, transcendentals=0),
    )(integrals, vir_coeff)


def cut_kernel(own, low, high):
    cut = low.shape[1]
    low[...] = own[:, :cut]
    high[...] = own[:, cut:]


def cut_in_two(own):
    vmem = pl.BlockSpec(memory_space=pltpu.VMEM)
    half = jax.ShapeDtypeStruct((own.shape[0], own.shape[1] // 2), own.dtype)
    return pl.pallas_call(
        cut_kernel,
        out_shape=(half, half),
        in_specs=[vmem],
        out_specs=(vmem, vmem),
        compiler_params=pltpu.CompilerParams(vmem_limit_bytes=VMEM_LIMIT),
        cost_estimate=pl.CostEstimate(flops=1, bytes_accessed=1, transcendentals=0),
    )(own)


def make_factors(place, kappa, occ, vir_rows, own_low, own_high, own_t, row_energies, row_factors):
    rows = own_t.shape[0]
    row_energy = vir_rows[pl.ds(place[1], 1), :] - occ(place[0])

    def down_columns(row):
        return jnp.transpose(jnp.broadcast_to(row, (LANES, rows)))

    own_t[:rows // 2, :] = jnp.transpose(own_low[...])
    own_t[rows // 2:, :] = jnp.transpose(own_high[...])
    row_energies[...] = down_columns(row_energy)
    for q in range(row_factors.shape[0]):
        row_factors[q] = down_columns(jnp.exp(-kappa(q) * row_energy))


def terms_kernel(pieces, mode, shape, place, energies, vir_rows, *refs):
    group_size, p_tile, turn = shape
    if turn:
        *refs, turned = refs
    if mode == "first":
        partners = refs[:len(pieces)]
        own_t, row_energies, row_factors, out, amp, ratio = refs[len(pieces):]
    else:
        own_t, row_energies, row_factors = refs[:3]
        partners = refs[3:3 + len(pieces)]
        partial, *refs = refs[3 + len(pieces):]
        if mode == "last":
            result, amp, ratio, out, sems = refs
        else:
            out, amp, ratio = refs
    nkap, rows = row_factors.shape[0], row_factors.shape[1]
    naux = own_t.shape[1]
    orbital, half, count = place[0], place[1], place[2]

    def kappa(q):
        return energies[q]

    def occ(index):
        return energies[nkap + index]

    if mode == "first":
        make_factors(
            place, kappa, occ, vir_rows, partners[0], partners[1], own_t, row_energies, row_factors
        )
    core_sign = 1 - 2 * lax.rem(orbital, 2)
    pair_sign = 1 - 2 * lax.rem(lax.div(orbital, 2), 2)
    offsets = dict(
        own=0, sibling=core_sign, third=-core_sign, near=HALF * pair_sign, far=-HALF * pair_sign
    )

    column_energies = []
    for (name, other, start), partner in zip(pieces, partners):
        index = lax.rem(orbital + offsets[name] + count, count)
        column_half = lax.rem(half + other, 2)
        energy = vir_rows[pl.ds(column_half, 1), :] - occ(index)
        for c in range(start, start + partner.shape[1], LANES):
            column_energies.append(energy[:, c:c + LANES])
    width = LANES * len(column_energies)

    def partner_columns(tile):
        return jnp.concatenate([partner[tile, :] for partner in partners], axis=1)

    for at in range(0, width, 2 * LANES):
        columns = partner_columns(slice(None))[:, at:at + 2 * LANES]
        coulomb = jnp.dot(own_t[...], columns, preferred_element_type=jnp.float32)
        for c in range(0, columns.shape[1], LANES):
            energy = column_energies[(at + c) // LANES]
            ratio[:, at + c:at + c + LANES] = -coulomb[:, c:c + LANES] / (
                row_energies[...] + energy
            )

    if turn:
        at = 0
        for partner in partners:
            turned[at:at + partner.shape[1], :] = jnp.transpose(partner[...])
            at += partner.shape[1]

    copies = []
    for group in range(0, nkap, group_size):
        top, bottom = group * rows, (group + group_size) * rows
        for q in range(group, group + group_size):
            for position, energy in enumerate(column_energies):
                columns = slice(position * LANES, (position + 1) * LANES)
                damping = 1.0 - row_factors[q] * jnp.exp(-kappa(q) * energy)
                amp[q * rows:(q + 1) * rows, columns] = (
                    ratio[:, columns] * damping * damping
                ).astype(amp.dtype)
        span = slice(group, group + group_size)
        for start in range(0, naux, p_tile):
            tile = slice(start, start + p_tile)
            value = lax.dot_general(
                amp[top:bottom, :],
                turned[:, tile] if turn else partner_columns(tile),
                (((1,), (0 if turn else 1,)), ((), ())),
                preferred_element_type=jnp.float32,
            ).reshape(group_size, rows, p_tile)
            if mode != "first":
                value = value + partial[span, :, tile]
            out[span, :, tile] = value.astype(out.dtype)
        if mode == "last":
            copy = pltpu.make_async_copy(
                out.at[span], result.at[span, 0], sems.at[group // group_size]
            )
            copy.start()
            copies.append(copy)
    for copy in copies:
        copy.wait()


def add_terms(place, energies, vir_rows, nkap, made, partners, partial, shape, last=False):
    pieces = tuple(partner[:3] for partner in partners)
    arrays = [partner[3] for partner in partners]
    naux = arrays[0].shape[0]
    rows = vir_rows.shape[1]
    width = sum(array.shape[1] for array in arrays)
    vmem = pl.BlockSpec(memory_space=pltpu.VMEM)
    smem = pl.BlockSpec(memory_space=pltpu.SMEM)
    density = jax.ShapeDtypeStruct((nkap, rows, naux), jnp.float32)
    scratch = [
        pltpu.VMEM((nkap * rows, width), jnp.bfloat16),
        pltpu.VMEM((rows, width), jnp.float32),
    ]
    aliases = {}
    if made is None:
        mode = "first"
        operands = [place, energies, vir_rows] + arrays
        out_shape = (
            jax.ShapeDtypeStruct((rows, naux), arrays[0].dtype),
            jax.ShapeDtypeStruct((rows, LANES), jnp.float32),
            jax.ShapeDtypeStruct((nkap, rows, LANES), jnp.float32),
            density,
        )
        out_specs = (vmem,) * 4
    else:
        mode = "last" if last else "middle"
        operands = [place, energies, vir_rows] + list(made) + arrays + [partial]
        if last:
            out_shape = jax.ShapeDtypeStruct((nkap, 1, rows, naux), jnp.bfloat16)
            out_specs = pl.BlockSpec(memory_space=pl.ANY)
            scratch.append(pltpu.VMEM((nkap, rows, naux), jnp.bfloat16))
            scratch.append(pltpu.SemaphoreType.DMA((nkap // shape[0],)))
        else:
            out_shape, out_specs = density, vmem
            aliases = {len(operands) - 1: 0}
    if shape[2]:
        scratch.append(pltpu.VMEM((width, naux), jnp.bfloat16))
    return pl.pallas_call(
        functools.partial(terms_kernel, pieces, mode, shape),
        out_shape=out_shape,
        input_output_aliases=aliases,
        in_specs=[smem, smem] + [vmem] * (len(operands) - 2),
        out_specs=out_specs,
        scratch_shapes=scratch,
        compiler_params=pltpu.CompilerParams(vmem_limit_bytes=VMEM_LIMIT),
        cost_estimate=pl.CostEstimate(flops=1, bytes_accessed=1, transcendentals=0),
    )(*operands)


def pair_terms(integrals, vir_coeff, occ_energy, vir_energy, kappas):
    occ_count = integrals.shape[1]
    vir_local = vir_coeff.shape[1]
    wide_index = lax.axis_index("wide")
    batch_index = lax.axis_index("batch")
    place = jnp.stack(
        [wide_index, batch_index, jnp.full((), occ_count, wide_index.dtype)]
    ).astype(jnp.int32)
    vir_rows = vir_energy.reshape(-1, vir_local)
    def to_owner(columns):
        owned = lax.all_to_all(columns, "wide", split_axis=0, concat_axis=0, tiled=True)
        return owned.reshape(-1, owned.shape[2])

    def over_batch(value):
        return from_behind(value, "batch", 1)

    def over_cores(value):
        return swap_by(value, "wide", 1)

    def over_pairs(value):
        return swap_by(value, "wide", 2)

    def along(value):
        return hand_along(value, "wide")

    together = lax.optimization_barrier
    sends_near = ((wide_index ^ (wide_index >> 1)) & 1) == 0
    energies = jnp.concatenate([kappas, occ_energy])
    own, sends_near, vir_rows, place, energies = together(
        (
            to_owner(transform(integrals, vir_coeff)),
            sends_near,
            vir_rows,
            place,
            energies,
        )
    )

    def for_sibling(near, far):
        return over_cores(
            jnp.concatenate([jnp.where(sends_near, *pair) for pair in zip(near, far)], axis=1)
        )

    cut = vir_local // 2
    sibling = over_cores(own)
    low, high = cut_in_two(own)
    step = functools.partial(add_terms, place, energies, vir_rows, kappas.shape[0])

    own_o_high = over_batch(high)
    near_low = over_pairs(low)
    *made, density = step(None, [("own", 0, 0, low), ("own", 0, cut, high)], None, (8, 512, False))
    step = functools.partial(step, made)

    low, high, density = together((low, high, density))
    own_o_low = over_batch(low)
    near_high = over_pairs(high)
    density = step([("sibling", 0, 0, sibling)], density, (2, 512, True))

    near_low, own_o_high, density = together((near_low, own_o_high, density))
    near_o_high = over_pairs(own_o_high)
    far_low = along(near_low)
    density = step(
        [("own", 1, cut, own_o_high), ("near", 0, 0, near_low)], density, (8, 512, True)
    )

    own_o_low, own_o_high, near_low, near_high, density = together(
        (own_o_low, own_o_high, near_low, near_high, density)
    )
    far_high = along(near_high)
    near_o_low = over_batch(near_low)
    sibling_o = over_cores(jnp.concatenate([own_o_low, own_o_high], axis=1))
    density = step([("own", 1, 0, own_o_low), ("near", 0, cut, near_high)], density, (8, 512, False))

    near_o_high, far_low, density = together((near_o_high, far_low, density))
    far_o_high = along(near_o_high)
    far_o_low = over_batch(far_low)
    density = step(
        [("far", 0, 0, far_low), ("near", 1, cut, near_o_high)], density, (2, 1536, True)
    )

    far_low, far_high, near_o_low, density = together((far_low, far_high, near_o_low, density))
    third_low = for_sibling((near_low,), (far_low,))
    third_high = for_sibling((near_high,), (far_high,))
    density = step(
        [("near", 1, 0, near_o_low), ("far", 0, cut, far_high), ("sibling", 1, 0, sibling_o)],
        density,
        (2, 512, True),
    )

    far_o_low, far_o_high, density = together((far_o_low, far_o_high, density))
    third_o_low = for_sibling((near_o_low,), (far_o_low,))
    third_o_high = for_sibling((near_o_high,), (far_o_high,))
    return step(
        [
            ("third", 0, 0, third_low),
            ("third", 0, cut, third_high),
            ("far", 1, 0, far_o_low),
            ("far", 1, cut, far_o_high),
            ("third", 1, 0, third_o_low),
            ("third", 1, cut, third_o_high),
        ],
        density,
        (2, 512, False),
        last=True,
    )


def pair_density(own_slice, partner, own_energy, partner_energy, row_energy, vir_energy, kappas):
    coulomb = lax.dot_general(
        own_slice, partner, (((0,), (0,)), ((), ())), preferred_element_type=jnp.float32
    )
    denominator = row_energy[:, None] + vir_energy[None, :] - own_energy - partner_energy
    damping = 1.0 - jnp.exp(-kappas[:, None, None] * denominator[None])
    amplitude = (-coulomb[None] * (damping * damping) / denominator[None]).astype(jnp.bfloat16)
    flat = amplitude.reshape(-1, amplitude.shape[2])
    density = lax.dot_general(
        flat, partner, (((1,), (1,)), ((), ())), preferred_element_type=jnp.float32
    )
    return density.reshape(kappas.shape[0], own_slice.shape[1], partner.shape[0])


def ring_terms(integrals, vir_coeff, occ_energy, vir_energy, kappas):
    aux_local, occ_count, basis = integrals.shape
    vir_local = vir_coeff.shape[1]
    batch_index = lax.axis_index("batch")
    wide_index = lax.axis_index("wide")
    flat_ints = integrals.reshape(aux_local * occ_count, basis)
    row_energy = lax.dynamic_slice_in_dim(vir_energy, batch_index * vir_local, vir_local, 0)
    own_energy = lax.dynamic_slice_in_dim(occ_energy, wide_index, 1, 0)[0]

    def term(partner, offset, own_slice):
        partner_index = (wide_index + offset) % occ_count
        partner_energy = lax.dynamic_slice_in_dim(occ_energy, partner_index, 1, 0)[0]
        return pair_density(
            own_slice, partner, own_energy, partner_energy, row_energy, vir_energy, kappas
        )

    transformed = jnp.dot(flat_ints, vir_coeff, preferred_element_type=jnp.float32).astype(
        jnp.bfloat16
    )
    transformed = transformed.reshape(aux_local, occ_count, vir_local)
    own_slice = lax.all_to_all(transformed, "wide", split_axis=1, concat_axis=0, tiled=True)[
        :, 0, :
    ]
    own_full = lax.all_gather(own_slice, "batch", axis=1, tiled=True)
    density = term(own_full, 0, own_slice)
    upper = own_full
    lower = own_full
    for offset in range(1, HALF + 1):
        upper = from_behind(upper, "wide", -1)
        lower = from_behind(lower, "wide", 1)
        density = density + term(upper, offset, own_slice) + term(lower, -offset, own_slice)
    return density.astype(jnp.bfloat16)[:, None, :, :]


def solution(mesh):
    paired = mesh.shape["batch"] == 2 and mesh.shape["wide"] % 4 == 0

    return jax.shard_map(
        pair_terms if paired else ring_terms,
        mesh=mesh,
        in_specs=(P("wide", None, None), P(None, "batch"), P(), P(), P()),
        out_specs=P(None, "wide", "batch", None),
        check_vma=False,
    )
```

```python
import functools

import jax
import jax.numpy as jnp
from jax import lax
from jax.experimental import pallas as pl
from jax.experimental.pallas import tpu as pltpu
from jax.sharding import PartitionSpec as P

HALF = 2
TRANSFORM_STEPS = 6
PARTNERS = ("own", "sibling", "third", "near", "far")
VMEM_LIMIT = 18 * 1024 * 1024
LANES = 128


def from_behind(shard, axis, by):
    peers = lax.axis_size(axis)
    return lax.ppermute(shard, axis, [(i, (i + by) % peers) for i in range(peers)])


def swap_by(shard, axis, bit):
    peers = lax.axis_size(axis)
    return lax.ppermute(shard, axis, [(i, i ^ bit) for i in range(peers)])


def hand_along(shard, axis):
    peers = lax.axis_size(axis)
    return lax.ppermute(
        shard,
        axis,
        [(i, (i + (4 if i // 2 % 2 == 0 else -4)) % peers) for i in range(peers)],
    )


def transform_kernel(integrals, vir_coeff, out, held, coeff, turned, sems):
    occ_count, aux_local, vir_local = out.shape
    rows = aux_local // TRANSFORM_STEPS
    size = rows * occ_count

    def fetch(step):
        span = pl.ds(step * rows, rows)
        return pltpu.make_async_copy(integrals.at[span], held.at[span], sems.at[step])

    def send(step):
        return pltpu.make_async_copy(
            turned.at[step], out.at[:, pl.ds(step * rows, rows), :], sems.at[step]
        )

    fetch_coeff = pltpu.make_async_copy(vir_coeff, coeff, sems.at[TRANSFORM_STEPS])
    fetch_coeff.start()
    for step in range(TRANSFORM_STEPS):
        fetch(step).start()
    source = lax.broadcasted_iota(jnp.int32, (1, size), 1)
    to = lax.rem(source, occ_count) * rows + lax.div(source, occ_count)
    reorder = (lax.broadcasted_iota(jnp.int32, (size, size), 0) == to).astype(out.dtype)
    fetch_coeff.wait()
    for step in range(TRANSFORM_STEPS):
        fetch(step).wait()
        product = jnp.dot(
            held[step * rows:(step + 1) * rows].reshape(size, held.shape[2]),
            coeff[...],
            preferred_element_type=jnp.float32,
        ).astype(out.dtype)
        product = jnp.dot(reorder, product, preferred_element_type=jnp.float32)
        turned[step] = product.astype(out.dtype).reshape(occ_count, rows, vir_local)
        send(step).start()
    for step in range(TRANSFORM_STEPS):
        send(step).wait()


def transform(integrals, vir_coeff):
    aux_local, occ_count, basis = integrals.shape
    vir_local = vir_coeff.shape[1]
    hbm = pl.BlockSpec(memory_space=pl.ANY)
    rows = aux_local // TRANSFORM_STEPS
    return pl.pallas_call(
        transform_kernel,
        out_shape=jax.ShapeDtypeStruct((occ_count, aux_local, vir_local), integrals.dtype),
        in_specs=[hbm, hbm],
        out_specs=hbm,
        scratch_shapes=[
            pltpu.VMEM((aux_local, occ_count, basis), integrals.dtype),
            pltpu.VMEM((basis, vir_local), integrals.dtype),
            pltpu.VMEM((TRANSFORM_STEPS, occ_count, rows, vir_local), integrals.dtype),
            pltpu.SemaphoreType.DMA((TRANSFORM_STEPS + 1,)),
        ],
        compiler_params=pltpu.CompilerParams(vmem_limit_bytes=60 * 1024 * 1024),
        cost_estimate=pl.CostEstimate(flops=1, bytes_accessed=1, transcendentals=0),
    )(integrals, vir_coeff)


def cut_kernel(own, low, high):
    cut = low.shape[1]
    low[...] = own[:, :cut]
    high[...] = own[:, cut:]


def cut_in_two(own):
    vmem = pl.BlockSpec(memory_space=pltpu.VMEM)
    half = jax.ShapeDtypeStruct((own.shape[0], own.shape[1] // 2), own.dtype)
    return pl.pallas_call(
        cut_kernel,
        out_shape=(half, half),
        in_specs=[vmem],
        out_specs=(vmem, vmem),
        compiler_params=pltpu.CompilerParams(vmem_limit_bytes=VMEM_LIMIT),
        cost_estimate=pl.CostEstimate(flops=1, bytes_accessed=1, transcendentals=0),
    )(own)


def make_tables(place, energies, vir_rows, own_low, own_high, made):
    own_t, row_energies, row_factors, column_energies, column_factors = made
    nkap, rows = row_factors.shape[0], own_t.shape[0]
    orbital, half, count = place[0], place[1], place[2]
    core_sign = 1 - 2 * lax.rem(orbital, 2)
    pair_sign = 1 - 2 * lax.rem(lax.div(orbital, 2), 2)
    offsets = dict(
        own=0, sibling=core_sign, third=-core_sign, near=HALF * pair_sign, far=-HALF * pair_sign
    )

    def down_columns(row):
        return jnp.transpose(jnp.broadcast_to(row, (LANES, rows)))

    own_t[:rows // 2, :] = jnp.transpose(own_low[...])
    own_t[rows // 2:, :] = jnp.transpose(own_high[...])
    row_energy = vir_rows[pl.ds(half, 1), :] - energies[nkap + orbital]
    row_energies[...] = down_columns(row_energy)
    for q in range(nkap):
        row_factors[q] = down_columns(jnp.exp(-energies[q] * row_energy))
    for row, name in enumerate(PARTNERS):
        index = lax.rem(orbital + offsets[name] + count, count)
        for other in range(2):
            energy = vir_rows[pl.ds(lax.rem(half + other, 2), 1), :] - energies[nkap + index]
            at = slice(2 * row + other, 2 * row + other + 1)
            column_energies[at, :] = energy
            for q in range(nkap):
                column_factors[q, at, :] = jnp.exp(-energies[q] * energy)


def terms_kernel(pieces, mode, shape, *refs):
    if mode == "first":
        place, energies, vir_rows = refs[:3]
        partners = refs[3:3 + len(pieces)]
        *made, out, amp, ratio = refs[3 + len(pieces):]
        make_tables(place, energies, vir_rows, partners[0], partners[1], made)
    else:
        made = refs[:5]
        partners = refs[5:5 + len(pieces)]
        partial, *refs = refs[5 + len(pieces):]
        if mode == "last":
            result, amp, ratio, out, sems = refs
        else:
            out, amp, ratio = refs
    own_t, row_energies, row_factors, column_energies, column_factors = made
    group_size, p_tile = shape
    nkap, rows = row_factors.shape[0], row_factors.shape[1]
    naux = own_t.shape[1]

    columns_at = []
    for (name, other, start), partner in zip(pieces, partners):
        row = 2 * PARTNERS.index(name) + other
        for c in range(start, start + partner.shape[1], LANES):
            columns_at.append((slice(row, row + 1), slice(c, c + LANES)))
    width = LANES * len(columns_at)

    def partner_columns(tile):
        return jnp.concatenate([partner[tile, :] for partner in partners], axis=1)

    for at in range(0, width, 2 * LANES):
        columns = partner_columns(slice(None))[:, at:at + 2 * LANES]
        coulomb = jnp.dot(own_t[...], columns, preferred_element_type=jnp.float32)
        for c in range(0, columns.shape[1], LANES):
            ratio[:, at + c:at + c + LANES] = -coulomb[:, c:c + LANES] / (
                row_energies[...] + column_energies[columns_at[(at + c) // LANES]]
            )

    copies = []
    for group in range(0, nkap, group_size):
        top, bottom = group * rows, (group + group_size) * rows
        for q in range(group, group + group_size):
            for position, (row, lanes) in enumerate(columns_at):
                columns = slice(position * LANES, (position + 1) * LANES)
                damping = 1.0 - row_factors[q] * column_factors[q, row, lanes]
                amp[q * rows:(q + 1) * rows, columns] = (
                    ratio[:, columns] * damping * damping
                ).astype(amp.dtype)
        span = slice(group, group + group_size)
        for start in range(0, naux, p_tile):
            tile = slice(start, start + p_tile)
            value = lax.dot_general(
                amp[top:bottom, :],
                partner_columns(tile),
                (((1,), (1,)), ((), ())),
                preferred_element_type=jnp.float32,
            ).reshape(group_size, rows, p_tile)
            if mode != "first":
                value = value + partial[span, :, tile]
            out[span, :, tile] = value.astype(out.dtype)
        if mode == "last":
            copy = pltpu.make_async_copy(
                out.at[span], result.at[span, 0], sems.at[group // group_size]
            )
            copy.start()
            copies.append(copy)
    for copy in copies:
        copy.wait()


def add_terms(place, energies, vir_rows, nkap, made, partners, partial, shape, last=False):
    pieces = tuple(partner[:3] for partner in partners)
    arrays = [partner[3] for partner in partners]
    naux = arrays[0].shape[0]
    rows = vir_rows.shape[1]
    width = sum(array.shape[1] for array in arrays)
    vmem = pl.BlockSpec(memory_space=pltpu.VMEM)
    smem = pl.BlockSpec(memory_space=pltpu.SMEM)
    density = jax.ShapeDtypeStruct((nkap, rows, naux), jnp.float32)
    scratch = [
        pltpu.VMEM((nkap * rows, width), jnp.bfloat16),
        pltpu.VMEM((rows, width), jnp.float32),
    ]
    aliases = {}
    if made is None:
        mode = "first"
        operands = [place, energies, vir_rows] + arrays
        in_specs = [smem, smem] + [vmem] * (1 + len(arrays))
        out_shape = (
            jax.ShapeDtypeStruct((rows, naux), arrays[0].dtype),
            jax.ShapeDtypeStruct((rows, LANES), jnp.float32),
            jax.ShapeDtypeStruct((nkap, rows, LANES), jnp.float32),
            jax.ShapeDtypeStruct((2 * len(PARTNERS), rows), jnp.float32),
            jax.ShapeDtypeStruct((nkap, 2 * len(PARTNERS), rows), jnp.float32),
            density,
        )
        out_specs = (vmem,) * 6
    else:
        mode = "last" if last else "middle"
        operands = list(made) + arrays + [partial]
        in_specs = [vmem] * len(operands)
        if last:
            out_shape = jax.ShapeDtypeStruct((nkap, 1, rows, naux), jnp.bfloat16)
            out_specs = pl.BlockSpec(memory_space=pl.ANY)
            scratch.append(pltpu.VMEM((nkap, rows, naux), jnp.bfloat16))
            scratch.append(pltpu.SemaphoreType.DMA((nkap // shape[0],)))
        else:
            out_shape, out_specs = density, vmem
            aliases = {len(operands) - 1: 0}
    return pl.pallas_call(
        functools.partial(terms_kernel, pieces, mode, shape),
        out_shape=out_shape,
        input_output_aliases=aliases,
        in_specs=in_specs,
        out_specs=out_specs,
        scratch_shapes=scratch,
        compiler_params=pltpu.CompilerParams(vmem_limit_bytes=VMEM_LIMIT),
        cost_estimate=pl.CostEstimate(flops=1, bytes_accessed=1, transcendentals=0),
    )(*operands)


def pair_terms(integrals, vir_coeff, occ_energy, vir_energy, kappas):
    occ_count = integrals.shape[1]
    vir_local = vir_coeff.shape[1]
    wide_index = lax.axis_index("wide")
    batch_index = lax.axis_index("batch")
    place = jnp.stack(
        [wide_index, batch_index, jnp.full((), occ_count, wide_index.dtype)]
    ).astype(jnp.int32)
    vir_rows = vir_energy.reshape(-1, vir_local)
    def to_owner(columns):
        owned = lax.all_to_all(columns, "wide", split_axis=0, concat_axis=0, tiled=True)
        return owned.reshape(-1, owned.shape[2])

    def over_batch(value):
        return from_behind(value, "batch", 1)

    def over_cores(value):
        return swap_by(value, "wide", 1)

    def over_pairs(value):
        return swap_by(value, "wide", 2)

    def along(value):
        return hand_along(value, "wide")

    together = lax.optimization_barrier
    sends_near = ((wide_index ^ (wide_index >> 1)) & 1) == 0
    energies = jnp.concatenate([kappas, occ_energy])
    own, sends_near, vir_rows, place, energies = together(
        (
            to_owner(transform(integrals, vir_coeff)),
            sends_near,
            vir_rows,
            place,
            energies,
        )
    )

    def for_sibling(near, far):
        return over_cores(
            jnp.concatenate([jnp.where(sends_near, *pair) for pair in zip(near, far)], axis=1)
        )

    cut = vir_local // 2
    sibling = over_cores(own)
    low, high = cut_in_two(own)
    step = functools.partial(add_terms, place, energies, vir_rows, kappas.shape[0])

    own_o_high = over_batch(high)
    near_low = over_pairs(low)
    *made, density = step(None, [("own", 0, 0, low), ("own", 0, cut, high)], None, (8, 512))
    step = functools.partial(step, made)

    low, high, density = together((low, high, density))
    own_o_low = over_batch(low)
    near_high = over_pairs(high)
    density = step([("sibling", 0, 0, sibling)], density, (8, 512))

    near_low, own_o_high, density = together((near_low, own_o_high, density))
    near_o_high = over_pairs(own_o_high)
    far_low = along(near_low)
    density = step([("own", 1, cut, own_o_high), ("near", 0, 0, near_low)], density, (8, 512))

    own_o_low, own_o_high, near_low, near_high, density = together(
        (own_o_low, own_o_high, near_low, near_high, density)
    )
    far_high = along(near_high)
    near_o_low = over_batch(near_low)
    sibling_o = over_cores(jnp.concatenate([own_o_low, own_o_high], axis=1))
    density = step([("own", 1, 0, own_o_low), ("near", 0, cut, near_high)], density, (8, 512))

    near_o_high, far_low, density = together((near_o_high, far_low, density))
    far_o_high = along(near_o_high)
    far_o_low = over_batch(far_low)
    density = step([("far", 0, 0, far_low), ("near", 1, cut, near_o_high)], density, (8, 512))

    far_low, far_high, near_o_low, density = together((far_low, far_high, near_o_low, density))
    third_low = for_sibling((near_low,), (far_low,))
    third_high = for_sibling((near_high,), (far_high,))
    density = step(
        [("near", 1, 0, near_o_low), ("far", 0, cut, far_high), ("sibling", 1, 0, sibling_o)],
        density,
        (2, 512),
    )

    far_o_low, far_o_high, density = together((far_o_low, far_o_high, density))
    third_o_low = for_sibling((near_o_low,), (far_o_low,))
    third_o_high = for_sibling((near_o_high,), (far_o_high,))
    return step(
        [
            ("third", 0, 0, third_low),
            ("third", 0, cut, third_high),
            ("far", 1, 0, far_o_low),
            ("far", 1, cut, far_o_high),
            ("third", 1, 0, third_o_low),
            ("third", 1, cut, third_o_high),
        ],
        density,
        (2, 512),
        last=True,
    )


def pair_density(own_slice, partner, own_energy, partner_energy, row_energy, vir_energy, kappas):
    coulomb = lax.dot_general(
        own_slice, partner, (((0,), (0,)), ((), ())), preferred_element_type=jnp.float32
    )
    denominator = row_energy[:, None] + vir_energy[None, :] - own_energy - partner_energy
    damping = 1.0 - jnp.exp(-kappas[:, None, None] * denominator[None])
    amplitude = (-coulomb[None] * (damping * damping) / denominator[None]).astype(jnp.bfloat16)
    flat = amplitude.reshape(-1, amplitude.shape[2])
    density = lax.dot_general(
        flat, partner, (((1,), (1,)), ((), ())), preferred_element_type=jnp.float32
    )
    return density.reshape(kappas.shape[0], own_slice.shape[1], partner.shape[0])


def ring_terms(integrals, vir_coeff, occ_energy, vir_energy, kappas):
    aux_local, occ_count, basis = integrals.shape
    vir_local = vir_coeff.shape[1]
    batch_index = lax.axis_index("batch")
    wide_index = lax.axis_index("wide")
    flat_ints = integrals.reshape(aux_local * occ_count, basis)
    row_energy = lax.dynamic_slice_in_dim(vir_energy, batch_index * vir_local, vir_local, 0)
    own_energy = lax.dynamic_slice_in_dim(occ_energy, wide_index, 1, 0)[0]

    def term(partner, offset, own_slice):
        partner_index = (wide_index + offset) % occ_count
        partner_energy = lax.dynamic_slice_in_dim(occ_energy, partner_index, 1, 0)[0]
        return pair_density(
            own_slice, partner, own_energy, partner_energy, row_energy, vir_energy, kappas
        )

    transformed = jnp.dot(flat_ints, vir_coeff, preferred_element_type=jnp.float32).astype(
        jnp.bfloat16
    )
    transformed = transformed.reshape(aux_local, occ_count, vir_local)
    own_slice = lax.all_to_all(transformed, "wide", split_axis=1, concat_axis=0, tiled=True)[
        :, 0, :
    ]
    own_full = lax.all_gather(own_slice, "batch", axis=1, tiled=True)
    density = term(own_full, 0, own_slice)
    upper = own_full
    lower = own_full
    for offset in range(1, HALF + 1):
        upper = from_behind(upper, "wide", -1)
        lower = from_behind(lower, "wide", 1)
        density = density + term(upper, offset, own_slice) + term(lower, -offset, own_slice)
    return density.astype(jnp.bfloat16)[:, None, :, :]


def solution(mesh):
    paired = mesh.shape["batch"] == 2 and mesh.shape["wide"] % 4 == 0

    return jax.shard_map(
        pair_terms if paired else ring_terms,
        mesh=mesh,
        in_specs=(P("wide", None, None), P(None, "batch"), P(), P(), P()),
        out_specs=P(None, "wide", "batch", None),
        check_vma=False,
    )
```

```python
import functools

import jax
import jax.numpy as jnp
from jax import lax
from jax.experimental import pallas as pl
from jax.experimental.pallas import tpu as pltpu
from jax.sharding import PartitionSpec as P

HALF = 2
PARTNERS = ("own", "sibling", "third", "near", "far")
VMEM_LIMIT = 18 * 1024 * 1024
LANES = 128


def from_behind(shard, axis, by):
    peers = lax.axis_size(axis)
    return lax.ppermute(shard, axis, [(i, (i + by) % peers) for i in range(peers)])


def swap_by(shard, axis, bit):
    peers = lax.axis_size(axis)
    return lax.ppermute(shard, axis, [(i, i ^ bit) for i in range(peers)])


def hand_along(shard, axis):
    peers = lax.axis_size(axis)
    return lax.ppermute(
        shard,
        axis,
        [(i, (i + (4 if i // 2 % 2 == 0 else -4)) % peers) for i in range(peers)],
    )


def cut_kernel(own, low, high):
    cut = low.shape[1]
    low[...] = own[:, :cut]
    high[...] = own[:, cut:]


def cut_in_two(own):
    vmem = pl.BlockSpec(memory_space=pltpu.VMEM)
    half = jax.ShapeDtypeStruct((own.shape[0], own.shape[1] // 2), own.dtype)
    return pl.pallas_call(
        cut_kernel,
        out_shape=(half, half),
        in_specs=[vmem],
        out_specs=(vmem, vmem),
        compiler_params=pltpu.CompilerParams(vmem_limit_bytes=VMEM_LIMIT),
        cost_estimate=pl.CostEstimate(flops=1, bytes_accessed=1, transcendentals=0),
    )(own)


def make_tables(place, energies, vir_rows, own_low, own_high, made):
    own_t, row_energies, row_factors, column_energies, column_factors = made
    nkap, rows = row_factors.shape[0], own_t.shape[0]
    orbital, half, count = place[0], place[1], place[2]
    core_sign = 1 - 2 * lax.rem(orbital, 2)
    pair_sign = 1 - 2 * lax.rem(lax.div(orbital, 2), 2)
    offsets = dict(
        own=0, sibling=core_sign, third=-core_sign, near=HALF * pair_sign, far=-HALF * pair_sign
    )

    def down_columns(row):
        return jnp.transpose(jnp.broadcast_to(row, (LANES, rows)))

    own_t[:rows // 2, :] = jnp.transpose(own_low[...])
    own_t[rows // 2:, :] = jnp.transpose(own_high[...])
    row_energy = vir_rows[pl.ds(half, 1), :] - energies[nkap + orbital]
    row_energies[...] = down_columns(row_energy)
    for q in range(nkap):
        row_factors[q] = down_columns(jnp.exp(-energies[q] * row_energy))
    for row, name in enumerate(PARTNERS):
        index = lax.rem(orbital + offsets[name] + count, count)
        for other in range(2):
            energy = vir_rows[pl.ds(lax.rem(half + other, 2), 1), :] - energies[nkap + index]
            at = slice(2 * row + other, 2 * row + other + 1)
            column_energies[at, :] = energy
            for q in range(nkap):
                column_factors[q, at, :] = jnp.exp(-energies[q] * energy)


def terms_kernel(pieces, mode, shape, *refs):
    if mode == "first":
        place, energies, vir_rows = refs[:3]
        partners = refs[3:3 + len(pieces)]
        *made, out, amp, ratio = refs[3 + len(pieces):]
        make_tables(place, energies, vir_rows, partners[0], partners[1], made)
    else:
        made = refs[:5]
        partners = refs[5:5 + len(pieces)]
        partial, *refs = refs[5 + len(pieces):]
        if mode == "last":
            result, amp, ratio, out, sems = refs
        else:
            out, amp, ratio = refs
    own_t, row_energies, row_factors, column_energies, column_factors = made
    group_size, p_tile = shape
    nkap, rows = row_factors.shape[0], row_factors.shape[1]
    naux = own_t.shape[1]

    columns_at = []
    for (name, other, start), partner in zip(pieces, partners):
        row = 2 * PARTNERS.index(name) + other
        for c in range(start, start + partner.shape[1], LANES):
            columns_at.append((slice(row, row + 1), slice(c, c + LANES)))
    width = LANES * len(columns_at)

    def partner_columns(tile):
        return jnp.concatenate([partner[tile, :] for partner in partners], axis=1)

    for at in range(0, width, 2 * LANES):
        columns = partner_columns(slice(None))[:, at:at + 2 * LANES]
        coulomb = jnp.dot(own_t[...], columns, preferred_element_type=jnp.float32)
        for c in range(0, columns.shape[1], LANES):
            ratio[:, at + c:at + c + LANES] = -coulomb[:, c:c + LANES] / (
                row_energies[...] + column_energies[columns_at[(at + c) // LANES]]
            )

    copies = []
    for group in range(0, nkap, group_size):
        top, bottom = group * rows, (group + group_size) * rows
        for q in range(group, group + group_size):
            for position, (row, lanes) in enumerate(columns_at):
                columns = slice(position * LANES, (position + 1) * LANES)
                damping = 1.0 - row_factors[q] * column_factors[q, row, lanes]
                amp[q * rows:(q + 1) * rows, columns] = (
                    ratio[:, columns] * damping * damping
                ).astype(amp.dtype)
        span = slice(group, group + group_size)
        for start in range(0, naux, p_tile):
            tile = slice(start, start + p_tile)
            value = lax.dot_general(
                amp[top:bottom, :],
                partner_columns(tile),
                (((1,), (1,)), ((), ())),
                preferred_element_type=jnp.float32,
            ).reshape(group_size, rows, p_tile)
            if mode != "first":
                value = value + partial[span, :, tile]
            out[span, :, tile] = value.astype(out.dtype)
            if mode == "last":
                copy = pltpu.make_async_copy(
                    out.at[span, :, tile], result.at[span, 0, :, tile], sems.at[len(copies)]
                )
                copy.start()
                copies.append(copy)
    for copy in copies:
        copy.wait()


def add_terms(place, energies, vir_rows, nkap, made, partners, partial, shape, last=False):
    pieces = tuple(partner[:3] for partner in partners)
    arrays = [partner[3] for partner in partners]
    naux = arrays[0].shape[0]
    rows = vir_rows.shape[1]
    width = sum(array.shape[1] for array in arrays)
    vmem = pl.BlockSpec(memory_space=pltpu.VMEM)
    smem = pl.BlockSpec(memory_space=pltpu.SMEM)
    density = jax.ShapeDtypeStruct((nkap, rows, naux), jnp.float32)
    scratch = [
        pltpu.VMEM((nkap * rows, width), jnp.bfloat16),
        pltpu.VMEM((rows, width), jnp.float32),
    ]
    aliases = {}
    if made is None:
        mode = "first"
        operands = [place, energies, vir_rows] + arrays
        in_specs = [smem, smem] + [vmem] * (1 + len(arrays))
        out_shape = (
            jax.ShapeDtypeStruct((rows, naux), arrays[0].dtype),
            jax.ShapeDtypeStruct((rows, LANES), jnp.float32),
            jax.ShapeDtypeStruct((nkap, rows, LANES), jnp.float32),
            jax.ShapeDtypeStruct((2 * len(PARTNERS), rows), jnp.float32),
            jax.ShapeDtypeStruct((nkap, 2 * len(PARTNERS), rows), jnp.float32),
            density,
        )
        out_specs = (vmem,) * 6
    else:
        mode = "last" if last else "middle"
        operands = list(made) + arrays + [partial]
        in_specs = [vmem] * len(operands)
        if last:
            out_shape = jax.ShapeDtypeStruct((nkap, 1, rows, naux), jnp.bfloat16)
            out_specs = pl.BlockSpec(memory_space=pl.ANY)
            scratch.append(pltpu.VMEM((nkap, rows, naux), jnp.bfloat16))
            scratch.append(pltpu.SemaphoreType.DMA((nkap // shape[0] * (naux // shape[1]),)))
        else:
            out_shape, out_specs = density, vmem
            aliases = {len(operands) - 1: 0}
    return pl.pallas_call(
        functools.partial(terms_kernel, pieces, mode, shape),
        out_shape=out_shape,
        input_output_aliases=aliases,
        in_specs=in_specs,
        out_specs=out_specs,
        scratch_shapes=scratch,
        compiler_params=pltpu.CompilerParams(vmem_limit_bytes=VMEM_LIMIT),
        cost_estimate=pl.CostEstimate(flops=1, bytes_accessed=1, transcendentals=0),
    )(*operands)


def pair_terms(integrals, vir_coeff, occ_energy, vir_energy, kappas):
    aux_local, occ_count, basis = integrals.shape
    vir_local = vir_coeff.shape[1]
    wide_index = lax.axis_index("wide")
    batch_index = lax.axis_index("batch")
    place = jnp.stack(
        [wide_index, batch_index, jnp.full((), occ_count, wide_index.dtype)]
    ).astype(jnp.int32)
    vir_rows = vir_energy.reshape(-1, vir_local)
    def to_owner(columns):
        return lax.all_to_all(columns, "wide", split_axis=1, concat_axis=0, tiled=True)[:, 0, :]

    def over_batch(value):
        return from_behind(value, "batch", 1)

    def over_cores(value):
        return swap_by(value, "wide", 1)

    def over_pairs(value):
        return swap_by(value, "wide", 2)

    def along(value):
        return hand_along(value, "wide")

    together = lax.optimization_barrier
    sends_near = ((wide_index ^ (wide_index >> 1)) & 1) == 0
    energies = jnp.concatenate([kappas, occ_energy])
    flat_ints = integrals.reshape(aux_local * occ_count, basis)
    transformed = jnp.dot(flat_ints, vir_coeff, preferred_element_type=jnp.float32).astype(
        jnp.bfloat16
    )
    own, sends_near, vir_rows, place, energies = together(
        (
            to_owner(transformed.reshape(aux_local, occ_count, vir_local)),
            sends_near,
            vir_rows,
            place,
            energies,
        )
    )

    def for_sibling(near, far):
        return over_cores(
            jnp.concatenate([jnp.where(sends_near, *pair) for pair in zip(near, far)], axis=1)
        )

    cut = vir_local // 2
    sibling = over_cores(own)
    low, high = cut_in_two(own)
    step = functools.partial(add_terms, place, energies, vir_rows, kappas.shape[0])

    own_o_high = over_batch(high)
    near_low = over_pairs(low)
    *made, density = step(None, [("own", 0, 0, low), ("own", 0, cut, high)], None, (8, 512))
    step = functools.partial(step, made)

    low, high, density = together((low, high, density))
    own_o_low = over_batch(low)
    near_high = over_pairs(high)
    density = step([("sibling", 0, 0, sibling)], density, (8, 512))

    near_low, own_o_high, density = together((near_low, own_o_high, density))
    near_o_high = over_pairs(own_o_high)
    far_low = along(near_low)
    density = step([("own", 1, cut, own_o_high), ("near", 0, 0, near_low)], density, (8, 512))

    own_o_low, own_o_high, near_low, near_high, density = together(
        (own_o_low, own_o_high, near_low, near_high, density)
    )
    far_high = along(near_high)
    near_o_low = over_batch(near_low)
    sibling_o = over_cores(jnp.concatenate([own_o_low, own_o_high], axis=1))
    density = step([("own", 1, 0, own_o_low), ("near", 0, cut, near_high)], density, (8, 512))

    near_o_high, far_low, density = together((near_o_high, far_low, density))
    far_o_high = along(near_o_high)
    far_o_low = over_batch(far_low)
    density = step([("far", 0, 0, far_low), ("near", 1, cut, near_o_high)], density, (8, 512))

    far_low, far_high, near_o_low, density = together((far_low, far_high, near_o_low, density))
    third_low = for_sibling((near_low,), (far_low,))
    third_high = for_sibling((near_high,), (far_high,))
    density = step(
        [("near", 1, 0, near_o_low), ("far", 0, cut, far_high), ("sibling", 1, 0, sibling_o)],
        density,
        (2, 512),
    )

    far_o_high, far_o_low, density = together((far_o_high, far_o_low, density))
    third_o_low = for_sibling((near_o_low,), (far_o_low,))
    third_o_high = for_sibling((near_o_high,), (far_o_high,))
    return step(
        [
            ("third", 0, 0, third_low),
            ("third", 0, cut, third_high),
            ("far", 1, 0, far_o_low),
            ("far", 1, cut, far_o_high),
            ("third", 1, 0, third_o_low),
            ("third", 1, cut, third_o_high),
        ],
        density,
        (2, 512),
        last=True,
    )


def pair_density(own_slice, partner, own_energy, partner_energy, row_energy, vir_energy, kappas):
    coulomb = lax.dot_general(
        own_slice, partner, (((0,), (0,)), ((), ())), preferred_element_type=jnp.float32
    )
    denominator = row_energy[:, None] + vir_energy[None, :] - own_energy - partner_energy
    damping = 1.0 - jnp.exp(-kappas[:, None, None] * denominator[None])
    amplitude = (-coulomb[None] * (damping * damping) / denominator[None]).astype(jnp.bfloat16)
    flat = amplitude.reshape(-1, amplitude.shape[2])
    density = lax.dot_general(
        flat, partner, (((1,), (1,)), ((), ())), preferred_element_type=jnp.float32
    )
    return density.reshape(kappas.shape[0], own_slice.shape[1], partner.shape[0])


def ring_terms(integrals, vir_coeff, occ_energy, vir_energy, kappas):
    aux_local, occ_count, basis = integrals.shape
    vir_local = vir_coeff.shape[1]
    batch_index = lax.axis_index("batch")
    wide_index = lax.axis_index("wide")
    flat_ints = integrals.reshape(aux_local * occ_count, basis)
    row_energy = lax.dynamic_slice_in_dim(vir_energy, batch_index * vir_local, vir_local, 0)
    own_energy = lax.dynamic_slice_in_dim(occ_energy, wide_index, 1, 0)[0]

    def term(partner, offset, own_slice):
        partner_index = (wide_index + offset) % occ_count
        partner_energy = lax.dynamic_slice_in_dim(occ_energy, partner_index, 1, 0)[0]
        return pair_density(
            own_slice, partner, own_energy, partner_energy, row_energy, vir_energy, kappas
        )

    transformed = jnp.dot(flat_ints, vir_coeff, preferred_element_type=jnp.float32).astype(
        jnp.bfloat16
    )
    transformed = transformed.reshape(aux_local, occ_count, vir_local)
    own_slice = lax.all_to_all(transformed, "wide", split_axis=1, concat_axis=0, tiled=True)[
        :, 0, :
    ]
    own_full = lax.all_gather(own_slice, "batch", axis=1, tiled=True)
    density = term(own_full, 0, own_slice)
    upper = own_full
    lower = own_full
    for offset in range(1, HALF + 1):
        upper = from_behind(upper, "wide", -1)
        lower = from_behind(lower, "wide", 1)
        density = density + term(upper, offset, own_slice) + term(lower, -offset, own_slice)
    return density.astype(jnp.bfloat16)[:, None, :, :]


def solution(mesh):
    paired = mesh.shape["batch"] == 2 and mesh.shape["wide"] % 4 == 0

    return jax.shard_map(
        pair_terms if paired else ring_terms,
        mesh=mesh,
        in_specs=(P("wide", None, None), P(None, "batch"), P(), P(), P()),
        out_specs=P(None, "wide", "batch", None),
        check_vma=False,
    )
```

```python
import functools

import jax
import jax.numpy as jnp
from jax import lax
from jax.experimental import pallas as pl
from jax.experimental.pallas import tpu as pltpu
from jax.sharding import PartitionSpec as P

HALF = 2
PARTNERS = ("own", "sibling", "third", "near", "far")
VMEM_LIMIT = 18 * 1024 * 1024
LANES = 128


def from_behind(shard, axis, by):
    peers = lax.axis_size(axis)
    return lax.ppermute(shard, axis, [(i, (i + by) % peers) for i in range(peers)])


def swap_by(shard, axis, bit):
    peers = lax.axis_size(axis)
    return lax.ppermute(shard, axis, [(i, i ^ bit) for i in range(peers)])


def hand_along(shard, axis):
    peers = lax.axis_size(axis)
    return lax.ppermute(
        shard,
        axis,
        [(i, (i + (4 if i // 2 % 2 == 0 else -4)) % peers) for i in range(peers)],
    )


def to_far_pair(shard, axis):
    peers = lax.axis_size(axis)
    return lax.ppermute(
        shard,
        axis,
        [(i, (i + (-2 if i // 2 % 2 == 0 else 2)) % peers) for i in range(peers)],
    )


def cut_kernel(own, low, high):
    cut = low.shape[1]
    low[...] = own[:, :cut]
    high[...] = own[:, cut:]


def cut_in_two(own):
    vmem = pl.BlockSpec(memory_space=pltpu.VMEM)
    half = jax.ShapeDtypeStruct((own.shape[0], own.shape[1] // 2), own.dtype)
    return pl.pallas_call(
        cut_kernel,
        out_shape=(half, half),
        in_specs=[vmem],
        out_specs=(vmem, vmem),
        compiler_params=pltpu.CompilerParams(vmem_limit_bytes=VMEM_LIMIT),
        cost_estimate=pl.CostEstimate(flops=1, bytes_accessed=1, transcendentals=0),
    )(own)


def make_tables(place, energies, vir_rows, own_low, own_high, made):
    own_t, row_energies, row_factors, column_energies, column_factors = made
    nkap, rows = row_factors.shape[0], own_t.shape[0]
    orbital, half, count = place[0], place[1], place[2]
    core_sign = 1 - 2 * lax.rem(orbital, 2)
    pair_sign = 1 - 2 * lax.rem(lax.div(orbital, 2), 2)
    offsets = dict(
        own=0, sibling=core_sign, third=-core_sign, near=HALF * pair_sign, far=-HALF * pair_sign
    )

    def down_columns(row):
        return jnp.transpose(jnp.broadcast_to(row, (LANES, rows)))

    own_t[:rows // 2, :] = jnp.transpose(own_low[...])
    own_t[rows // 2:, :] = jnp.transpose(own_high[...])
    row_energy = vir_rows[pl.ds(half, 1), :] - energies[nkap + orbital]
    row_energies[...] = down_columns(row_energy)
    for q in range(nkap):
        row_factors[q] = down_columns(jnp.exp(-energies[q] * row_energy))
    for row, name in enumerate(PARTNERS):
        index = lax.rem(orbital + offsets[name] + count, count)
        for other in range(2):
            energy = vir_rows[pl.ds(lax.rem(half + other, 2), 1), :] - energies[nkap + index]
            at = slice(2 * row + other, 2 * row + other + 1)
            column_energies[at, :] = energy
            for q in range(nkap):
                column_factors[q, at, :] = jnp.exp(-energies[q] * energy)


def terms_kernel(pieces, mode, shape, *refs):
    if mode == "first":
        place, energies, vir_rows = refs[:3]
        partners = refs[3:3 + len(pieces)]
        *made, out, amp, ratio = refs[3 + len(pieces):]
        make_tables(place, energies, vir_rows, partners[0], partners[1], made)
    else:
        made = refs[:5]
        partners = refs[5:5 + len(pieces)]
        partial, *refs = refs[5 + len(pieces):]
        if mode == "last":
            result, amp, ratio, out, sems = refs
        else:
            out, amp, ratio = refs
    own_t, row_energies, row_factors, column_energies, column_factors = made
    group_size, p_tile = shape
    nkap, rows = row_factors.shape[0], row_factors.shape[1]
    naux = own_t.shape[1]

    columns_at = []
    for (name, other, start), partner in zip(pieces, partners):
        row = 2 * PARTNERS.index(name) + other
        for c in range(start, start + partner.shape[1], LANES):
            columns_at.append((slice(row, row + 1), slice(c, c + LANES)))
    width = LANES * len(columns_at)

    def partner_columns(tile):
        return jnp.concatenate([partner[tile, :] for partner in partners], axis=1)

    for at in range(0, width, 2 * LANES):
        columns = partner_columns(slice(None))[:, at:at + 2 * LANES]
        coulomb = jnp.dot(own_t[...], columns, preferred_element_type=jnp.float32)
        for c in range(0, columns.shape[1], LANES):
            ratio[:, at + c:at + c + LANES] = -coulomb[:, c:c + LANES] / (
                row_energies[...] + column_energies[columns_at[(at + c) // LANES]]
            )

    copies = []
    for group in range(0, nkap, group_size):
        top, bottom = group * rows, (group + group_size) * rows
        for q in range(group, group + group_size):
            for position, (row, lanes) in enumerate(columns_at):
                columns = slice(position * LANES, (position + 1) * LANES)
                damping = 1.0 - row_factors[q] * column_factors[q, row, lanes]
                amp[q * rows:(q + 1) * rows, columns] = (
                    ratio[:, columns] * damping * damping
                ).astype(amp.dtype)
        span = slice(group, group + group_size)
        for start in range(0, naux, p_tile):
            tile = slice(start, start + p_tile)
            value = lax.dot_general(
                amp[top:bottom, :],
                partner_columns(tile),
                (((1,), (1,)), ((), ())),
                preferred_element_type=jnp.float32,
            ).reshape(group_size, rows, p_tile)
            if mode != "first":
                value = value + partial[span, :, tile]
            out[span, :, tile] = value.astype(out.dtype)
            if mode == "last":
                copy = pltpu.make_async_copy(
                    out.at[span, :, tile], result.at[span, 0, :, tile], sems.at[len(copies)]
                )
                copy.start()
                copies.append(copy)
    for copy in copies:
        copy.wait()


def add_terms(place, energies, vir_rows, nkap, made, partners, partial, shape, last=False):
    pieces = tuple(partner[:3] for partner in partners)
    arrays = [partner[3] for partner in partners]
    naux = arrays[0].shape[0]
    rows = vir_rows.shape[1]
    width = sum(array.shape[1] for array in arrays)
    vmem = pl.BlockSpec(memory_space=pltpu.VMEM)
    smem = pl.BlockSpec(memory_space=pltpu.SMEM)
    density = jax.ShapeDtypeStruct((nkap, rows, naux), jnp.float32)
    scratch = [
        pltpu.VMEM((nkap * rows, width), jnp.bfloat16),
        pltpu.VMEM((rows, width), jnp.float32),
    ]
    aliases = {}
    if made is None:
        mode = "first"
        operands = [place, energies, vir_rows] + arrays
        in_specs = [smem, smem] + [vmem] * (1 + len(arrays))
        out_shape = (
            jax.ShapeDtypeStruct((rows, naux), arrays[0].dtype),
            jax.ShapeDtypeStruct((rows, LANES), jnp.float32),
            jax.ShapeDtypeStruct((nkap, rows, LANES), jnp.float32),
            jax.ShapeDtypeStruct((2 * len(PARTNERS), rows), jnp.float32),
            jax.ShapeDtypeStruct((nkap, 2 * len(PARTNERS), rows), jnp.float32),
            density,
        )
        out_specs = (vmem,) * 6
    else:
        mode = "last" if last else "middle"
        operands = list(made) + arrays + [partial]
        in_specs = [vmem] * len(operands)
        if last:
            out_shape = jax.ShapeDtypeStruct((nkap, 1, rows, naux), jnp.bfloat16)
            out_specs = pl.BlockSpec(memory_space=pl.ANY)
            scratch.append(pltpu.VMEM((nkap, rows, naux), jnp.bfloat16))
            scratch.append(pltpu.SemaphoreType.DMA((nkap // shape[0] * (naux // shape[1]),)))
        else:
            out_shape, out_specs = density, vmem
            aliases = {len(operands) - 1: 0}
    return pl.pallas_call(
        functools.partial(terms_kernel, pieces, mode, shape),
        out_shape=out_shape,
        input_output_aliases=aliases,
        in_specs=in_specs,
        out_specs=out_specs,
        scratch_shapes=scratch,
        compiler_params=pltpu.CompilerParams(vmem_limit_bytes=VMEM_LIMIT),
        cost_estimate=pl.CostEstimate(flops=1, bytes_accessed=1, transcendentals=0),
    )(*operands)


def pair_terms(integrals, vir_coeff, occ_energy, vir_energy, kappas):
    aux_local, occ_count, basis = integrals.shape
    vir_local = vir_coeff.shape[1]
    wide_index = lax.axis_index("wide")
    batch_index = lax.axis_index("batch")
    place = jnp.stack(
        [wide_index, batch_index, jnp.full((), occ_count, wide_index.dtype)]
    ).astype(jnp.int32)
    vir_rows = vir_energy.reshape(-1, vir_local)
    def to_owner(columns):
        return lax.all_to_all(columns, "wide", split_axis=1, concat_axis=0, tiled=True)[:, 0, :]

    def over_batch(value):
        return from_behind(value, "batch", 1)

    def over_cores(value):
        return swap_by(value, "wide", 1)

    def over_pairs(value):
        return swap_by(value, "wide", 2)

    def along(value):
        return hand_along(value, "wide")

    together = lax.optimization_barrier
    sends_near = ((wide_index ^ (wide_index >> 1)) & 1) == 0
    energies = jnp.concatenate([kappas, occ_energy])
    flat_ints = integrals.reshape(aux_local * occ_count, basis)
    transformed = jnp.dot(flat_ints, vir_coeff, preferred_element_type=jnp.float32).astype(
        jnp.bfloat16
    )
    own, sends_near, vir_rows, place, energies = together(
        (
            to_owner(transformed.reshape(aux_local, occ_count, vir_local)),
            sends_near,
            vir_rows,
            place,
            energies,
        )
    )

    def for_sibling(near, far):
        return over_cores(
            jnp.concatenate([jnp.where(sends_near, *pair) for pair in zip(near, far)], axis=1)
        )

    cut = vir_local // 2
    sibling = over_cores(own)
    low, high = cut_in_two(own)
    step = functools.partial(add_terms, place, energies, vir_rows, kappas.shape[0])

    own_o_high = over_batch(high)
    near_low = over_pairs(low)
    *made, density = step(None, [("own", 0, 0, low), ("own", 0, cut, high)], None, (8, 512))
    step = functools.partial(step, made)

    low, high, density = together((low, high, density))
    own_o_low = over_batch(low)
    near_high = over_pairs(high)
    density = step([("sibling", 0, 0, sibling)], density, (8, 512))

    near_low, own_o_high, density = together((near_low, own_o_high, density))
    near_o_high = over_pairs(own_o_high)
    far_low = along(near_low)
    far_o_high = to_far_pair(own_o_high, "wide")
    density = step([("own", 1, cut, own_o_high), ("near", 0, 0, near_low)], density, (8, 512))

    near_low, near_high, own_o_low, density = together((near_low, near_high, own_o_low, density))
    far_high = along(near_high)
    near_o_low = over_batch(near_low)
    density = step([("own", 1, 0, own_o_low), ("near", 0, cut, near_high)], density, (8, 512))

    own_o_low, own_o_high, far_low, density = together((own_o_low, own_o_high, far_low, density))
    far_o_low = over_batch(far_low)
    sibling_o = over_cores(jnp.concatenate([own_o_low, own_o_high], axis=1))
    density = step([("far", 0, 0, far_low), ("near", 1, cut, near_o_high)], density, (8, 512))

    far_low, far_high, near_o_low, density = together((far_low, far_high, near_o_low, density))
    third_low = for_sibling((near_low,), (far_low,))
    third_high = for_sibling((near_high,), (far_high,))
    density = step(
        [("near", 1, 0, near_o_low), ("far", 0, cut, far_high), ("sibling", 1, 0, sibling_o)],
        density,
        (2, 512),
    )

    far_o_high, far_o_low, density = together((far_o_high, far_o_low, density))
    third_o_low = for_sibling((near_o_low,), (far_o_low,))
    third_o_high = for_sibling((near_o_high,), (far_o_high,))
    return step(
        [
            ("third", 0, 0, third_low),
            ("third", 0, cut, third_high),
            ("far", 1, 0, far_o_low),
            ("far", 1, cut, far_o_high),
            ("third", 1, 0, third_o_low),
            ("third", 1, cut, third_o_high),
        ],
        density,
        (2, 512),
        last=True,
    )


def pair_density(own_slice, partner, own_energy, partner_energy, row_energy, vir_energy, kappas):
    coulomb = lax.dot_general(
        own_slice, partner, (((0,), (0,)), ((), ())), preferred_element_type=jnp.float32
    )
    denominator = row_energy[:, None] + vir_energy[None, :] - own_energy - partner_energy
    damping = 1.0 - jnp.exp(-kappas[:, None, None] * denominator[None])
    amplitude = (-coulomb[None] * (damping * damping) / denominator[None]).astype(jnp.bfloat16)
    flat = amplitude.reshape(-1, amplitude.shape[2])
    density = lax.dot_general(
        flat, partner, (((1,), (1,)), ((), ())), preferred_element_type=jnp.float32
    )
    return density.reshape(kappas.shape[0], own_slice.shape[1], partner.shape[0])


def ring_terms(integrals, vir_coeff, occ_energy, vir_energy, kappas):
    aux_local, occ_count, basis = integrals.shape
    vir_local = vir_coeff.shape[1]
    batch_index = lax.axis_index("batch")
    wide_index = lax.axis_index("wide")
    flat_ints = integrals.reshape(aux_local * occ_count, basis)
    row_energy = lax.dynamic_slice_in_dim(vir_energy, batch_index * vir_local, vir_local, 0)
    own_energy = lax.dynamic_slice_in_dim(occ_energy, wide_index, 1, 0)[0]

    def term(partner, offset, own_slice):
        partner_index = (wide_index + offset) % occ_count
        partner_energy = lax.dynamic_slice_in_dim(occ_energy, partner_index, 1, 0)[0]
        return pair_density(
            own_slice, partner, own_energy, partner_energy, row_energy, vir_energy, kappas
        )

    transformed = jnp.dot(flat_ints, vir_coeff, preferred_element_type=jnp.float32).astype(
        jnp.bfloat16
    )
    transformed = transformed.reshape(aux_local, occ_count, vir_local)
    own_slice = lax.all_to_all(transformed, "wide", split_axis=1, concat_axis=0, tiled=True)[
        :, 0, :
    ]
    own_full = lax.all_gather(own_slice, "batch", axis=1, tiled=True)
    density = term(own_full, 0, own_slice)
    upper = own_full
    lower = own_full
    for offset in range(1, HALF + 1):
        upper = from_behind(upper, "wide", -1)
        lower = from_behind(lower, "wide", 1)
        density = density + term(upper, offset, own_slice) + term(lower, -offset, own_slice)
    return density.astype(jnp.bfloat16)[:, None, :, :]


def solution(mesh):
    paired = mesh.shape["batch"] == 2 and mesh.shape["wide"] % 4 == 0

    return jax.shard_map(
        pair_terms if paired else ring_terms,
        mesh=mesh,
        in_specs=(P("wide", None, None), P(None, "batch"), P(), P(), P()),
        out_specs=P(None, "wide", "batch", None),
        check_vma=False,
    )
```

```python
import functools

import jax
import jax.numpy as jnp
from jax import lax
from jax.experimental import pallas as pl
from jax.experimental.pallas import tpu as pltpu
from jax.sharding import PartitionSpec as P

HALF = 2
PARTNERS = ("own", "sibling", "third", "near", "far")
VMEM_LIMIT = 18 * 1024 * 1024
LANES = 128


def from_behind(shard, axis, by):
    peers = lax.axis_size(axis)
    return lax.ppermute(shard, axis, [(i, (i + by) % peers) for i in range(peers)])


def swap_by(shard, axis, bit):
    peers = lax.axis_size(axis)
    return lax.ppermute(shard, axis, [(i, i ^ bit) for i in range(peers)])


def hand_along(shard, axis):
    peers = lax.axis_size(axis)
    return lax.ppermute(
        shard,
        axis,
        [(i, (i + (4 if i // 2 % 2 == 0 else -4)) % peers) for i in range(peers)],
    )


def make_tables(place, energies, vir_rows, own_low, own_high, made):
    own_t, row_energies, row_factors, column_energies, column_factors = made
    nkap, rows = row_factors.shape[0], own_t.shape[0]
    orbital, half, count = place[0], place[1], place[2]
    core_sign = 1 - 2 * lax.rem(orbital, 2)
    pair_sign = 1 - 2 * lax.rem(lax.div(orbital, 2), 2)
    offsets = dict(
        own=0, sibling=core_sign, third=-core_sign, near=HALF * pair_sign, far=-HALF * pair_sign
    )

    def down_columns(row):
        return jnp.transpose(jnp.broadcast_to(row, (LANES, rows)))

    own_t[:rows // 2, :] = jnp.transpose(own_low[...])
    own_t[rows // 2:, :] = jnp.transpose(own_high[...])
    row_energy = vir_rows[pl.ds(half, 1), :] - energies[nkap + orbital]
    row_energies[...] = down_columns(row_energy)
    for q in range(nkap):
        row_factors[q] = down_columns(jnp.exp(-energies[q] * row_energy))
    for row, name in enumerate(PARTNERS):
        index = lax.rem(orbital + offsets[name] + count, count)
        for other in range(2):
            energy = vir_rows[pl.ds(lax.rem(half + other, 2), 1), :] - energies[nkap + index]
            at = slice(2 * row + other, 2 * row + other + 1)
            column_energies[at, :] = energy
            for q in range(nkap):
                column_factors[q, at, :] = jnp.exp(-energies[q] * energy)


def terms_kernel(pieces, mode, shape, *refs):
    if mode == "first":
        place, energies, vir_rows = refs[:3]
        partners = refs[3:3 + len(pieces)]
        *made, out, amp, ratio = refs[3 + len(pieces):]
        make_tables(place, energies, vir_rows, partners[0], partners[1], made)
    else:
        made = refs[:5]
        partners = refs[5:5 + len(pieces)]
        partial, *refs = refs[5 + len(pieces):]
        if mode == "last":
            result, amp, ratio, out, sems = refs
        else:
            out, amp, ratio = refs
    own_t, row_energies, row_factors, column_energies, column_factors = made
    group_size, p_tile = shape
    nkap, rows = row_factors.shape[0], row_factors.shape[1]
    naux = own_t.shape[1]

    columns_at = []
    for (name, other, start), partner in zip(pieces, partners):
        row = 2 * PARTNERS.index(name) + other
        for c in range(start, start + partner.shape[1], LANES):
            columns_at.append((slice(row, row + 1), slice(c, c + LANES)))
    width = LANES * len(columns_at)

    def partner_columns(tile):
        return jnp.concatenate([partner[tile, :] for partner in partners], axis=1)

    for at in range(0, width, 2 * LANES):
        columns = partner_columns(slice(None))[:, at:at + 2 * LANES]
        coulomb = jnp.dot(own_t[...], columns, preferred_element_type=jnp.float32)
        for c in range(0, columns.shape[1], LANES):
            ratio[:, at + c:at + c + LANES] = -coulomb[:, c:c + LANES] / (
                row_energies[...] + column_energies[columns_at[(at + c) // LANES]]
            )

    copies = []
    for group in range(0, nkap, group_size):
        top, bottom = group * rows, (group + group_size) * rows
        for q in range(group, group + group_size):
            for position, (row, lanes) in enumerate(columns_at):
                columns = slice(position * LANES, (position + 1) * LANES)
                damping = 1.0 - row_factors[q] * column_factors[q, row, lanes]
                amp[q * rows:(q + 1) * rows, columns] = (
                    ratio[:, columns] * damping * damping
                ).astype(amp.dtype)
        span = slice(group, group + group_size)
        for start in range(0, naux, p_tile):
            tile = slice(start, start + p_tile)
            value = lax.dot_general(
                amp[top:bottom, :],
                partner_columns(tile),
                (((1,), (1,)), ((), ())),
                preferred_element_type=jnp.float32,
            ).reshape(group_size, rows, p_tile)
            if mode != "first":
                value = value + partial[span, :, tile]
            out[span, :, tile] = value.astype(out.dtype)
            if mode == "last":
                copy = pltpu.make_async_copy(
                    out.at[span, :, tile], result.at[span, 0, :, tile], sems.at[len(copies)]
                )
                copy.start()
                copies.append(copy)
    for copy in copies:
        copy.wait()


def add_terms(place, energies, vir_rows, nkap, made, partners, partial, shape, last=False):
    pieces = tuple(partner[:3] for partner in partners)
    arrays = [partner[3] for partner in partners]
    naux = arrays[0].shape[0]
    rows = vir_rows.shape[1]
    width = sum(array.shape[1] for array in arrays)
    vmem = pl.BlockSpec(memory_space=pltpu.VMEM)
    smem = pl.BlockSpec(memory_space=pltpu.SMEM)
    density = jax.ShapeDtypeStruct((nkap, rows, naux), jnp.float32)
    scratch = [
        pltpu.VMEM((nkap * rows, width), jnp.bfloat16),
        pltpu.VMEM((rows, width), jnp.float32),
    ]
    aliases = {}
    if made is None:
        mode = "first"
        operands = [place, energies, vir_rows] + arrays
        in_specs = [smem, smem] + [vmem] * (1 + len(arrays))
        out_shape = (
            jax.ShapeDtypeStruct((rows, naux), arrays[0].dtype),
            jax.ShapeDtypeStruct((rows, LANES), jnp.float32),
            jax.ShapeDtypeStruct((nkap, rows, LANES), jnp.float32),
            jax.ShapeDtypeStruct((2 * len(PARTNERS), rows), jnp.float32),
            jax.ShapeDtypeStruct((nkap, 2 * len(PARTNERS), rows), jnp.float32),
            density,
        )
        out_specs = (vmem,) * 6
    else:
        mode = "last" if last else "middle"
        operands = list(made) + arrays + [partial]
        in_specs = [vmem] * len(operands)
        if last:
            out_shape = jax.ShapeDtypeStruct((nkap, 1, rows, naux), jnp.bfloat16)
            out_specs = pl.BlockSpec(memory_space=pl.ANY)
            scratch.append(pltpu.VMEM((nkap, rows, naux), jnp.bfloat16))
            scratch.append(pltpu.SemaphoreType.DMA((nkap // shape[0] * (naux // shape[1]),)))
        else:
            out_shape, out_specs = density, vmem
            aliases = {len(operands) - 1: 0}
    return pl.pallas_call(
        functools.partial(terms_kernel, pieces, mode, shape),
        out_shape=out_shape,
        input_output_aliases=aliases,
        in_specs=in_specs,
        out_specs=out_specs,
        scratch_shapes=scratch,
        compiler_params=pltpu.CompilerParams(vmem_limit_bytes=VMEM_LIMIT),
        cost_estimate=pl.CostEstimate(flops=1, bytes_accessed=1, transcendentals=0),
    )(*operands)


def pair_terms(integrals, vir_coeff, occ_energy, vir_energy, kappas):
    aux_local, occ_count, basis = integrals.shape
    vir_local = vir_coeff.shape[1]
    wide_index = lax.axis_index("wide")
    batch_index = lax.axis_index("batch")
    place = jnp.stack(
        [wide_index, batch_index, jnp.full((), occ_count, wide_index.dtype)]
    ).astype(jnp.int32)
    vir_rows = vir_energy.reshape(-1, vir_local)
    def to_owner(columns):
        return lax.all_to_all(columns, "wide", split_axis=1, concat_axis=0, tiled=True)[:, 0, :]

    def over_batch(value):
        return from_behind(value, "batch", 1)

    def over_cores(value):
        return swap_by(value, "wide", 1)

    def over_pairs(value):
        return swap_by(value, "wide", 2)

    def along(value):
        return hand_along(value, "wide")

    together = lax.optimization_barrier
    sends_near = ((wide_index ^ (wide_index >> 1)) & 1) == 0
    energies = jnp.concatenate([kappas, occ_energy])
    flat_ints = integrals.reshape(aux_local * occ_count, basis)
    transformed = jnp.dot(flat_ints, vir_coeff, preferred_element_type=jnp.float32).astype(
        jnp.bfloat16
    )
    transformed = transformed.reshape(aux_local, occ_count, vir_local)
    cut = vir_local // 2
    low, high = to_owner(transformed[:, :, :cut]), to_owner(transformed[:, :, cut:])
    low, sends_near, vir_rows, place, energies = together(
        (low, sends_near, vir_rows, place, energies)
    )

    def for_sibling(near, far):
        return over_cores(
            jnp.concatenate([jnp.where(sends_near, *pair) for pair in zip(near, far)], axis=1)
        )

    step = functools.partial(add_terms, place, energies, vir_rows, kappas.shape[0])

    own_o_low = over_batch(low)
    near_low = over_pairs(low)
    sibling_low = over_cores(low)
    high, sibling_low = together((high, sibling_low))

    own_o_high = over_batch(high)
    near_high = over_pairs(high)
    sibling_high = over_cores(high)
    *made, density = step(None, [("own", 0, 0, low), ("own", 0, cut, high)], None, (8, 512))
    step = functools.partial(step, made)

    near_low, own_o_low, density = together((near_low, own_o_low, density))
    near_o_low = over_pairs(own_o_low)
    far_low = along(near_low)
    density = step(
        [("sibling", 0, 0, sibling_low), ("sibling", 0, cut, sibling_high)], density, (8, 512)
    )

    own_o_high, near_high, density = together((own_o_high, near_high, density))
    far_high = along(near_high)
    near_o_high = over_batch(near_high)
    sibling_o = over_cores(jnp.concatenate([own_o_low, own_o_high], axis=1))
    density = step(
        [
            ("own", 1, 0, own_o_low),
            ("near", 0, 0, near_low),
            ("own", 1, cut, own_o_high),
            ("near", 0, cut, near_high),
        ],
        density,
        (2, 512),
    )

    near_o_low, far_low, far_high, density = together((near_o_low, far_low, far_high, density))
    far_o_low = along(near_o_low)
    far_o_high = over_batch(far_high)
    third_low = for_sibling((near_low,), (far_low,))
    third_high = for_sibling((near_high,), (far_high,))
    density = step(
        [
            ("far", 0, 0, far_low),
            ("near", 1, 0, near_o_low),
            ("near", 1, cut, near_o_high),
            ("far", 0, cut, far_high),
        ],
        density,
        (2, 512),
    )
    density = step([("sibling", 1, 0, sibling_o)], density, (8, 512))

    far_o_low, far_o_high, density = together((far_o_low, far_o_high, density))
    third_o_low = for_sibling((near_o_low,), (far_o_low,))
    third_o_high = for_sibling((near_o_high,), (far_o_high,))
    return step(
        [
            ("third", 0, 0, third_low),
            ("third", 0, cut, third_high),
            ("far", 1, 0, far_o_low),
            ("far", 1, cut, far_o_high),
            ("third", 1, 0, third_o_low),
            ("third", 1, cut, third_o_high),
        ],
        density,
        (2, 512),
        last=True,
    )


def pair_density(own_slice, partner, own_energy, partner_energy, row_energy, vir_energy, kappas):
    coulomb = lax.dot_general(
        own_slice, partner, (((0,), (0,)), ((), ())), preferred_element_type=jnp.float32
    )
    denominator = row_energy[:, None] + vir_energy[None, :] - own_energy - partner_energy
    damping = 1.0 - jnp.exp(-kappas[:, None, None] * denominator[None])
    amplitude = (-coulomb[None] * (damping * damping) / denominator[None]).astype(jnp.bfloat16)
    flat = amplitude.reshape(-1, amplitude.shape[2])
    density = lax.dot_general(
        flat, partner, (((1,), (1,)), ((), ())), preferred_element_type=jnp.float32
    )
    return density.reshape(kappas.shape[0], own_slice.shape[1], partner.shape[0])


def ring_terms(integrals, vir_coeff, occ_energy, vir_energy, kappas):
    aux_local, occ_count, basis = integrals.shape
    vir_local = vir_coeff.shape[1]
    batch_index = lax.axis_index("batch")
    wide_index = lax.axis_index("wide")
    flat_ints = integrals.reshape(aux_local * occ_count, basis)
    row_energy = lax.dynamic_slice_in_dim(vir_energy, batch_index * vir_local, vir_local, 0)
    own_energy = lax.dynamic_slice_in_dim(occ_energy, wide_index, 1, 0)[0]

    def term(partner, offset, own_slice):
        partner_index = (wide_index + offset) % occ_count
        partner_energy = lax.dynamic_slice_in_dim(occ_energy, partner_index, 1, 0)[0]
        return pair_density(
            own_slice, partner, own_energy, partner_energy, row_energy, vir_energy, kappas
        )

    transformed = jnp.dot(flat_ints, vir_coeff, preferred_element_type=jnp.float32).astype(
        jnp.bfloat16
    )
    transformed = transformed.reshape(aux_local, occ_count, vir_local)
    own_slice = lax.all_to_all(transformed, "wide", split_axis=1, concat_axis=0, tiled=True)[
        :, 0, :
    ]
    own_full = lax.all_gather(own_slice, "batch", axis=1, tiled=True)
    density = term(own_full, 0, own_slice)
    upper = own_full
    lower = own_full
    for offset in range(1, HALF + 1):
        upper = from_behind(upper, "wide", -1)
        lower = from_behind(lower, "wide", 1)
        density = density + term(upper, offset, own_slice) + term(lower, -offset, own_slice)
    return density.astype(jnp.bfloat16)[:, None, :, :]


def solution(mesh):
    paired = mesh.shape["batch"] == 2 and mesh.shape["wide"] % 4 == 0

    return jax.shard_map(
        pair_terms if paired else ring_terms,
        mesh=mesh,
        in_specs=(P("wide", None, None), P(None, "batch"), P(), P(), P()),
        out_specs=P(None, "wide", "batch", None),
        check_vma=False,
    )
```

```python
import functools

import jax
import jax.numpy as jnp
from jax import lax
from jax.experimental import pallas as pl
from jax.experimental.pallas import tpu as pltpu
from jax.sharding import PartitionSpec as P

HALF = 2
PARTNERS = ("own", "sibling", "third", "near", "far")
VMEM_LIMIT = 18 * 1024 * 1024
LANES = 128


def from_behind(shard, axis, by):
    peers = lax.axis_size(axis)
    return lax.ppermute(shard, axis, [(i, (i + by) % peers) for i in range(peers)])


def swap_by(shard, axis, bit):
    peers = lax.axis_size(axis)
    return lax.ppermute(shard, axis, [(i, i ^ bit) for i in range(peers)])


def hand_along(shard, axis):
    peers = lax.axis_size(axis)
    return lax.ppermute(
        shard,
        axis,
        [(i, (i + (4 if i // 2 % 2 == 0 else -4)) % peers) for i in range(peers)],
    )


def cut_kernel(own, low, high):
    cut = low.shape[1]
    low[...] = own[:, :cut]
    high[...] = own[:, cut:]


def cut_in_two(own):
    vmem = pl.BlockSpec(memory_space=pltpu.VMEM)
    half = jax.ShapeDtypeStruct((own.shape[0], own.shape[1] // 2), own.dtype)
    return pl.pallas_call(
        cut_kernel,
        out_shape=(half, half),
        in_specs=[vmem],
        out_specs=(vmem, vmem),
        compiler_params=pltpu.CompilerParams(vmem_limit_bytes=VMEM_LIMIT),
        cost_estimate=pl.CostEstimate(flops=1, bytes_accessed=1, transcendentals=0),
    )(own)


def make_tables(place, energies, vir_rows, own_low, own_high, made):
    own_t, row_energies, row_factors, column_energies, column_factors = made
    nkap, rows = row_factors.shape[0], own_t.shape[0]
    orbital, half, count = place[0], place[1], place[2]
    core_sign = 1 - 2 * lax.rem(orbital, 2)
    pair_sign = 1 - 2 * lax.rem(lax.div(orbital, 2), 2)
    offsets = dict(
        own=0, sibling=core_sign, third=-core_sign, near=HALF * pair_sign, far=-HALF * pair_sign
    )

    def down_columns(row):
        return jnp.transpose(jnp.broadcast_to(row, (LANES, rows)))

    own_t[:rows // 2, :] = jnp.transpose(own_low[...])
    own_t[rows // 2:, :] = jnp.transpose(own_high[...])
    row_energy = vir_rows[pl.ds(half, 1), :] - energies[nkap + orbital]
    row_energies[...] = down_columns(row_energy)
    for q in range(nkap):
        row_factors[q] = down_columns(jnp.exp(-energies[q] * row_energy))
    for row, name in enumerate(PARTNERS):
        index = lax.rem(orbital + offsets[name] + count, count)
        for other in range(2):
            energy = vir_rows[pl.ds(lax.rem(half + other, 2), 1), :] - energies[nkap + index]
            at = slice(2 * row + other, 2 * row + other + 1)
            column_energies[at, :] = energy
            for q in range(nkap):
                column_factors[q, at, :] = jnp.exp(-energies[q] * energy)


def terms_kernel(pieces, mode, shape, *refs):
    if mode == "first":
        place, energies, vir_rows = refs[:3]
        partners = refs[3:3 + len(pieces)]
        *made, out, amp, ratio = refs[3 + len(pieces):]
        make_tables(place, energies, vir_rows, partners[0], partners[1], made)
    else:
        made = refs[:5]
        partners = refs[5:5 + len(pieces)]
        partial, *refs = refs[5 + len(pieces):]
        if mode == "last":
            result, amp, ratio, out, sems = refs
        else:
            out, amp, ratio = refs
    own_t, row_energies, row_factors, column_energies, column_factors = made
    group_size, p_tile = shape
    nkap, rows = row_factors.shape[0], row_factors.shape[1]
    naux = own_t.shape[1]

    columns_at = []
    for (name, other, start), partner in zip(pieces, partners):
        row = 2 * PARTNERS.index(name) + other
        for c in range(start, start + partner.shape[1], LANES):
            columns_at.append((slice(row, row + 1), slice(c, c + LANES)))
    width = LANES * len(columns_at)

    def partner_columns(tile):
        return jnp.concatenate([partner[tile, :] for partner in partners], axis=1)

    coulomb = jnp.dot(
        own_t[...], partner_columns(slice(None)), preferred_element_type=jnp.float32
    )
    for position, (row, lanes) in enumerate(columns_at):
        columns = slice(position * LANES, (position + 1) * LANES)
        ratio[:, columns] = -coulomb[:, columns] / (
            row_energies[...] + column_energies[row, lanes]
        )

    copies = []
    for group in range(0, nkap, group_size):
        top, bottom = group * rows, (group + group_size) * rows
        for q in range(group, group + group_size):
            for position, (row, lanes) in enumerate(columns_at):
                columns = slice(position * LANES, (position + 1) * LANES)
                damping = 1.0 - row_factors[q] * column_factors[q, row, lanes]
                amp[q * rows:(q + 1) * rows, columns] = (
                    ratio[:, columns] * damping * damping
                ).astype(amp.dtype)
        span = slice(group, group + group_size)
        for start in range(0, naux, p_tile):
            tile = slice(start, start + p_tile)
            value = lax.dot_general(
                amp[top:bottom, :],
                partner_columns(tile),
                (((1,), (1,)), ((), ())),
                preferred_element_type=jnp.float32,
            ).reshape(group_size, rows, p_tile)
            if mode != "first":
                value = value + partial[span, :, tile]
            out[span, :, tile] = value.astype(out.dtype)
            if mode == "last":
                copy = pltpu.make_async_copy(
                    out.at[span, :, tile], result.at[span, 0, :, tile], sems.at[len(copies)]
                )
                copy.start()
                copies.append(copy)
    for copy in copies:
        copy.wait()


def add_terms(place, energies, vir_rows, nkap, made, partners, partial, shape, last=False):
    pieces = tuple(partner[:3] for partner in partners)
    arrays = [partner[3] for partner in partners]
    naux = arrays[0].shape[0]
    rows = vir_rows.shape[1]
    width = sum(array.shape[1] for array in arrays)
    vmem = pl.BlockSpec(memory_space=pltpu.VMEM)
    smem = pl.BlockSpec(memory_space=pltpu.SMEM)
    density = jax.ShapeDtypeStruct((nkap, rows, naux), jnp.float32)
    scratch = [
        pltpu.VMEM((nkap * rows, width), jnp.bfloat16),
        pltpu.VMEM((rows, width), jnp.float32),
    ]
    aliases = {}
    if made is None:
        mode = "first"
        operands = [place, energies, vir_rows] + arrays
        in_specs = [smem, smem] + [vmem] * (1 + len(arrays))
        out_shape = (
            jax.ShapeDtypeStruct((rows, naux), arrays[0].dtype),
            jax.ShapeDtypeStruct((rows, LANES), jnp.float32),
            jax.ShapeDtypeStruct((nkap, rows, LANES), jnp.float32),
            jax.ShapeDtypeStruct((2 * len(PARTNERS), rows), jnp.float32),
            jax.ShapeDtypeStruct((nkap, 2 * len(PARTNERS), rows), jnp.float32),
            density,
        )
        out_specs = (vmem,) * 6
    else:
        mode = "last" if last else "middle"
        operands = list(made) + arrays + [partial]
        in_specs = [vmem] * len(operands)
        if last:
            out_shape = jax.ShapeDtypeStruct((nkap, 1, rows, naux), jnp.bfloat16)
            out_specs = pl.BlockSpec(memory_space=pl.ANY)
            scratch.append(pltpu.VMEM((nkap, rows, naux), jnp.bfloat16))
            scratch.append(pltpu.SemaphoreType.DMA((nkap // shape[0] * (naux // shape[1]),)))
        else:
            out_shape, out_specs = density, vmem
            aliases = {len(operands) - 1: 0}
    return pl.pallas_call(
        functools.partial(terms_kernel, pieces, mode, shape),
        out_shape=out_shape,
        input_output_aliases=aliases,
        in_specs=in_specs,
        out_specs=out_specs,
        scratch_shapes=scratch,
        compiler_params=pltpu.CompilerParams(vmem_limit_bytes=VMEM_LIMIT),
        cost_estimate=pl.CostEstimate(flops=1, bytes_accessed=1, transcendentals=0),
    )(*operands)


def pair_terms(integrals, vir_coeff, occ_energy, vir_energy, kappas):
    aux_local, occ_count, basis = integrals.shape
    vir_local = vir_coeff.shape[1]
    wide_index = lax.axis_index("wide")
    batch_index = lax.axis_index("batch")
    place = jnp.stack(
        [wide_index, batch_index, jnp.full((), occ_count, wide_index.dtype)]
    ).astype(jnp.int32)
    vir_rows = vir_energy.reshape(-1, vir_local)
    def to_owner(columns):
        return lax.all_to_all(columns, "wide", split_axis=1, concat_axis=0, tiled=True)[:, 0, :]

    def over_batch(value):
        return from_behind(value, "batch", 1)

    def over_cores(value):
        return swap_by(value, "wide", 1)

    def over_pairs(value):
        return swap_by(value, "wide", 2)

    def along(value):
        return hand_along(value, "wide")

    together = lax.optimization_barrier
    sends_near = ((wide_index ^ (wide_index >> 1)) & 1) == 0
    energies = jnp.concatenate([kappas, occ_energy])
    flat_ints = integrals.reshape(aux_local * occ_count, basis)
    transformed = jnp.dot(flat_ints, vir_coeff, preferred_element_type=jnp.float32).astype(
        jnp.bfloat16
    )
    own, sends_near, vir_rows, place, energies = together(
        (
            to_owner(transformed.reshape(aux_local, occ_count, vir_local)),
            sends_near,
            vir_rows,
            place,
            energies,
        )
    )

    def for_sibling(near, far):
        return over_cores(
            jnp.concatenate([jnp.where(sends_near, *pair) for pair in zip(near, far)], axis=1)
        )

    cut = vir_local // 2
    sibling = over_cores(own)
    low, high = cut_in_two(own)
    step = functools.partial(add_terms, place, energies, vir_rows, kappas.shape[0])

    own_o_high = over_batch(high)
    near_low = over_pairs(low)
    *made, density = step(None, [("own", 0, 0, low), ("own", 0, cut, high)], None, (8, 512))
    step = functools.partial(step, made)

    low, high, density = together((low, high, density))
    own_o_low = over_batch(low)
    near_high = over_pairs(high)
    density = step([("sibling", 0, 0, sibling)], density, (2, 512))

    near_low, own_o_high, density = together((near_low, own_o_high, density))
    near_o_high = over_pairs(own_o_high)
    far_low = along(near_low)
    density = step([("own", 1, cut, own_o_high), ("near", 0, 0, near_low)], density, (2, 1536))

    own_o_low, own_o_high, near_low, near_high, density = together(
        (own_o_low, own_o_high, near_low, near_high, density)
    )
    far_high = along(near_high)
    near_o_low = over_batch(near_low)
    sibling_o = over_cores(jnp.concatenate([own_o_low, own_o_high], axis=1))
    density = step([("own", 1, 0, own_o_low), ("near", 0, cut, near_high)], density, (8, 512))

    near_o_high, far_low, density = together((near_o_high, far_low, density))
    far_o_high = along(near_o_high)
    far_o_low = over_batch(far_low)
    density = step([("far", 0, 0, far_low), ("near", 1, cut, near_o_high)], density, (8, 512))

    far_low, far_high, near_o_low, density = together((far_low, far_high, near_o_low, density))
    third_low = for_sibling((near_low,), (far_low,))
    third_high = for_sibling((near_high,), (far_high,))
    density = step(
        [("near", 1, 0, near_o_low), ("far", 0, cut, far_high), ("sibling", 1, 0, sibling_o)],
        density,
        (2, 1536),
    )

    far_o_high, far_o_low, density = together((far_o_high, far_o_low, density))
    third_o_low = for_sibling((near_o_low,), (far_o_low,))
    third_o_high = for_sibling((near_o_high,), (far_o_high,))
    return step(
        [
            ("third", 0, 0, third_low),
            ("third", 0, cut, third_high),
            ("far", 1, 0, far_o_low),
            ("far", 1, cut, far_o_high),
            ("third", 1, 0, third_o_low),
            ("third", 1, cut, third_o_high),
        ],
        density,
        (2, 768),
        last=True,
    )


def pair_density(own_slice, partner, own_energy, partner_energy, row_energy, vir_energy, kappas):
    coulomb = lax.dot_general(
        own_slice, partner, (((0,), (0,)), ((), ())), preferred_element_type=jnp.float32
    )
    denominator = row_energy[:, None] + vir_energy[None, :] - own_energy - partner_energy
    damping = 1.0 - jnp.exp(-kappas[:, None, None] * denominator[None])
    amplitude = (-coulomb[None] * (damping * damping) / denominator[None]).astype(jnp.bfloat16)
    flat = amplitude.reshape(-1, amplitude.shape[2])
    density = lax.dot_general(
        flat, partner, (((1,), (1,)), ((), ())), preferred_element_type=jnp.float32
    )
    return density.reshape(kappas.shape[0], own_slice.shape[1], partner.shape[0])


def ring_terms(integrals, vir_coeff, occ_energy, vir_energy, kappas):
    aux_local, occ_count, basis = integrals.shape
    vir_local = vir_coeff.shape[1]
    batch_index = lax.axis_index("batch")
    wide_index = lax.axis_index("wide")
    flat_ints = integrals.reshape(aux_local * occ_count, basis)
    row_energy = lax.dynamic_slice_in_dim(vir_energy, batch_index * vir_local, vir_local, 0)
    own_energy = lax.dynamic_slice_in_dim(occ_energy, wide_index, 1, 0)[0]

    def term(partner, offset, own_slice):
        partner_index = (wide_index + offset) % occ_count
        partner_energy = lax.dynamic_slice_in_dim(occ_energy, partner_index, 1, 0)[0]
        return pair_density(
            own_slice, partner, own_energy, partner_energy, row_energy, vir_energy, kappas
        )

    transformed = jnp.dot(flat_ints, vir_coeff, preferred_element_type=jnp.float32).astype(
        jnp.bfloat16
    )
    transformed = transformed.reshape(aux_local, occ_count, vir_local)
    own_slice = lax.all_to_all(transformed, "wide", split_axis=1, concat_axis=0, tiled=True)[
        :, 0, :
    ]
    own_full = lax.all_gather(own_slice, "batch", axis=1, tiled=True)
    density = term(own_full, 0, own_slice)
    upper = own_full
    lower = own_full
    for offset in range(1, HALF + 1):
        upper = from_behind(upper, "wide", -1)
        lower = from_behind(lower, "wide", 1)
        density = density + term(upper, offset, own_slice) + term(lower, -offset, own_slice)
    return density.astype(jnp.bfloat16)[:, None, :, :]


def solution(mesh):
    paired = mesh.shape["batch"] == 2 and mesh.shape["wide"] % 4 == 0

    return jax.shard_map(
        pair_terms if paired else ring_terms,
        mesh=mesh,
        in_specs=(P("wide", None, None), P(None, "batch"), P(), P(), P()),
        out_specs=P(None, "wide", "batch", None),
        check_vma=False,
    )
```

```python
import functools

import jax
import jax.numpy as jnp
from jax import lax
from jax.experimental import pallas as pl
from jax.experimental.pallas import tpu as pltpu
from jax.sharding import PartitionSpec as P

HALF = 2
PARTNERS = ("own", "sibling", "third", "near", "far")
VMEM_LIMIT = 18 * 1024 * 1024
LANES = 128


def from_behind(shard, axis, by):
    peers = lax.axis_size(axis)
    return lax.ppermute(shard, axis, [(i, (i + by) % peers) for i in range(peers)])


def swap_by(shard, axis, bit):
    peers = lax.axis_size(axis)
    return lax.ppermute(shard, axis, [(i, i ^ bit) for i in range(peers)])


def hand_along(shard, axis):
    peers = lax.axis_size(axis)
    return lax.ppermute(
        shard,
        axis,
        [(i, (i + (4 if i // 2 % 2 == 0 else -4)) % peers) for i in range(peers)],
    )


def cut_kernel(own, low, high):
    cut = low.shape[1]
    low[...] = own[:, :cut]
    high[...] = own[:, cut:]


def cut_in_two(own):
    vmem = pl.BlockSpec(memory_space=pltpu.VMEM)
    half = jax.ShapeDtypeStruct((own.shape[0], own.shape[1] // 2), own.dtype)
    return pl.pallas_call(
        cut_kernel,
        out_shape=(half, half),
        in_specs=[vmem],
        out_specs=(vmem, vmem),
        compiler_params=pltpu.CompilerParams(vmem_limit_bytes=VMEM_LIMIT),
        cost_estimate=pl.CostEstimate(flops=1, bytes_accessed=1, transcendentals=0),
    )(own)


def make_tables(place, energies, vir_rows, own_low, own_high, made):
    own_t, row_energies, row_factors, column_energies, column_factors = made
    nkap, rows = row_factors.shape[0], own_t.shape[0]
    orbital, half, count = place[0], place[1], place[2]
    core_sign = 1 - 2 * lax.rem(orbital, 2)
    pair_sign = 1 - 2 * lax.rem(lax.div(orbital, 2), 2)
    offsets = dict(
        own=0, sibling=core_sign, third=-core_sign, near=HALF * pair_sign, far=-HALF * pair_sign
    )

    def down_columns(row):
        return jnp.transpose(jnp.broadcast_to(row, (LANES, rows)))

    own_t[:rows // 2, :] = jnp.transpose(own_low[...])
    own_t[rows // 2:, :] = jnp.transpose(own_high[...])
    row_energy = vir_rows[pl.ds(half, 1), :] - energies[nkap + orbital]
    row_energies[...] = down_columns(row_energy)
    for q in range(nkap):
        row_factors[q] = down_columns(jnp.exp(-energies[q] * row_energy))
    for row, name in enumerate(PARTNERS):
        index = lax.rem(orbital + offsets[name] + count, count)
        for other in range(2):
            energy = vir_rows[pl.ds(lax.rem(half + other, 2), 1), :] - energies[nkap + index]
            at = slice(2 * row + other, 2 * row + other + 1)
            column_energies[at, :] = energy
            for q in range(nkap):
                column_factors[q, at, :] = jnp.exp(-energies[q] * energy)


def columns_of(pieces, partners):
    columns_at = []
    for (name, other, start), partner in zip(pieces, partners):
        row = 2 * PARTNERS.index(name) + other
        for c in range(start, start + partner.shape[1], LANES):
            columns_at.append((slice(row, row + 1), slice(c, c + LANES)))
    return columns_at


def make_ratios(columns_at, partners, made, ratio):
    own_t, row_energies, _, column_energies, _ = made
    width = LANES * len(columns_at)
    for at in range(0, width, 2 * LANES):
        columns = jnp.concatenate([partner[...] for partner in partners], axis=1)
        columns = columns[:, at:at + 2 * LANES]
        coulomb = jnp.dot(own_t[...], columns, preferred_element_type=jnp.float32)
        for c in range(0, columns.shape[1], LANES):
            ratio[:, at + c:at + c + LANES] = -coulomb[:, c:c + LANES] / (
                row_energies[...] + column_energies[columns_at[(at + c) // LANES]]
            )


def make_amplitudes(q, columns_at, made, ratio, amp):
    _, _, row_factors, _, column_factors = made
    rows = row_factors.shape[1]
    for position, (row, lanes) in enumerate(columns_at):
        columns = slice(position * LANES, (position + 1) * LANES)
        damping = 1.0 - row_factors[q] * column_factors[q, row, lanes]
        amp[q * rows:(q + 1) * rows, columns] = (
            ratio[:, columns] * damping * damping
        ).astype(amp.dtype)


def amplitudes_kernel(pieces, *refs):
    made, partners, (amp, ratio) = refs[:5], refs[5:5 + len(pieces)], refs[5 + len(pieces):]
    columns_at = columns_of(pieces, partners)
    make_ratios(columns_at, partners, made, ratio)
    for q in range(made[2].shape[0]):
        make_amplitudes(q, columns_at, made, ratio, amp)


def amplitudes_of(made, partners):
    arrays = [partner[3] for partner in partners]
    nkap, rows = made[2].shape[0], made[0].shape[0]
    width = sum(array.shape[1] for array in arrays)
    vmem = pl.BlockSpec(memory_space=pltpu.VMEM)
    operands = list(made) + arrays
    return pl.pallas_call(
        functools.partial(amplitudes_kernel, tuple(partner[:3] for partner in partners)),
        out_shape=jax.ShapeDtypeStruct((nkap * rows, width), jnp.bfloat16),
        in_specs=[vmem] * len(operands),
        out_specs=vmem,
        scratch_shapes=[pltpu.VMEM((rows, width), jnp.float32)],
        compiler_params=pltpu.CompilerParams(vmem_limit_bytes=VMEM_LIMIT),
        cost_estimate=pl.CostEstimate(flops=1, bytes_accessed=1, transcendentals=0),
    )(*operands)


def terms_kernel(pieces, mode, shape, *refs):
    ready_amp, ready_partners = None, []
    if mode == "first":
        place, energies, vir_rows = refs[:3]
        partners = refs[3:3 + len(pieces)]
        *made, out, amp, ratio = refs[3 + len(pieces):]
        make_tables(place, energies, vir_rows, partners[0], partners[1], made)
    else:
        made = refs[:5]
        partners = refs[5:5 + len(pieces)]
        partial, *refs = refs[5 + len(pieces):]
        if mode == "last":
            ready_amp, *ready_partners, result, amp, ratio, out, sems = refs
        else:
            out, amp, ratio = refs
    group_size, p_tile = shape
    nkap, rows = made[2].shape[0], made[2].shape[1]
    naux = made[0].shape[1]
    columns_at = columns_of(pieces, partners)
    make_ratios(columns_at, partners, made, ratio)

    copies = []
    for group in range(0, nkap, group_size):
        top, bottom = group * rows, (group + group_size) * rows
        for q in range(group, group + group_size):
            make_amplitudes(q, columns_at, made, ratio, amp)
        left = amp[top:bottom, :]
        if mode == "last":
            left = jnp.concatenate([ready_amp[top:bottom, :], left], axis=1)
        span = slice(group, group + group_size)
        for start in range(0, naux, p_tile):
            tile = slice(start, start + p_tile)
            right = [partner[tile, :] for partner in (*ready_partners, *partners)]
            value = lax.dot_general(
                left,
                jnp.concatenate(right, axis=1),
                (((1,), (1,)), ((), ())),
                preferred_element_type=jnp.float32,
            ).reshape(group_size, rows, p_tile)
            if mode != "first":
                value = value + partial[span, :, tile]
            out[span, :, tile] = value.astype(out.dtype)
            if mode == "last":
                copy = pltpu.make_async_copy(
                    out.at[span, :, tile], result.at[span, 0, :, tile], sems.at[len(copies)]
                )
                copy.start()
                copies.append(copy)
    for copy in copies:
        copy.wait()


def add_terms(place, energies, vir_rows, nkap, made, partners, partial, shape, ready=None):
    pieces = tuple(partner[:3] for partner in partners)
    arrays = [partner[3] for partner in partners]
    naux = arrays[0].shape[0]
    rows = vir_rows.shape[1]
    width = sum(array.shape[1] for array in arrays)
    vmem = pl.BlockSpec(memory_space=pltpu.VMEM)
    smem = pl.BlockSpec(memory_space=pltpu.SMEM)
    density = jax.ShapeDtypeStruct((nkap, rows, naux), jnp.float32)
    scratch = [
        pltpu.VMEM((nkap * rows, width), jnp.bfloat16),
        pltpu.VMEM((rows, width), jnp.float32),
    ]
    aliases = {}
    if made is None:
        mode = "first"
        operands = [place, energies, vir_rows] + arrays
        in_specs = [smem, smem] + [vmem] * (1 + len(arrays))
        out_shape = (
            jax.ShapeDtypeStruct((rows, naux), arrays[0].dtype),
            jax.ShapeDtypeStruct((rows, LANES), jnp.float32),
            jax.ShapeDtypeStruct((nkap, rows, LANES), jnp.float32),
            jax.ShapeDtypeStruct((2 * len(PARTNERS), rows), jnp.float32),
            jax.ShapeDtypeStruct((nkap, 2 * len(PARTNERS), rows), jnp.float32),
            density,
        )
        out_specs = (vmem,) * 6
    else:
        mode = "middle" if ready is None else "last"
        operands = list(made) + arrays + [partial] + list(ready or ())
        in_specs = [vmem] * len(operands)
        if ready is not None:
            out_shape = jax.ShapeDtypeStruct((nkap, 1, rows, naux), jnp.bfloat16)
            out_specs = pl.BlockSpec(memory_space=pl.ANY)
            scratch.append(pltpu.VMEM((nkap, rows, naux), jnp.bfloat16))
            scratch.append(pltpu.SemaphoreType.DMA((nkap // shape[0] * (naux // shape[1]),)))
        else:
            out_shape, out_specs = density, vmem
            aliases = {len(operands) - 1: 0}
    return pl.pallas_call(
        functools.partial(terms_kernel, pieces, mode, shape),
        out_shape=out_shape,
        input_output_aliases=aliases,
        in_specs=in_specs,
        out_specs=out_specs,
        scratch_shapes=scratch,
        compiler_params=pltpu.CompilerParams(vmem_limit_bytes=VMEM_LIMIT),
        cost_estimate=pl.CostEstimate(flops=1, bytes_accessed=1, transcendentals=0),
    )(*operands)


def pair_terms(integrals, vir_coeff, occ_energy, vir_energy, kappas):
    aux_local, occ_count, basis = integrals.shape
    vir_local = vir_coeff.shape[1]
    wide_index = lax.axis_index("wide")
    batch_index = lax.axis_index("batch")
    place = jnp.stack(
        [wide_index, batch_index, jnp.full((), occ_count, wide_index.dtype)]
    ).astype(jnp.int32)
    vir_rows = vir_energy.reshape(-1, vir_local)
    def to_owner(columns):
        return lax.all_to_all(columns, "wide", split_axis=1, concat_axis=0, tiled=True)[:, 0, :]

    def over_batch(value):
        return from_behind(value, "batch", 1)

    def over_cores(value):
        return swap_by(value, "wide", 1)

    def over_pairs(value):
        return swap_by(value, "wide", 2)

    def along(value):
        return hand_along(value, "wide")

    together = lax.optimization_barrier
    sends_near = ((wide_index ^ (wide_index >> 1)) & 1) == 0
    energies = jnp.concatenate([kappas, occ_energy])
    flat_ints = integrals.reshape(aux_local * occ_count, basis)
    transformed = jnp.dot(flat_ints, vir_coeff, preferred_element_type=jnp.float32).astype(
        jnp.bfloat16
    )
    own, sends_near, vir_rows, place, energies = together(
        (
            to_owner(transformed.reshape(aux_local, occ_count, vir_local)),
            sends_near,
            vir_rows,
            place,
            energies,
        )
    )

    def for_sibling(near, far):
        return over_cores(
            jnp.concatenate([jnp.where(sends_near, *pair) for pair in zip(near, far)], axis=1)
        )

    cut = vir_local // 2
    sibling = over_cores(own)
    low, high = cut_in_two(own)
    step = functools.partial(add_terms, place, energies, vir_rows, kappas.shape[0])

    own_o_high = over_batch(high)
    near_low = over_pairs(low)
    *made, density = step(None, [("own", 0, 0, low), ("own", 0, cut, high)], None, (8, 512))
    step = functools.partial(step, made)

    low, high, density = together((low, high, density))
    own_o_low = over_batch(low)
    near_high = over_pairs(high)
    density = step([("sibling", 0, 0, sibling)], density, (8, 512))

    near_low, own_o_high, density = together((near_low, own_o_high, density))
    near_o_high = over_pairs(own_o_high)
    far_low = along(near_low)
    density = step([("own", 1, cut, own_o_high), ("near", 0, 0, near_low)], density, (8, 512))

    own_o_low, own_o_high, near_low, near_high, density = together(
        (own_o_low, own_o_high, near_low, near_high, density)
    )
    far_high = along(near_high)
    near_o_low = over_batch(near_low)
    sibling_o = over_cores(jnp.concatenate([own_o_low, own_o_high], axis=1))
    density = step([("own", 1, 0, own_o_low), ("near", 0, cut, near_high)], density, (8, 512))

    near_o_high, far_low, density = together((near_o_high, far_low, density))
    far_o_high = along(near_o_high)
    far_o_low = over_batch(far_low)
    density = step([("far", 0, 0, far_low), ("near", 1, cut, near_o_high)], density, (8, 512))

    far_low, far_high, near_o_low, density = together((far_low, far_high, near_o_low, density))
    third_low = for_sibling((near_low,), (far_low,))
    third_high = for_sibling((near_high,), (far_high,))
    density = step(
        [("near", 1, 0, near_o_low), ("far", 0, cut, far_high), ("sibling", 1, 0, sibling_o)],
        density,
        (2, 512),
    )

    far_o_high, far_o_low, density = together((far_o_high, far_o_low, density))
    third_o_low = for_sibling((near_o_low,), (far_o_low,))
    third_o_high = for_sibling((near_o_high,), (far_o_high,))
    *held, _ = together((*made, density))
    ready = amplitudes_of(held, [("third", 0, 0, third_low), ("third", 0, cut, third_high)])
    return step(
        [
            ("far", 1, 0, far_o_low),
            ("far", 1, cut, far_o_high),
            ("third", 1, 0, third_o_low),
            ("third", 1, cut, third_o_high),
        ],
        density,
        (2, 512),
        (ready, third_low, third_high),
    )


def pair_density(own_slice, partner, own_energy, partner_energy, row_energy, vir_energy, kappas):
    coulomb = lax.dot_general(
        own_slice, partner, (((0,), (0,)), ((), ())), preferred_element_type=jnp.float32
    )
    denominator = row_energy[:, None] + vir_energy[None, :] - own_energy - partner_energy
    damping = 1.0 - jnp.exp(-kappas[:, None, None] * denominator[None])
    amplitude = (-coulomb[None] * (damping * damping) / denominator[None]).astype(jnp.bfloat16)
    flat = amplitude.reshape(-1, amplitude.shape[2])
    density = lax.dot_general(
        flat, partner, (((1,), (1,)), ((), ())), preferred_element_type=jnp.float32
    )
    return density.reshape(kappas.shape[0], own_slice.shape[1], partner.shape[0])


def ring_terms(integrals, vir_coeff, occ_energy, vir_energy, kappas):
    aux_local, occ_count, basis = integrals.shape
    vir_local = vir_coeff.shape[1]
    batch_index = lax.axis_index("batch")
    wide_index = lax.axis_index("wide")
    flat_ints = integrals.reshape(aux_local * occ_count, basis)
    row_energy = lax.dynamic_slice_in_dim(vir_energy, batch_index * vir_local, vir_local, 0)
    own_energy = lax.dynamic_slice_in_dim(occ_energy, wide_index, 1, 0)[0]

    def term(partner, offset, own_slice):
        partner_index = (wide_index + offset) % occ_count
        partner_energy = lax.dynamic_slice_in_dim(occ_energy, partner_index, 1, 0)[0]
        return pair_density(
            own_slice, partner, own_energy, partner_energy, row_energy, vir_energy, kappas
        )

    transformed = jnp.dot(flat_ints, vir_coeff, preferred_element_type=jnp.float32).astype(
        jnp.bfloat16
    )
    transformed = transformed.reshape(aux_local, occ_count, vir_local)
    own_slice = lax.all_to_all(transformed, "wide", split_axis=1, concat_axis=0, tiled=True)[
        :, 0, :
    ]
    own_full = lax.all_gather(own_slice, "batch", axis=1, tiled=True)
    density = term(own_full, 0, own_slice)
    upper = own_full
    lower = own_full
    for offset in range(1, HALF + 1):
        upper = from_behind(upper, "wide", -1)
        lower = from_behind(lower, "wide", 1)
        density = density + term(upper, offset, own_slice) + term(lower, -offset, own_slice)
    return density.astype(jnp.bfloat16)[:, None, :, :]


def solution(mesh):
    paired = mesh.shape["batch"] == 2 and mesh.shape["wide"] % 4 == 0

    return jax.shard_map(
        pair_terms if paired else ring_terms,
        mesh=mesh,
        in_specs=(P("wide", None, None), P(None, "batch"), P(), P(), P()),
        out_specs=P(None, "wide", "batch", None),
        check_vma=False,
    )
```

```python
import functools

import jax
import jax.numpy as jnp
from jax import lax
from jax.experimental import pallas as pl
from jax.experimental.pallas import tpu as pltpu
from jax.sharding import PartitionSpec as P

HALF = 2
PARTNERS = ("own", "sibling", "third", "near", "far")
VMEM_LIMIT = 18 * 1024 * 1024
LANES = 128


def from_behind(shard, axis, by):
    peers = lax.axis_size(axis)
    return lax.ppermute(shard, axis, [(i, (i + by) % peers) for i in range(peers)])


def swap_by(shard, axis, bit):
    peers = lax.axis_size(axis)
    return lax.ppermute(shard, axis, [(i, i ^ bit) for i in range(peers)])


def hand_along(shard, axis):
    peers = lax.axis_size(axis)
    return lax.ppermute(
        shard,
        axis,
        [(i, (i + (4 if i // 2 % 2 == 0 else -4)) % peers) for i in range(peers)],
    )


def cut_kernel(own, low, high):
    cut = low.shape[1]
    low[...] = own[:, :cut]
    high[...] = own[:, cut:]


def cut_in_two(own):
    vmem = pl.BlockSpec(memory_space=pltpu.VMEM)
    half = jax.ShapeDtypeStruct((own.shape[0], own.shape[1] // 2), own.dtype)
    return pl.pallas_call(
        cut_kernel,
        out_shape=(half, half),
        in_specs=[vmem],
        out_specs=(vmem, vmem),
        compiler_params=pltpu.CompilerParams(vmem_limit_bytes=VMEM_LIMIT),
        cost_estimate=pl.CostEstimate(flops=1, bytes_accessed=1, transcendentals=0),
    )(own)


def make_tables(place, energies, vir_rows, own_low, own_high, made):
    own_t, row_energies, row_factors, column_energies, column_factors = made
    nkap, rows = row_factors.shape[0], own_t.shape[0]
    orbital, half, count = place[0], place[1], place[2]
    core_sign = 1 - 2 * lax.rem(orbital, 2)
    pair_sign = 1 - 2 * lax.rem(lax.div(orbital, 2), 2)
    offsets = dict(
        own=0, sibling=core_sign, third=-core_sign, near=HALF * pair_sign, far=-HALF * pair_sign
    )

    def down_columns(row):
        return jnp.transpose(jnp.broadcast_to(row, (LANES, rows)))

    own_t[:rows // 2, :] = jnp.transpose(own_low[...])
    own_t[rows // 2:, :] = jnp.transpose(own_high[...])
    row_energy = vir_rows[pl.ds(half, 1), :] - energies[nkap + orbital]
    row_energies[...] = down_columns(row_energy)
    for q in range(nkap):
        row_factors[q] = down_columns(jnp.exp(-energies[q] * row_energy))
    for row, name in enumerate(PARTNERS):
        index = lax.rem(orbital + offsets[name] + count, count)
        for other in range(2):
            energy = vir_rows[pl.ds(lax.rem(half + other, 2), 1), :] - energies[nkap + index]
            at = slice(2 * row + other, 2 * row + other + 1)
            column_energies[at, :] = energy
            for q in range(nkap):
                column_factors[q, at, :] = jnp.exp(-energies[q] * energy)


def terms_kernel(pieces, mode, shape, *refs):
    if mode == "first":
        place, energies, vir_rows = refs[:3]
        partners = refs[3:3 + len(pieces)]
        *made, out, amp, ratio = refs[3 + len(pieces):]
        make_tables(place, energies, vir_rows, partners[0], partners[1], made)
    else:
        made = refs[:5]
        partners = refs[5:5 + len(pieces)]
        partial, *refs = refs[5 + len(pieces):]
        if mode == "last":
            result, amp, ratio, out, sems = refs
        else:
            out, amp, ratio = refs
    own_t, row_energies, row_factors, column_energies, column_factors = made
    group_size, p_tile = shape
    nkap, rows = row_factors.shape[0], row_factors.shape[1]
    naux = own_t.shape[1]

    columns_at = []
    for (name, other, start), partner in zip(pieces, partners):
        row = 2 * PARTNERS.index(name) + other
        for c in range(start, start + partner.shape[1], LANES):
            columns_at.append((slice(row, row + 1), slice(c, c + LANES)))
    width = LANES * len(columns_at)

    def partner_columns(tile):
        return jnp.concatenate([partner[tile, :] for partner in partners], axis=1)

    for at in range(0, width, 2 * LANES):
        columns = partner_columns(slice(None))[:, at:at + 2 * LANES]
        coulomb = jnp.dot(own_t[...], columns, preferred_element_type=jnp.float32)
        for c in range(0, columns.shape[1], LANES):
            ratio[:, at + c:at + c + LANES] = -coulomb[:, c:c + LANES] / (
                row_energies[...] + column_energies[columns_at[(at + c) // LANES]]
            )

    copies = []
    for group in range(0, nkap, group_size):
        top, bottom = group * rows, (group + group_size) * rows
        for q in range(group, group + group_size):
            for position, (row, lanes) in enumerate(columns_at):
                columns = slice(position * LANES, (position + 1) * LANES)
                damping = 1.0 - row_factors[q] * column_factors[q, row, lanes]
                amp[q * rows:(q + 1) * rows, columns] = (
                    ratio[:, columns] * damping * damping
                ).astype(amp.dtype)
        span = slice(group, group + group_size)
        for start in range(0, naux, p_tile):
            tile = slice(start, start + p_tile)
            value = lax.dot_general(
                amp[top:bottom, :],
                partner_columns(tile),
                (((1,), (1,)), ((), ())),
                preferred_element_type=jnp.float32,
            ).reshape(group_size, rows, p_tile)
            if mode != "first":
                value = value + partial[span, :, tile]
            out[span, :, tile] = value.astype(out.dtype)
            if mode == "last":
                copy = pltpu.make_async_copy(
                    out.at[span, :, tile], result.at[span, 0, :, tile], sems.at[len(copies)]
                )
                copy.start()
                copies.append(copy)
    for copy in copies:
        copy.wait()


def add_terms(place, energies, vir_rows, nkap, made, partners, partial, shape, last=False):
    pieces = tuple(partner[:3] for partner in partners)
    arrays = [partner[3] for partner in partners]
    naux = arrays[0].shape[0]
    rows = vir_rows.shape[1]
    width = sum(array.shape[1] for array in arrays)
    vmem = pl.BlockSpec(memory_space=pltpu.VMEM)
    smem = pl.BlockSpec(memory_space=pltpu.SMEM)
    density = jax.ShapeDtypeStruct((nkap, rows, naux), jnp.float32)
    scratch = [
        pltpu.VMEM((nkap * rows, width), jnp.bfloat16),
        pltpu.VMEM((rows, width), jnp.float32),
    ]
    aliases = {}
    if made is None:
        mode = "first"
        operands = [place, energies, vir_rows] + arrays
        in_specs = [smem, smem] + [vmem] * (1 + len(arrays))
        out_shape = (
            jax.ShapeDtypeStruct((rows, naux), arrays[0].dtype),
            jax.ShapeDtypeStruct((rows, LANES), jnp.float32),
            jax.ShapeDtypeStruct((nkap, rows, LANES), jnp.float32),
            jax.ShapeDtypeStruct((2 * len(PARTNERS), rows), jnp.float32),
            jax.ShapeDtypeStruct((nkap, 2 * len(PARTNERS), rows), jnp.float32),
            density,
        )
        out_specs = (vmem,) * 6
    else:
        mode = "last" if last else "middle"
        operands = list(made) + arrays + [partial]
        in_specs = [vmem] * len(operands)
        if last:
            out_shape = jax.ShapeDtypeStruct((nkap, 1, rows, naux), jnp.bfloat16)
            out_specs = pl.BlockSpec(memory_space=pl.ANY)
            scratch.append(pltpu.VMEM((nkap, rows, naux), jnp.bfloat16))
            scratch.append(pltpu.SemaphoreType.DMA((nkap // shape[0] * (naux // shape[1]),)))
        else:
            out_shape, out_specs = density, vmem
            aliases = {len(operands) - 1: 0}
    return pl.pallas_call(
        functools.partial(terms_kernel, pieces, mode, shape),
        out_shape=out_shape,
        input_output_aliases=aliases,
        in_specs=in_specs,
        out_specs=out_specs,
        scratch_shapes=scratch,
        compiler_params=pltpu.CompilerParams(vmem_limit_bytes=VMEM_LIMIT),
        cost_estimate=pl.CostEstimate(flops=1, bytes_accessed=1, transcendentals=0),
    )(*operands)


def pair_terms(integrals, vir_coeff, occ_energy, vir_energy, kappas):
    aux_local, occ_count, basis = integrals.shape
    vir_local = vir_coeff.shape[1]
    wide_index = lax.axis_index("wide")
    batch_index = lax.axis_index("batch")
    place = jnp.stack(
        [wide_index, batch_index, jnp.full((), occ_count, wide_index.dtype)]
    ).astype(jnp.int32)
    vir_rows = vir_energy.reshape(-1, vir_local)
    def to_owner(columns):
        return lax.all_to_all(columns, "wide", split_axis=1, concat_axis=0, tiled=True)[:, 0, :]

    def over_batch(value):
        return from_behind(value, "batch", 1)

    def over_cores(value):
        return swap_by(value, "wide", 1)

    def over_pairs(value):
        return swap_by(value, "wide", 2)

    def along(value):
        return hand_along(value, "wide")

    together = lax.optimization_barrier
    sends_near = ((wide_index ^ (wide_index >> 1)) & 1) == 0
    energies = jnp.concatenate([kappas, occ_energy])
    flat_ints = integrals.reshape(aux_local * occ_count, basis)
    transformed = jnp.dot(flat_ints, vir_coeff, preferred_element_type=jnp.float32).astype(
        jnp.bfloat16
    )
    own, sends_near, vir_rows, place, energies = together(
        (
            to_owner(transformed.reshape(aux_local, occ_count, vir_local)),
            sends_near,
            vir_rows,
            place,
            energies,
        )
    )

    def for_sibling(near, far):
        return over_cores(
            jnp.concatenate([jnp.where(sends_near, *pair) for pair in zip(near, far)], axis=1)
        )

    cut = vir_local // 2
    sibling = over_cores(own)
    low, high = cut_in_two(own)
    step = functools.partial(add_terms, place, energies, vir_rows, kappas.shape[0])

    own_o_high = over_batch(high)
    near_low = over_pairs(low)
    *made, density = step(None, [("own", 0, 0, low), ("own", 0, cut, high)], None, (8, 512))
    step = functools.partial(step, made)

    low, high, density = together((low, high, density))
    own_o_low = over_batch(low)
    near_high = over_pairs(high)
    density = step([("sibling", 0, 0, sibling)], density, (8, 512))

    near_low, own_o_high, density = together((near_low, own_o_high, density))
    near_o_high = over_pairs(own_o_high)
    far_low = along(near_low)
    density = step([("own", 1, cut, own_o_high), ("near", 0, 0, near_low)], density, (8, 512))

    own_o_low, own_o_high, near_low, near_high, density = together(
        (own_o_low, own_o_high, near_low, near_high, density)
    )
    far_high = along(near_high)
    near_o_low = over_batch(near_low)
    sibling_o = over_cores(jnp.concatenate([own_o_low, own_o_high], axis=1))
    density = step([("own", 1, 0, own_o_low), ("near", 0, cut, near_high)], density, (8, 512))

    near_o_high, far_low, density = together((near_o_high, far_low, density))
    far_o_high = along(near_o_high)
    far_o_low = over_batch(far_low)
    density = step([("far", 0, 0, far_low), ("near", 1, cut, near_o_high)], density, (8, 512))

    far_low, far_high, near_o_low, density = together((far_low, far_high, near_o_low, density))
    third_low = for_sibling((near_low,), (far_low,))
    third_high = for_sibling((near_high,), (far_high,))
    density = step(
        [("near", 1, 0, near_o_low), ("far", 0, cut, far_high), ("sibling", 1, 0, sibling_o)],
        density,
        (1, 1536),
    )

    far_o_high, far_o_low, density = together((far_o_high, far_o_low, density))
    third_o_low = for_sibling((near_o_low,), (far_o_low,))
    third_o_high = for_sibling((near_o_high,), (far_o_high,))
    return step(
        [
            ("third", 0, 0, third_low),
            ("third", 0, cut, third_high),
            ("far", 1, 0, far_o_low),
            ("far", 1, cut, far_o_high),
            ("third", 1, 0, third_o_low),
            ("third", 1, cut, third_o_high),
        ],
        density,
        (1, 512),
        last=True,
    )


def pair_density(own_slice, partner, own_energy, partner_energy, row_energy, vir_energy, kappas):
    coulomb = lax.dot_general(
        own_slice, partner, (((0,), (0,)), ((), ())), preferred_element_type=jnp.float32
    )
    denominator = row_energy[:, None] + vir_energy[None, :] - own_energy - partner_energy
    damping = 1.0 - jnp.exp(-kappas[:, None, None] * denominator[None])
    amplitude = (-coulomb[None] * (damping * damping) / denominator[None]).astype(jnp.bfloat16)
    flat = amplitude.reshape(-1, amplitude.shape[2])
    density = lax.dot_general(
        flat, partner, (((1,), (1,)), ((), ())), preferred_element_type=jnp.float32
    )
    return density.reshape(kappas.shape[0], own_slice.shape[1], partner.shape[0])


def ring_terms(integrals, vir_coeff, occ_energy, vir_energy, kappas):
    aux_local, occ_count, basis = integrals.shape
    vir_local = vir_coeff.shape[1]
    batch_index = lax.axis_index("batch")
    wide_index = lax.axis_index("wide")
    flat_ints = integrals.reshape(aux_local * occ_count, basis)
    row_energy = lax.dynamic_slice_in_dim(vir_energy, batch_index * vir_local, vir_local, 0)
    own_energy = lax.dynamic_slice_in_dim(occ_energy, wide_index, 1, 0)[0]

    def term(partner, offset, own_slice):
        partner_index = (wide_index + offset) % occ_count
        partner_energy = lax.dynamic_slice_in_dim(occ_energy, partner_index, 1, 0)[0]
        return pair_density(
            own_slice, partner, own_energy, partner_energy, row_energy, vir_energy, kappas
        )

    transformed = jnp.dot(flat_ints, vir_coeff, preferred_element_type=jnp.float32).astype(
        jnp.bfloat16
    )
    transformed = transformed.reshape(aux_local, occ_count, vir_local)
    own_slice = lax.all_to_all(transformed, "wide", split_axis=1, concat_axis=0, tiled=True)[
        :, 0, :
    ]
    own_full = lax.all_gather(own_slice, "batch", axis=1, tiled=True)
    density = term(own_full, 0, own_slice)
    upper = own_full
    lower = own_full
    for offset in range(1, HALF + 1):
        upper = from_behind(upper, "wide", -1)
        lower = from_behind(lower, "wide", 1)
        density = density + term(upper, offset, own_slice) + term(lower, -offset, own_slice)
    return density.astype(jnp.bfloat16)[:, None, :, :]


def solution(mesh):
    paired = mesh.shape["batch"] == 2 and mesh.shape["wide"] % 4 == 0

    return jax.shard_map(
        pair_terms if paired else ring_terms,
        mesh=mesh,
        in_specs=(P("wide", None, None), P(None, "batch"), P(), P(), P()),
        out_specs=P(None, "wide", "batch", None),
        check_vma=False,
    )
```

```python
import functools

import jax
import jax.numpy as jnp
from jax import lax
from jax.experimental import pallas as pl
from jax.experimental.pallas import tpu as pltpu
from jax.sharding import PartitionSpec as P

HALF = 2
PARTNERS = ("own", "sibling", "third", "near", "far")
VMEM_LIMIT = 18 * 1024 * 1024
LANES = 128


def from_behind(shard, axis, by):
    peers = lax.axis_size(axis)
    return lax.ppermute(shard, axis, [(i, (i + by) % peers) for i in range(peers)])


def swap_by(shard, axis, bit):
    peers = lax.axis_size(axis)
    return lax.ppermute(shard, axis, [(i, i ^ bit) for i in range(peers)])


def hand_along(shard, axis):
    peers = lax.axis_size(axis)
    return lax.ppermute(
        shard,
        axis,
        [(i, (i + (4 if i // 2 % 2 == 0 else -4)) % peers) for i in range(peers)],
    )


def cut_kernel(own, low, high):
    cut = low.shape[1]
    low[...] = own[:, :cut]
    high[...] = own[:, cut:]


def cut_in_two(own):
    vmem = pl.BlockSpec(memory_space=pltpu.VMEM)
    half = jax.ShapeDtypeStruct((own.shape[0], own.shape[1] // 2), own.dtype)
    return pl.pallas_call(
        cut_kernel,
        out_shape=(half, half),
        in_specs=[vmem],
        out_specs=(vmem, vmem),
        compiler_params=pltpu.CompilerParams(vmem_limit_bytes=VMEM_LIMIT),
        cost_estimate=pl.CostEstimate(flops=1, bytes_accessed=1, transcendentals=0),
    )(own)


def make_tables(place, energies, vir_rows, own_low, own_high, made):
    own_t, row_energies, row_factors, column_energies, column_factors = made
    nkap, rows = row_factors.shape[0], own_t.shape[0]
    orbital, half, count = place[0], place[1], place[2]
    core_sign = 1 - 2 * lax.rem(orbital, 2)
    pair_sign = 1 - 2 * lax.rem(lax.div(orbital, 2), 2)
    offsets = dict(
        own=0, sibling=core_sign, third=-core_sign, near=HALF * pair_sign, far=-HALF * pair_sign
    )

    def down_columns(row):
        return jnp.transpose(jnp.broadcast_to(row, (LANES, rows)))

    own_t[:rows // 2, :] = jnp.transpose(own_low[...])
    own_t[rows // 2:, :] = jnp.transpose(own_high[...])
    row_energy = vir_rows[pl.ds(half, 1), :] - energies[nkap + orbital]
    row_energies[...] = down_columns(row_energy)
    for q in range(nkap):
        row_factors[q] = down_columns(jnp.exp(-energies[q] * row_energy))
    for row, name in enumerate(PARTNERS):
        index = lax.rem(orbital + offsets[name] + count, count)
        for other in range(2):
            energy = vir_rows[pl.ds(lax.rem(half + other, 2), 1), :] - energies[nkap + index]
            at = slice(2 * row + other, 2 * row + other + 1)
            column_energies[at, :] = energy
            for q in range(nkap):
                column_factors[q, at, :] = jnp.exp(-energies[q] * energy)


def terms_kernel(pieces, mode, shape, *refs):
    if mode == "first":
        place, energies, vir_rows = refs[:3]
        partners = refs[3:3 + len(pieces)]
        *made, out, amp, ratio = refs[3 + len(pieces):]
        make_tables(place, energies, vir_rows, partners[0], partners[1], made)
    else:
        made = refs[:5]
        partners = refs[5:5 + len(pieces)]
        partial, *refs = refs[5 + len(pieces):]
        if mode == "last":
            result, amp, ratio, out, sems = refs
        else:
            out, amp, ratio = refs
    own_t, row_energies, row_factors, column_energies, column_factors = made
    group_size, p_tile = shape
    nkap, rows = row_factors.shape[0], row_factors.shape[1]
    naux = own_t.shape[1]

    columns_at = []
    for (name, other, start), partner in zip(pieces, partners):
        row = 2 * PARTNERS.index(name) + other
        for c in range(start, start + partner.shape[1], LANES):
            columns_at.append((slice(row, row + 1), slice(c, c + LANES)))
    width = LANES * len(columns_at)

    def partner_columns(tile):
        return jnp.concatenate([partner[tile, :] for partner in partners], axis=1)

    for at in range(0, width, 2 * LANES):
        columns = partner_columns(slice(None))[:, at:at + 2 * LANES]
        coulomb = jnp.dot(own_t[...], columns, preferred_element_type=jnp.float32)
        for c in range(0, columns.shape[1], LANES):
            ratio[:, at + c:at + c + LANES] = -coulomb[:, c:c + LANES] / (
                row_energies[...] + column_energies[columns_at[(at + c) // LANES]]
            )

    copies = []
    for group in range(0, nkap, group_size):
        top, bottom = group * rows, (group + group_size) * rows
        for q in range(group, group + group_size):
            for position, (row, lanes) in enumerate(columns_at):
                columns = slice(position * LANES, (position + 1) * LANES)
                damping = 1.0 - row_factors[q] * column_factors[q, row, lanes]
                amp[q * rows:(q + 1) * rows, columns] = (
                    ratio[:, columns] * damping * damping
                ).astype(amp.dtype)
        span = slice(group, group + group_size)
        for start in range(0, naux, p_tile):
            tile = slice(start, start + p_tile)
            value = lax.dot_general(
                amp[top:bottom, :],
                partner_columns(tile),
                (((1,), (1,)), ((), ())),
                preferred_element_type=jnp.float32,
            ).reshape(group_size, rows, p_tile)
            if mode != "first":
                value = value + partial[span, :, tile]
            out[span, :, tile] = value.astype(out.dtype)
            if mode == "last":
                copy = pltpu.make_async_copy(
                    out.at[span, :, tile], result.at[span, 0, :, tile], sems.at[len(copies)]
                )
                copy.start()
                copies.append(copy)
    for copy in copies:
        copy.wait()


def add_terms(place, energies, vir_rows, nkap, made, partners, partial, shape, last=False):
    pieces = tuple(partner[:3] for partner in partners)
    arrays = [partner[3] for partner in partners]
    naux = arrays[0].shape[0]
    rows = vir_rows.shape[1]
    width = sum(array.shape[1] for array in arrays)
    vmem = pl.BlockSpec(memory_space=pltpu.VMEM)
    smem = pl.BlockSpec(memory_space=pltpu.SMEM)
    density = jax.ShapeDtypeStruct((nkap, rows, naux), jnp.float32)
    scratch = [
        pltpu.VMEM((nkap * rows, width), jnp.bfloat16),
        pltpu.VMEM((rows, width), jnp.float32),
    ]
    aliases = {}
    if made is None:
        mode = "first"
        operands = [place, energies, vir_rows] + arrays
        in_specs = [smem, smem] + [vmem] * (1 + len(arrays))
        out_shape = (
            jax.ShapeDtypeStruct((rows, naux), arrays[0].dtype),
            jax.ShapeDtypeStruct((rows, LANES), jnp.float32),
            jax.ShapeDtypeStruct((nkap, rows, LANES), jnp.float32),
            jax.ShapeDtypeStruct((2 * len(PARTNERS), rows), jnp.float32),
            jax.ShapeDtypeStruct((nkap, 2 * len(PARTNERS), rows), jnp.float32),
            density,
        )
        out_specs = (vmem,) * 6
    else:
        mode = "last" if last else "middle"
        operands = list(made) + arrays + [partial]
        in_specs = [vmem] * len(operands)
        if last:
            out_shape = jax.ShapeDtypeStruct((nkap, 1, rows, naux), jnp.bfloat16)
            out_specs = pl.BlockSpec(memory_space=pl.ANY)
            scratch.append(pltpu.VMEM((nkap, rows, naux), jnp.bfloat16))
            scratch.append(pltpu.SemaphoreType.DMA((nkap // shape[0] * (naux // shape[1]),)))
        else:
            out_shape, out_specs = density, vmem
            aliases = {len(operands) - 1: 0}
    return pl.pallas_call(
        functools.partial(terms_kernel, pieces, mode, shape),
        out_shape=out_shape,
        input_output_aliases=aliases,
        in_specs=in_specs,
        out_specs=out_specs,
        scratch_shapes=scratch,
        compiler_params=pltpu.CompilerParams(vmem_limit_bytes=VMEM_LIMIT),
        cost_estimate=pl.CostEstimate(flops=1, bytes_accessed=1, transcendentals=0),
    )(*operands)


def pair_terms(integrals, vir_coeff, occ_energy, vir_energy, kappas):
    aux_local, occ_count, basis = integrals.shape
    vir_local = vir_coeff.shape[1]
    wide_index = lax.axis_index("wide")
    batch_index = lax.axis_index("batch")
    place = jnp.stack(
        [wide_index, batch_index, jnp.full((), occ_count, wide_index.dtype)]
    ).astype(jnp.int32)
    vir_rows = vir_energy.reshape(-1, vir_local)
    def to_owner(columns):
        return lax.all_to_all(columns, "wide", split_axis=1, concat_axis=0, tiled=True)[:, 0, :]

    def over_batch(value):
        return from_behind(value, "batch", 1)

    def over_cores(value):
        return swap_by(value, "wide", 1)

    def over_pairs(value):
        return swap_by(value, "wide", 2)

    def along(value):
        return hand_along(value, "wide")

    together = lax.optimization_barrier
    sends_near = ((wide_index ^ (wide_index >> 1)) & 1) == 0
    energies = jnp.concatenate([kappas, occ_energy])
    flat_ints = integrals.reshape(aux_local * occ_count, basis)
    transformed = jnp.dot(flat_ints, vir_coeff, preferred_element_type=jnp.float32).astype(
        jnp.bfloat16
    )
    own, sends_near, vir_rows, place, energies = together(
        (
            to_owner(transformed.reshape(aux_local, occ_count, vir_local)),
            sends_near,
            vir_rows,
            place,
            energies,
        )
    )

    def for_sibling(near, far):
        return over_cores(
            jnp.concatenate([jnp.where(sends_near, *pair) for pair in zip(near, far)], axis=1)
        )

    cut = vir_local // 2
    sibling = over_cores(own)
    low, high = cut_in_two(own)
    step = functools.partial(add_terms, place, energies, vir_rows, kappas.shape[0])

    own_o_high = over_batch(high)
    near_low = over_pairs(low)
    *made, density = step(None, [("own", 0, 0, low), ("own", 0, cut, high)], None, (8, 512))
    step = functools.partial(step, made)

    low, high, density = together((low, high, density))
    own_o_low = over_batch(low)
    near_high = over_pairs(high)
    density = step([("sibling", 0, 0, sibling)], density, (8, 512))

    near_low, own_o_high, density = together((near_low, own_o_high, density))
    near_o_high = over_pairs(own_o_high)
    far_low = along(near_low)
    density = step([("own", 1, cut, own_o_high), ("near", 0, 0, near_low)], density, (8, 512))

    own_o_low, own_o_high, near_low, near_high, density = together(
        (own_o_low, own_o_high, near_low, near_high, density)
    )
    far_high = along(near_high)
    near_o_low = over_batch(near_low)
    sibling_o = over_cores(jnp.concatenate([own_o_low, own_o_high], axis=1))
    density = step([("own", 1, 0, own_o_low), ("near", 0, cut, near_high)], density, (8, 512))

    near_o_high, far_low, density = together((near_o_high, far_low, density))
    far_o_high = along(near_o_high)
    far_o_low = over_batch(far_low)
    density = step([("far", 0, 0, far_low), ("near", 1, cut, near_o_high)], density, (8, 512))

    far_low, far_high, near_o_low, density = together((far_low, far_high, near_o_low, density))
    third_low = for_sibling((near_low,), (far_low,))
    third_high = for_sibling((near_high,), (far_high,))
    density = step(
        [("near", 1, 0, near_o_low), ("far", 0, cut, far_high), ("sibling", 1, 0, sibling_o)],
        density,
        (2, 512),
    )

    far_o_high, far_o_low, density = together((far_o_high, far_o_low, density))
    third_o_low = for_sibling((near_o_low,), (far_o_low,))
    third_o_high = for_sibling((near_o_high,), (far_o_high,))
    density = step(
        [("third", 0, 0, third_low), ("third", 0, cut, third_high)], density, (8, 512)
    )
    return step(
        [
            ("far", 1, 0, far_o_low),
            ("far", 1, cut, far_o_high),
            ("third", 1, 0, third_o_low),
            ("third", 1, cut, third_o_high),
        ],
        density,
        (2, 512),
        last=True,
    )


def pair_density(own_slice, partner, own_energy, partner_energy, row_energy, vir_energy, kappas):
    coulomb = lax.dot_general(
        own_slice, partner, (((0,), (0,)), ((), ())), preferred_element_type=jnp.float32
    )
    denominator = row_energy[:, None] + vir_energy[None, :] - own_energy - partner_energy
    damping = 1.0 - jnp.exp(-kappas[:, None, None] * denominator[None])
    amplitude = (-coulomb[None] * (damping * damping) / denominator[None]).astype(jnp.bfloat16)
    flat = amplitude.reshape(-1, amplitude.shape[2])
    density = lax.dot_general(
        flat, partner, (((1,), (1,)), ((), ())), preferred_element_type=jnp.float32
    )
    return density.reshape(kappas.shape[0], own_slice.shape[1], partner.shape[0])


def ring_terms(integrals, vir_coeff, occ_energy, vir_energy, kappas):
    aux_local, occ_count, basis = integrals.shape
    vir_local = vir_coeff.shape[1]
    batch_index = lax.axis_index("batch")
    wide_index = lax.axis_index("wide")
    flat_ints = integrals.reshape(aux_local * occ_count, basis)
    row_energy = lax.dynamic_slice_in_dim(vir_energy, batch_index * vir_local, vir_local, 0)
    own_energy = lax.dynamic_slice_in_dim(occ_energy, wide_index, 1, 0)[0]

    def term(partner, offset, own_slice):
        partner_index = (wide_index + offset) % occ_count
        partner_energy = lax.dynamic_slice_in_dim(occ_energy, partner_index, 1, 0)[0]
        return pair_density(
            own_slice, partner, own_energy, partner_energy, row_energy, vir_energy, kappas
        )

    transformed = jnp.dot(flat_ints, vir_coeff, preferred_element_type=jnp.float32).astype(
        jnp.bfloat16
    )
    transformed = transformed.reshape(aux_local, occ_count, vir_local)
    own_slice = lax.all_to_all(transformed, "wide", split_axis=1, concat_axis=0, tiled=True)[
        :, 0, :
    ]
    own_full = lax.all_gather(own_slice, "batch", axis=1, tiled=True)
    density = term(own_full, 0, own_slice)
    upper = own_full
    lower = own_full
    for offset in range(1, HALF + 1):
        upper = from_behind(upper, "wide", -1)
        lower = from_behind(lower, "wide", 1)
        density = density + term(upper, offset, own_slice) + term(lower, -offset, own_slice)
    return density.astype(jnp.bfloat16)[:, None, :, :]


def solution(mesh):
    paired = mesh.shape["batch"] == 2 and mesh.shape["wide"] % 4 == 0

    return jax.shard_map(
        pair_terms if paired else ring_terms,
        mesh=mesh,
        in_specs=(P("wide", None, None), P(None, "batch"), P(), P(), P()),
        out_specs=P(None, "wide", "batch", None),
        check_vma=False,
    )
```

```python
import functools

import jax
import jax.numpy as jnp
from jax import lax
from jax.experimental import pallas as pl
from jax.experimental.pallas import tpu as pltpu
from jax.sharding import PartitionSpec as P

HALF = 2
PARTNERS = ("own", "sibling", "third", "near", "far")
VMEM_LIMIT = 18 * 1024 * 1024
LANES = 128


def from_behind(shard, axis, by):
    peers = lax.axis_size(axis)
    return lax.ppermute(shard, axis, [(i, (i + by) % peers) for i in range(peers)])


def swap_by(shard, axis, bit):
    peers = lax.axis_size(axis)
    return lax.ppermute(shard, axis, [(i, i ^ bit) for i in range(peers)])


def hand_along(shard, axis):
    peers = lax.axis_size(axis)
    return lax.ppermute(
        shard,
        axis,
        [(i, (i + (4 if i // 2 % 2 == 0 else -4)) % peers) for i in range(peers)],
    )


def cut_kernel(own, low, high):
    cut = low.shape[1]
    low[...] = own[:, :cut]
    high[...] = own[:, cut:]


def cut_in_two(own):
    vmem = pl.BlockSpec(memory_space=pltpu.VMEM)
    half = jax.ShapeDtypeStruct((own.shape[0], own.shape[1] // 2), own.dtype)
    return pl.pallas_call(
        cut_kernel,
        out_shape=(half, half),
        in_specs=[vmem],
        out_specs=(vmem, vmem),
        compiler_params=pltpu.CompilerParams(vmem_limit_bytes=VMEM_LIMIT),
        cost_estimate=pl.CostEstimate(flops=1, bytes_accessed=1, transcendentals=0),
    )(own)


def make_tables(place, energies, vir_rows, own_low, own_high, made):
    own_t, row_energies, row_factors, column_energies, column_factors = made
    nkap, rows = row_factors.shape[0], own_t.shape[0]
    orbital, half, count = place[0], place[1], place[2]
    core_sign = 1 - 2 * lax.rem(orbital, 2)
    pair_sign = 1 - 2 * lax.rem(lax.div(orbital, 2), 2)
    offsets = dict(
        own=0, sibling=core_sign, third=-core_sign, near=HALF * pair_sign, far=-HALF * pair_sign
    )

    def down_columns(row):
        return jnp.transpose(jnp.broadcast_to(row, (LANES, rows)))

    own_t[:rows // 2, :] = jnp.transpose(own_low[...])
    own_t[rows // 2:, :] = jnp.transpose(own_high[...])
    row_energy = vir_rows[pl.ds(half, 1), :] - energies[nkap + orbital]
    row_energies[...] = down_columns(row_energy)
    for q in range(nkap):
        row_factors[q] = down_columns(jnp.exp(-energies[q] * row_energy))
    for row, name in enumerate(PARTNERS):
        index = lax.rem(orbital + offsets[name] + count, count)
        for other in range(2):
            energy = vir_rows[pl.ds(lax.rem(half + other, 2), 1), :] - energies[nkap + index]
            at = slice(2 * row + other, 2 * row + other + 1)
            column_energies[at, :] = energy
            for q in range(nkap):
                column_factors[q, at, :] = jnp.exp(-energies[q] * energy)


def terms_kernel(pieces, mode, shape, *refs):
    if mode == "first":
        place, energies, vir_rows = refs[:3]
        partners = refs[3:3 + len(pieces)]
        *made, out, amp, ratio = refs[3 + len(pieces):]
        make_tables(place, energies, vir_rows, partners[0], partners[1], made)
    else:
        made = refs[:5]
        partners = refs[5:5 + len(pieces)]
        partial, *refs = refs[5 + len(pieces):]
        if mode == "last":
            result, amp, ratio, out, sems = refs
        else:
            out, amp, ratio = refs
    own_t, row_energies, row_factors, column_energies, column_factors = made
    group_size, p_tile = shape
    nkap, rows = row_factors.shape[0], row_factors.shape[1]
    naux = own_t.shape[1]

    columns_at = []
    for (name, other, start), partner in zip(pieces, partners):
        row = 2 * PARTNERS.index(name) + other
        for c in range(start, start + partner.shape[1], LANES):
            columns_at.append((slice(row, row + 1), slice(c, c + LANES)))
    width = LANES * len(columns_at)

    def partner_columns(tile):
        return jnp.concatenate([partner[tile, :] for partner in partners], axis=1)

    for at in range(0, width, 2 * LANES):
        columns = partner_columns(slice(None))[:, at:at + 2 * LANES]
        coulomb = jnp.dot(own_t[...], columns, preferred_element_type=jnp.float32)
        for c in range(0, columns.shape[1], LANES):
            ratio[:, at + c:at + c + LANES] = -coulomb[:, c:c + LANES] / (
                row_energies[...] + column_energies[columns_at[(at + c) // LANES]]
            )

    copies = []
    for group in range(0, nkap, group_size):
        top, bottom = group * rows, (group + group_size) * rows
        for q in range(group, group + group_size):
            for position, (row, lanes) in enumerate(columns_at):
                columns = slice(position * LANES, (position + 1) * LANES)
                damping = 1.0 - row_factors[q] * column_factors[q, row, lanes]
                amp[q * rows:(q + 1) * rows, columns] = (
                    ratio[:, columns] * damping * damping
                ).astype(amp.dtype)
        span = slice(group, group + group_size)
        for start in range(0, naux, p_tile):
            tile = slice(start, start + p_tile)
            value = lax.dot_general(
                amp[top:bottom, :],
                partner_columns(tile),
                (((1,), (1,)), ((), ())),
                preferred_element_type=jnp.float32,
            ).reshape(group_size, rows, p_tile)
            if mode != "first":
                value = value + partial[span, :, tile]
            out[span, :, tile] = value.astype(out.dtype)
            if mode == "last":
                copy = pltpu.make_async_copy(
                    out.at[span, :, tile], result.at[span, 0, :, tile], sems.at[len(copies)]
                )
                copy.start()
                copies.append(copy)
    for copy in copies:
        copy.wait()


def add_terms(place, energies, vir_rows, nkap, made, partners, partial, shape, last=False):
    pieces = tuple(partner[:3] for partner in partners)
    arrays = [partner[3] for partner in partners]
    naux = arrays[0].shape[0]
    rows = vir_rows.shape[1]
    width = sum(array.shape[1] for array in arrays)
    vmem = pl.BlockSpec(memory_space=pltpu.VMEM)
    smem = pl.BlockSpec(memory_space=pltpu.SMEM)
    density = jax.ShapeDtypeStruct((nkap, rows, naux), jnp.float32)
    scratch = [
        pltpu.VMEM((nkap * rows, width), jnp.bfloat16),
        pltpu.VMEM((rows, width), jnp.float32),
    ]
    aliases = {}
    if made is None:
        mode = "first"
        operands = [place, energies, vir_rows] + arrays
        in_specs = [smem, smem] + [vmem] * (1 + len(arrays))
        out_shape = (
            jax.ShapeDtypeStruct((rows, naux), arrays[0].dtype),
            jax.ShapeDtypeStruct((rows, LANES), jnp.float32),
            jax.ShapeDtypeStruct((nkap, rows, LANES), jnp.float32),
            jax.ShapeDtypeStruct((2 * len(PARTNERS), rows), jnp.float32),
            jax.ShapeDtypeStruct((nkap, 2 * len(PARTNERS), rows), jnp.float32),
            density,
        )
        out_specs = (vmem,) * 6
    else:
        mode = "last" if last else "middle"
        operands = list(made) + arrays + [partial]
        in_specs = [vmem] * len(operands)
        if last:
            out_shape = jax.ShapeDtypeStruct((nkap, 1, rows, naux), jnp.bfloat16)
            out_specs = pl.BlockSpec(memory_space=pl.ANY)
            scratch.append(pltpu.VMEM((nkap, rows, naux), jnp.bfloat16))
            scratch.append(pltpu.SemaphoreType.DMA((nkap // shape[0] * (naux // shape[1]),)))
        else:
            out_shape, out_specs = density, vmem
            aliases = {len(operands) - 1: 0}
    return pl.pallas_call(
        functools.partial(terms_kernel, pieces, mode, shape),
        out_shape=out_shape,
        input_output_aliases=aliases,
        in_specs=in_specs,
        out_specs=out_specs,
        scratch_shapes=scratch,
        compiler_params=pltpu.CompilerParams(vmem_limit_bytes=VMEM_LIMIT),
        cost_estimate=pl.CostEstimate(flops=1, bytes_accessed=1, transcendentals=0),
    )(*operands)


def pair_terms(integrals, vir_coeff, occ_energy, vir_energy, kappas):
    aux_local, occ_count, basis = integrals.shape
    vir_local = vir_coeff.shape[1]
    wide_index = lax.axis_index("wide")
    batch_index = lax.axis_index("batch")
    place = jnp.stack(
        [wide_index, batch_index, jnp.full((), occ_count, wide_index.dtype)]
    ).astype(jnp.int32)
    vir_rows = vir_energy.reshape(-1, vir_local)
    def to_owner(columns):
        return lax.all_to_all(columns, "wide", split_axis=1, concat_axis=0, tiled=True)[:, 0, :]

    def over_batch(value):
        return from_behind(value, "batch", 1)

    def over_cores(value):
        return swap_by(value, "wide", 1)

    def over_pairs(value):
        return swap_by(value, "wide", 2)

    def along(value):
        return hand_along(value, "wide")

    together = lax.optimization_barrier
    sends_near = ((wide_index ^ (wide_index >> 1)) & 1) == 0
    energies = jnp.concatenate([kappas, occ_energy])
    flat_ints = integrals.reshape(aux_local * occ_count, basis)
    transformed = jnp.dot(flat_ints, vir_coeff, preferred_element_type=jnp.float32).astype(
        jnp.bfloat16
    )
    own, sends_near, vir_rows, place, energies = together(
        (
            to_owner(transformed.reshape(aux_local, occ_count, vir_local)),
            sends_near,
            vir_rows,
            place,
            energies,
        )
    )

    def for_sibling(near, far):
        return over_cores(
            jnp.concatenate([jnp.where(sends_near, *pair) for pair in zip(near, far)], axis=1)
        )

    cut = vir_local // 2
    sibling = over_cores(own)
    low, high = cut_in_two(own)
    step = functools.partial(add_terms, place, energies, vir_rows, kappas.shape[0])

    own_o_high = over_batch(high)
    near_low = over_pairs(low)
    *made, density = step(None, [("own", 0, 0, low), ("own", 0, cut, high)], None, (8, 512))
    step = functools.partial(step, made)

    low, high, density = together((low, high, density))
    own_o_low = over_batch(low)
    near_high = over_pairs(high)
    density = step([("sibling", 0, 0, sibling)], density, (8, 512))

    near_low, own_o_high, density = together((near_low, own_o_high, density))
    near_o_high = over_pairs(own_o_high)
    far_low = along(near_low)
    density = step([("own", 1, cut, own_o_high), ("near", 0, 0, near_low)], density, (8, 512))

    own_o_low, own_o_high, near_low, near_high, density = together(
        (own_o_low, own_o_high, near_low, near_high, density)
    )
    far_high = along(near_high)
    near_o_low = over_batch(near_low)
    sibling_o = over_cores(jnp.concatenate([own_o_low, own_o_high], axis=1))
    density = step([("own", 1, 0, own_o_low), ("near", 0, cut, near_high)], density, (8, 512))

    near_o_high, far_low, density = together((near_o_high, far_low, density))
    far_o_high = along(near_o_high)
    far_o_low = over_batch(far_low)
    density = step([("far", 0, 0, far_low), ("near", 1, cut, near_o_high)], density, (8, 512))

    near_o_low, far_low, far_high, density = together((near_o_low, far_low, far_high, density))
    third_low = for_sibling((near_low,), (far_low,))
    third_high = for_sibling((near_high,), (far_high,))
    density = step(
        [("near", 1, 0, near_o_low), ("far", 0, cut, far_high), ("sibling", 1, 0, sibling_o)],
        density,
        (2, 512),
    )

    far_o_high, far_o_low, density = together((far_o_high, far_o_low, density))
    third_o_low = for_sibling((near_o_low,), (far_o_low,))
    third_o_high = for_sibling((near_o_high,), (far_o_high,))
    density = step(
        [("third", 0, 0, third_low), ("third", 0, cut, third_high)], density, (8, 512)
    )
    return step(
        [
            ("far", 1, 0, far_o_low),
            ("far", 1, cut, far_o_high),
            ("third", 1, 0, third_o_low),
            ("third", 1, cut, third_o_high),
        ],
        density,
        (2, 512),
        last=True,
    )


def pair_density(own_slice, partner, own_energy, partner_energy, row_energy, vir_energy, kappas):
    coulomb = lax.dot_general(
        own_slice, partner, (((0,), (0,)), ((), ())), preferred_element_type=jnp.float32
    )
    denominator = row_energy[:, None] + vir_energy[None, :] - own_energy - partner_energy
    damping = 1.0 - jnp.exp(-kappas[:, None, None] * denominator[None])
    amplitude = (-coulomb[None] * (damping * damping) / denominator[None]).astype(jnp.bfloat16)
    flat = amplitude.reshape(-1, amplitude.shape[2])
    density = lax.dot_general(
        flat, partner, (((1,), (1,)), ((), ())), preferred_element_type=jnp.float32
    )
    return density.reshape(kappas.shape[0], own_slice.shape[1], partner.shape[0])


def ring_terms(integrals, vir_coeff, occ_energy, vir_energy, kappas):
    aux_local, occ_count, basis = integrals.shape
    vir_local = vir_coeff.shape[1]
    batch_index = lax.axis_index("batch")
    wide_index = lax.axis_index("wide")
    flat_ints = integrals.reshape(aux_local * occ_count, basis)
    row_energy = lax.dynamic_slice_in_dim(vir_energy, batch_index * vir_local, vir_local, 0)
    own_energy = lax.dynamic_slice_in_dim(occ_energy, wide_index, 1, 0)[0]

    def term(partner, offset, own_slice):
        partner_index = (wide_index + offset) % occ_count
        partner_energy = lax.dynamic_slice_in_dim(occ_energy, partner_index, 1, 0)[0]
        return pair_density(
            own_slice, partner, own_energy, partner_energy, row_energy, vir_energy, kappas
        )

    transformed = jnp.dot(flat_ints, vir_coeff, preferred_element_type=jnp.float32).astype(
        jnp.bfloat16
    )
    transformed = transformed.reshape(aux_local, occ_count, vir_local)
    own_slice = lax.all_to_all(transformed, "wide", split_axis=1, concat_axis=0, tiled=True)[
        :, 0, :
    ]
    own_full = lax.all_gather(own_slice, "batch", axis=1, tiled=True)
    density = term(own_full, 0, own_slice)
    upper = own_full
    lower = own_full
    for offset in range(1, HALF + 1):
        upper = from_behind(upper, "wide", -1)
        lower = from_behind(lower, "wide", 1)
        density = density + term(upper, offset, own_slice) + term(lower, -offset, own_slice)
    return density.astype(jnp.bfloat16)[:, None, :, :]


def solution(mesh):
    paired = mesh.shape["batch"] == 2 and mesh.shape["wide"] % 4 == 0

    return jax.shard_map(
        pair_terms if paired else ring_terms,
        mesh=mesh,
        in_specs=(P("wide", None, None), P(None, "batch"), P(), P(), P()),
        out_specs=P(None, "wide", "batch", None),
        check_vma=False,
    )
```

```python
import functools

import jax
import jax.numpy as jnp
from jax import lax
from jax.experimental import pallas as pl
from jax.experimental.pallas import tpu as pltpu
from jax.sharding import PartitionSpec as P

HALF = 2
PARTNERS = ("own", "sibling", "third", "near", "far")
VMEM_LIMIT = 18 * 1024 * 1024
LANES = 128


def from_behind(shard, axis, by):
    peers = lax.axis_size(axis)
    return lax.ppermute(shard, axis, [(i, (i + by) % peers) for i in range(peers)])


def swap_by(shard, axis, bit):
    peers = lax.axis_size(axis)
    return lax.ppermute(shard, axis, [(i, i ^ bit) for i in range(peers)])


def hand_along(shard, axis):
    peers = lax.axis_size(axis)
    return lax.ppermute(
        shard,
        axis,
        [(i, (i + (4 if i // 2 % 2 == 0 else -4)) % peers) for i in range(peers)],
    )


def cut_kernel(own, low, high):
    cut = low.shape[1]
    low[...] = own[:, :cut]
    high[...] = own[:, cut:]


def cut_in_two(own):
    vmem = pl.BlockSpec(memory_space=pltpu.VMEM)
    half = jax.ShapeDtypeStruct((own.shape[0], own.shape[1] // 2), own.dtype)
    return pl.pallas_call(
        cut_kernel,
        out_shape=(half, half),
        in_specs=[vmem],
        out_specs=(vmem, vmem),
        compiler_params=pltpu.CompilerParams(vmem_limit_bytes=VMEM_LIMIT),
        cost_estimate=pl.CostEstimate(flops=1, bytes_accessed=1, transcendentals=0),
    )(own)


def make_tables(place, energies, vir_rows, own_low, own_high, made):
    own_t, row_energies, row_factors, column_energies, column_factors = made
    nkap, rows = row_factors.shape[0], own_t.shape[0]
    orbital, half, count = place[0], place[1], place[2]
    core_sign = 1 - 2 * lax.rem(orbital, 2)
    pair_sign = 1 - 2 * lax.rem(lax.div(orbital, 2), 2)
    offsets = dict(
        own=0, sibling=core_sign, third=-core_sign, near=HALF * pair_sign, far=-HALF * pair_sign
    )

    def down_columns(row):
        return jnp.transpose(jnp.broadcast_to(row, (LANES, rows)))

    own_t[:rows // 2, :] = jnp.transpose(own_low[...])
    own_t[rows // 2:, :] = jnp.transpose(own_high[...])
    row_energy = vir_rows[pl.ds(half, 1), :] - energies[nkap + orbital]
    row_energies[...] = down_columns(row_energy)
    for q in range(nkap):
        row_factors[q] = down_columns(jnp.exp(-energies[q] * row_energy))
    for row, name in enumerate(PARTNERS):
        index = lax.rem(orbital + offsets[name] + count, count)
        for other in range(2):
            energy = vir_rows[pl.ds(lax.rem(half + other, 2), 1), :] - energies[nkap + index]
            at = slice(2 * row + other, 2 * row + other + 1)
            column_energies[at, :] = energy
            for q in range(nkap):
                column_factors[q, at, :] = jnp.exp(-energies[q] * energy)


def terms_kernel(pieces, mode, shape, *refs):
    if mode == "first":
        place, energies, vir_rows = refs[:3]
        partners = refs[3:3 + len(pieces)]
        *made, out, amp, ratio = refs[3 + len(pieces):]
        make_tables(place, energies, vir_rows, partners[0], partners[1], made)
    else:
        made = refs[:5]
        partners = refs[5:5 + len(pieces)]
        partial, *refs = refs[5 + len(pieces):]
        if mode == "last":
            result, amp, ratio, out, sems = refs
        else:
            out, amp, ratio = refs
    own_t, row_energies, row_factors, column_energies, column_factors = made
    group_size, p_tile = shape
    nkap, rows = row_factors.shape[0], row_factors.shape[1]
    naux = own_t.shape[1]

    columns_at = []
    for (name, other, start), partner in zip(pieces, partners):
        row = 2 * PARTNERS.index(name) + other
        for c in range(start, start + partner.shape[1], LANES):
            columns_at.append((slice(row, row + 1), slice(c, c + LANES)))
    width = LANES * len(columns_at)

    def partner_columns(tile):
        return jnp.concatenate([partner[tile, :] for partner in partners], axis=1)

    for at in range(0, width, 2 * LANES):
        columns = partner_columns(slice(None))[:, at:at + 2 * LANES]
        coulomb = jnp.dot(own_t[...], columns, preferred_element_type=jnp.float32)
        for c in range(0, columns.shape[1], LANES):
            ratio[:, at + c:at + c + LANES] = -coulomb[:, c:c + LANES] / (
                row_energies[...] + column_energies[columns_at[(at + c) // LANES]]
            )

    copies = []
    for group in range(0, nkap, group_size):
        top, bottom = group * rows, (group + group_size) * rows
        for q in range(group, group + group_size):
            for position, (row, lanes) in enumerate(columns_at):
                columns = slice(position * LANES, (position + 1) * LANES)
                damping = 1.0 - row_factors[q] * column_factors[q, row, lanes]
                amp[q * rows:(q + 1) * rows, columns] = (
                    ratio[:, columns] * damping * damping
                ).astype(amp.dtype)
        span = slice(group, group + group_size)
        for start in range(0, naux, p_tile):
            tile = slice(start, start + p_tile)
            value = lax.dot_general(
                amp[top:bottom, :],
                partner_columns(tile),
                (((1,), (1,)), ((), ())),
                preferred_element_type=jnp.float32,
            ).reshape(group_size, rows, p_tile)
            if mode != "first":
                value = value + partial[span, :, tile]
            out[span, :, tile] = value.astype(out.dtype)
            if mode == "last":
                copy = pltpu.make_async_copy(
                    out.at[span, :, tile], result.at[span, 0, :, tile], sems.at[len(copies)]
                )
                copy.start()
                copies.append(copy)
    for copy in copies:
        copy.wait()


def add_terms(place, energies, vir_rows, nkap, made, partners, partial, shape, last=False):
    pieces = tuple(partner[:3] for partner in partners)
    arrays = [partner[3] for partner in partners]
    naux = arrays[0].shape[0]
    rows = vir_rows.shape[1]
    width = sum(array.shape[1] for array in arrays)
    vmem = pl.BlockSpec(memory_space=pltpu.VMEM)
    smem = pl.BlockSpec(memory_space=pltpu.SMEM)
    density = jax.ShapeDtypeStruct((nkap, rows, naux), jnp.float32)
    scratch = [
        pltpu.VMEM((nkap * rows, width), jnp.bfloat16),
        pltpu.VMEM((rows, width), jnp.float32),
    ]
    aliases = {}
    if made is None:
        mode = "first"
        operands = [place, energies, vir_rows] + arrays
        in_specs = [smem, smem] + [vmem] * (1 + len(arrays))
        out_shape = (
            jax.ShapeDtypeStruct((rows, naux), arrays[0].dtype),
            jax.ShapeDtypeStruct((rows, LANES), jnp.float32),
            jax.ShapeDtypeStruct((nkap, rows, LANES), jnp.float32),
            jax.ShapeDtypeStruct((2 * len(PARTNERS), rows), jnp.float32),
            jax.ShapeDtypeStruct((nkap, 2 * len(PARTNERS), rows), jnp.float32),
            density,
        )
        out_specs = (vmem,) * 6
    else:
        mode = "last" if last else "middle"
        operands = list(made) + arrays + [partial]
        in_specs = [vmem] * len(operands)
        if last:
            out_shape = jax.ShapeDtypeStruct((nkap, 1, rows, naux), jnp.bfloat16)
            out_specs = pl.BlockSpec(memory_space=pl.ANY)
            scratch.append(pltpu.VMEM((nkap, rows, naux), jnp.bfloat16))
            scratch.append(pltpu.SemaphoreType.DMA((nkap // shape[0] * (naux // shape[1]),)))
        else:
            out_shape, out_specs = density, vmem
            aliases = {len(operands) - 1: 0}
    return pl.pallas_call(
        functools.partial(terms_kernel, pieces, mode, shape),
        out_shape=out_shape,
        input_output_aliases=aliases,
        in_specs=in_specs,
        out_specs=out_specs,
        scratch_shapes=scratch,
        compiler_params=pltpu.CompilerParams(vmem_limit_bytes=VMEM_LIMIT),
        cost_estimate=pl.CostEstimate(flops=1, bytes_accessed=1, transcendentals=0),
    )(*operands)


def pair_terms(integrals, vir_coeff, occ_energy, vir_energy, kappas):
    aux_local, occ_count, basis = integrals.shape
    vir_local = vir_coeff.shape[1]
    wide_index = lax.axis_index("wide")
    batch_index = lax.axis_index("batch")
    place = jnp.stack(
        [wide_index, batch_index, jnp.full((), occ_count, wide_index.dtype)]
    ).astype(jnp.int32)
    vir_rows = vir_energy.reshape(-1, vir_local)
    def to_owner(columns):
        return lax.all_to_all(columns, "wide", split_axis=1, concat_axis=0, tiled=True)[:, 0, :]

    def over_batch(value):
        return from_behind(value, "batch", 1)

    def over_cores(value):
        return swap_by(value, "wide", 1)

    def over_pairs(value):
        return swap_by(value, "wide", 2)

    def along(value):
        return hand_along(value, "wide")

    together = lax.optimization_barrier
    sends_near = ((wide_index ^ (wide_index >> 1)) & 1) == 0
    energies = jnp.concatenate([kappas, occ_energy])
    flat_ints = integrals.reshape(aux_local * occ_count, basis)
    transformed = jnp.dot(flat_ints, vir_coeff, preferred_element_type=jnp.float32).astype(
        jnp.bfloat16
    )
    own, sends_near, vir_rows, place, energies = together(
        (
            to_owner(transformed.reshape(aux_local, occ_count, vir_local)),
            sends_near,
            vir_rows,
            place,
            energies,
        )
    )

    def for_sibling(near, far):
        return over_cores(
            jnp.concatenate([jnp.where(sends_near, *pair) for pair in zip(near, far)], axis=1)
        )

    cut = vir_local // 2
    sibling = over_cores(own)
    low, high = cut_in_two(own)
    step = functools.partial(add_terms, place, energies, vir_rows, kappas.shape[0])

    own_o_high = over_batch(high)
    near_low = over_pairs(low)
    *made, density = step(None, [("own", 0, 0, low), ("own", 0, cut, high)], None, (8, 512))
    step = functools.partial(step, made)

    low, high, density = together((low, high, density))
    own_o_low = over_batch(low)
    near_high = over_pairs(high)
    density = step([("sibling", 0, 0, sibling)], density, (8, 512))

    near_low, own_o_high, density = together((near_low, own_o_high, density))
    near_o_high = over_pairs(own_o_high)
    far_low = along(near_low)
    density = step([("own", 1, cut, own_o_high), ("near", 0, 0, near_low)], density, (8, 512))

    own_o_low, own_o_high, near_low, near_high, density = together(
        (own_o_low, own_o_high, near_low, near_high, density)
    )
    far_high = along(near_high)
    near_o_low = over_batch(near_low)
    sibling_o = over_cores(jnp.concatenate([own_o_low, own_o_high], axis=1))
    density = step([("own", 1, 0, own_o_low), ("near", 0, cut, near_high)], density, (8, 512))

    near_o_high, far_low, density = together((near_o_high, far_low, density))
    far_o_high = along(near_o_high)
    far_o_low = over_batch(far_low)
    density = step([("far", 0, 0, far_low), ("near", 1, cut, near_o_high)], density, (8, 512))

    near_o_low, far_low, far_high, density = together((near_o_low, far_low, far_high, density))
    third_low = for_sibling((near_low,), (far_low,))
    third_high = for_sibling((near_high,), (far_high,))
    density = step(
        [("near", 1, 0, near_o_low), ("far", 0, cut, far_high), ("sibling", 1, 0, sibling_o)],
        density,
        (2, 768),
    )

    far_o_high, far_o_low, density = together((far_o_high, far_o_low, density))
    third_o_low = for_sibling((near_o_low,), (far_o_low,))
    third_o_high = for_sibling((near_o_high,), (far_o_high,))
    density = step(
        [("third", 0, 0, third_low), ("third", 0, cut, third_high)], density, (8, 512)
    )
    return step(
        [
            ("far", 1, 0, far_o_low),
            ("far", 1, cut, far_o_high),
            ("third", 1, 0, third_o_low),
            ("third", 1, cut, third_o_high),
        ],
        density,
        (2, 768),
        last=True,
    )


def pair_density(own_slice, partner, own_energy, partner_energy, row_energy, vir_energy, kappas):
    coulomb = lax.dot_general(
        own_slice, partner, (((0,), (0,)), ((), ())), preferred_element_type=jnp.float32
    )
    denominator = row_energy[:, None] + vir_energy[None, :] - own_energy - partner_energy
    damping = 1.0 - jnp.exp(-kappas[:, None, None] * denominator[None])
    amplitude = (-coulomb[None] * (damping * damping) / denominator[None]).astype(jnp.bfloat16)
    flat = amplitude.reshape(-1, amplitude.shape[2])
    density = lax.dot_general(
        flat, partner, (((1,), (1,)), ((), ())), preferred_element_type=jnp.float32
    )
    return density.reshape(kappas.shape[0], own_slice.shape[1], partner.shape[0])


def ring_terms(integrals, vir_coeff, occ_energy, vir_energy, kappas):
    aux_local, occ_count, basis = integrals.shape
    vir_local = vir_coeff.shape[1]
    batch_index = lax.axis_index("batch")
    wide_index = lax.axis_index("wide")
    flat_ints = integrals.reshape(aux_local * occ_count, basis)
    row_energy = lax.dynamic_slice_in_dim(vir_energy, batch_index * vir_local, vir_local, 0)
    own_energy = lax.dynamic_slice_in_dim(occ_energy, wide_index, 1, 0)[0]

    def term(partner, offset, own_slice):
        partner_index = (wide_index + offset) % occ_count
        partner_energy = lax.dynamic_slice_in_dim(occ_energy, partner_index, 1, 0)[0]
        return pair_density(
            own_slice, partner, own_energy, partner_energy, row_energy, vir_energy, kappas
        )

    transformed = jnp.dot(flat_ints, vir_coeff, preferred_element_type=jnp.float32).astype(
        jnp.bfloat16
    )
    transformed = transformed.reshape(aux_local, occ_count, vir_local)
    own_slice = lax.all_to_all(transformed, "wide", split_axis=1, concat_axis=0, tiled=True)[
        :, 0, :
    ]
    own_full = lax.all_gather(own_slice, "batch", axis=1, tiled=True)
    density = term(own_full, 0, own_slice)
    upper = own_full
    lower = own_full
    for offset in range(1, HALF + 1):
        upper = from_behind(upper, "wide", -1)
        lower = from_behind(lower, "wide", 1)
        density = density + term(upper, offset, own_slice) + term(lower, -offset, own_slice)
    return density.astype(jnp.bfloat16)[:, None, :, :]


def solution(mesh):
    paired = mesh.shape["batch"] == 2 and mesh.shape["wide"] % 4 == 0

    return jax.shard_map(
        pair_terms if paired else ring_terms,
        mesh=mesh,
        in_specs=(P("wide", None, None), P(None, "batch"), P(), P(), P()),
        out_specs=P(None, "wide", "batch", None),
        check_vma=False,
    )
```
